32 devices in a mesh: batch: 8 (over z, x), chan: 4 (over y, core).
Axes of the slice: x: 2, y: 2, z: 4, core: 2. Of those that a mesh axis runs over, the one named last changes fastest.
Arguments:
- tokens: bfloat16 [16, 1024, 768], P('batch', 'chan'), may hold values from -6 to 6
- lengths: int32 [16], P('batch'), may hold values from 256 to 1024, as said below
- buckets: int32 [16], P('batch'), may hold values from 0 to 1
- w_in: bfloat16 [768, 3, 768], P('batch', None, 'chan'), may hold values from -0.21875 to 0.21875
- long_filter: bfloat16 [2, 1024, 768], P(None, 'batch', 'chan'), may hold values from -0.1875 to 0.1875
- w_out: bfloat16 [768, 768], P('chan', 'batch'), may hold values from -0.21875 to 0.21875
- w_gu: bfloat16 [768, 2, 3072], P('batch', None, 'chan'), may hold values from -0.21875 to 0.21875
- w_down: bfloat16 [3072, 768], P('chan', 'batch'), may hold values from -0.109375 to 0.109375
- norm_gains: bfloat16 [2, 768], replicated, may hold values from 0.5 to 1.5
- short_taps: bfloat16 [3, 3, 768], P(None, None, 'chan'), may hold values from -3.5 to 3.5
- cond_taps: bfloat16 [3, 768], P(None, 'chan'), may hold values from -0.1875 to 0.1875
- cotangent: bfloat16 [16, 1024, 768], P('batch', 'chan'), may hold values from -6 to 6
Outputs:
- output: bfloat16 [16, 1024, 768], P('batch', 'chan')
- d_tokens: float32 [16, 1024, 768], P('batch', 'chan')
- grad_w_in: float32 [768, 3, 768], P('batch', None, 'chan')
- grad_long_filter: float32 [2, 1024, 768], P(None, 'batch', 'chan')
- grad_w_out: float32 [768, 768], P('chan', 'batch')
- grad_w_gu: float32 [768, 2, 3072], P('batch', None, 'chan')
- grad_w_down: float32 [3072, 768], P('chan', 'batch')
- grad_norm_gains: float32 [2, 768], replicated
- grad_short_taps: float32 [3, 3, 768], P(None, None, 'chan')
- grad_cond_taps: float32 [3, 768], P(None, 'chan')
The draws below stay inside these ranges and needn't reach their ends.
Inputs may be any that keep to these rules, and one draw needn't show every extreme that they name: `lengths`: A row of bucket 0 has at most 512 live tokens; a row of bucket 1 has at least 384.
All inputs are finite; a program needn't handle non-finite values.
Results may differ from the reference program's by a relative error of at most 0.025.
Values may be sent and summed in bfloat16 or wider, within the bound.
No kernel may reach another device: no remote copies, remote signals or barrier semaphores. Data moves between devices by JAX's collectives and lax.ppermute only.
A program may use at most 256 MiB of HBM per device.

```python
import jax
import jax.numpy as jnp
from jax import lax

D = 768
FF = 3072
LMAX = 1024
MICRO = 2
RMB = 1
SEQS = 16
N_BATCH = 8


def rows_drawn(key):
    bucket_ids = jax.random.randint(jax.random.fold_in(key, 11), (SEQS,), 0, 2).astype(jnp.int32)
    bucket_ids = bucket_ids.at[0].set(1).at[1].set(0)
    lowest = jnp.where(bucket_ids == 1, 3 * LMAX // 8, LMAX // 4).astype(jnp.int32)
    topmost = jnp.where(bucket_ids == 1, LMAX, LMAX // 2).astype(jnp.int32)
    row_lengths = jax.random.randint(jax.random.fold_in(key, 12), (SEQS,), lowest, topmost + 1).astype(jnp.int32)
    row_lengths = row_lengths.at[0].set(LMAX).at[1].set(LMAX // 4)
    return (bucket_ids, row_lengths)


def draw_lengths(key, part):
    shared_rows = rows_drawn(key)
    return shared_rows[1]


def draw_buckets(key, part):
    shared_rows = rows_drawn(key)
    return shared_rows[0]


def levels(key, dims, cuts, smallest, high):
    def one(dim, blocks):
        steps = jax.random.uniform(jax.random.fold_in(jax.random.fold_in(key, 6), dim), (blocks,), jnp.float32, smallest / len(cuts), high / len(cuts))
        return jnp.repeat(jnp.exp(steps), dims[dim] // blocks).reshape((-1,) + (1,) * (len(dims) - dim - 1))

    level = one(*cuts[0])
    for cut in cuts[1:]:
        level = level * one(*cut)
    return level


def gaussian(key, dims, scale, most, cuts=(), kind=jnp.bfloat16):
    entries = scale * jax.random.normal(key, dims, jnp.float32)
    if cuts:
        entries = entries * levels(key, dims, cuts, -0.22, 0.18)
    return jnp.clip(entries, -most, most).astype(kind)


def setup_inputs(seed: int = 0) -> dict:
    seeds = jax.random.split(jax.random.key(seed), 13)
    return {
        "tokens": gaussian(seeds[0], (SEQS, LMAX, D), 1.0, 6.0, ((0, 8), (1, 4))),
        "lengths": draw_lengths(jax.random.fold_in(seeds[12], 71), 0),
        "buckets": draw_buckets(jax.random.fold_in(seeds[12], 71), 0),
        "w_in": gaussian(seeds[3], (D, 3, D), D ** -0.5, 0.21875, ((0, 8), (2, 4))),
        "long_filter": gaussian(seeds[4], (2, LMAX, D), LMAX ** -0.5, 0.1875, ((1, 8), (2, 4))),
        "w_out": gaussian(seeds[5], (D, D), D ** -0.5, 0.21875, ((0, 4), (1, 8))),
        "w_gu": gaussian(seeds[6], (D, 2, FF), D ** -0.5, 0.21875, ((0, 8), (2, 4))),
        "w_down": gaussian(seeds[7], (FF, D), FF ** -0.5, 0.109375, ((0, 4), (1, 8))),
        "norm_gains": jnp.clip(1.0 + 0.1 * jax.random.normal(seeds[8], (2, D), jnp.float32), 0.5, 1.5).astype(jnp.bfloat16),
        "short_taps": gaussian(seeds[9], (3, 3, D), 0.6, 3.5, ((2, 4),)),
        "cond_taps": gaussian(seeds[10], (3, D), 0.03, 0.1875, ((1, 4),)),
        "cotangent": gaussian(seeds[11], (SEQS, LMAX, D), 1.0, 6.0, ((0, 8), (1, 4))),
    }


@jax.custom_vjp
def low(v):
    return lax.optimization_barrier(v.astype(jnp.bfloat16)).astype(jnp.float32)

@jax.custom_vjp
def low_back(v):
    return v

def low_keep(v):
    return (low(v), None)

def low_pass(kept, grad):
    return (grad,)

def back_keep(v):
    return (v, None)

def back_low(kept, grad):
    return (low(grad),)
low.defvjp(low_keep, low_pass)
low_back.defvjp(back_keep, back_low)
epsilon = 1e-05
highest = lax.Precision.HIGHEST

def norm_rows(values, gain_row):
    centre = lax.optimization_barrier(jnp.mean(values, axis=-1, keepdims=True))
    spread = lax.optimization_barrier(jnp.mean(values * values, axis=-1, keepdims=True)) - centre * centre
    return (values - centre) * lax.rsqrt(spread + epsilon) * gain_row

def causal_taps(series, tap_weights):
    result = tap_weights[0] * series
    for offset in (1, 2):
        moved = jnp.pad(series, ((0, 0), (offset, 0), (0, 0)))[:, :-offset]
        result = result + tap_weights[offset] * moved
    return result

def long_conv(kernel, series):
    length = kernel.shape[1]
    spectrum = jnp.fft.rfft(kernel, n=2 * length, axis=1) * jnp.fft.rfft(series, n=2 * length, axis=1)
    return jnp.fft.irfft(spectrum, n=2 * length, axis=1)[:, :length]

def layer(tokens, w_in, long_filter, w_out, w_gu, w_down, norm_gains, short_taps, cond_taps, valid_mask, row_bucket):
    h_first = low(norm_rows(tokens, norm_gains[0]))
    projected = low_back(low(jnp.einsum('rtd,dsc->rtsc', h_first, w_in, precision=highest)))
    streams = [causal_taps(projected[:, :, stream_id], short_taps[stream_id]) * valid_mask for stream_id in range(3)]
    row_filter = jnp.where((row_bucket == 0)[:, None, None], long_filter[0][None], long_filter[1][None])
    kernel = row_filter + causal_taps(streams[1], cond_taps)
    mixed = low(long_conv(kernel, streams[2]) * streams[0])
    branch = low_back(jnp.einsum('rtc,cd->rtd', mixed, w_out, precision=highest))
    residual = tokens + branch
    h_second = low(norm_rows(residual, norm_gains[1]))
    gate_up = low_back(jnp.einsum('rtd,dsf->rtsf', h_second, w_gu, precision=highest))
    hidden = low(jax.nn.gelu(gate_up[:, :, 0]) * gate_up[:, :, 1])
    return (residual + jnp.einsum('rtf,fd->rtd', hidden, w_down, precision=highest)) * valid_mask

def reference(tokens, lengths, buckets, w_in, long_filter, w_out, w_gu, w_down, norm_gains, short_taps, cond_taps, cotangent):
    group_rows = MICRO * RMB
    weights = tuple((weight_arg.astype(jnp.float32) for weight_arg in (w_in, long_filter, w_out, w_gu, w_down, norm_gains, short_taps, cond_taps)))
    positions = jnp.arange(LMAX, dtype=jnp.int32)

    def one_group(totals, group_id):
        first_row = (group_id * group_rows).astype(jnp.int32)
        block_tokens = lax.dynamic_slice_in_dim(tokens, first_row, group_rows, 0).astype(jnp.float32)
        block_lengths = lax.dynamic_slice_in_dim(lengths, first_row, group_rows, 0)
        block_buckets = lax.dynamic_slice_in_dim(buckets, first_row, group_rows, 0)
        block_cot = lax.dynamic_slice_in_dim(cotangent, first_row, group_rows, 0).astype(jnp.float32)
        valid_mask = (positions[None, :] < block_lengths[:, None]).astype(jnp.float32)[:, :, None]

        def forward_pass(inputs, *params):
            return layer(inputs, *params, valid_mask, block_buckets)
        results, pullback = jax.vjp(forward_pass, block_tokens, *weights)
        gradients = pullback(block_cot)
        new_totals = tuple((running + update for running, update in zip(totals, gradients[1:])))
        return (new_totals, (results.astype(jnp.bfloat16), gradients[0]))
    start_totals = tuple((jnp.zeros_like(weight_arg) for weight_arg in weights))
    totals, (results, d_tokens) = lax.scan(one_group, start_totals, jnp.arange(N_BATCH, dtype=jnp.int32))
    results = results.reshape(tokens.shape)
    d_tokens = d_tokens.reshape(tokens.shape)
    return (results, d_tokens, totals[0], totals[1], totals[2], totals[3], totals[4], totals[5], totals[6], totals[7])
```

```python
import functools
import math

import jax
import jax.numpy as jnp
import numpy as np
from jax import lax
from jax.sharding import PartitionSpec as P

EPSILON = 1e-05
LOW = jnp.bfloat16
WIDE = jnp.float32
RING = (0, 2, 4, 6, 7, 5, 3, 1)


def dot(left, right, left_dim, right_dim, kind=WIDE):
    return lax.dot_general(
        left, right, (((left_dim,), (right_dim,)), ((), ())), preferred_element_type=kind
    )


@functools.lru_cache(maxsize=None)
def wave_table(length):
    bins = np.arange(length, dtype=np.int64)[:, None]
    places = np.arange(length, dtype=np.int64)[None, :]
    turns = ((2 * bins + 1) * places) % (4 * length)
    angles = turns * (2.0 * math.pi / (4 * length))
    return np.concatenate([np.cos(angles), -np.sin(angles)], axis=0).astype(jnp.bfloat16)


def swap(block, step):
    size = lax.axis_size("chan")
    return lax.ppermute(block, "chan", [(i, i ^ step) for i in range(size)])


def spread(block):
    far = swap(block, 2)
    near = swap(block, 1)
    return [block, near, far, swap(far, 1)]


def in_order(blocks, me):
    rows = blocks[0].shape[0]
    whole = jnp.zeros((4 * rows,) + blocks[0].shape[1:], blocks[0].dtype)
    for step, block in enumerate(blocks):
        whole = lax.dynamic_update_slice_in_dim(whole, block, (me ^ step) * rows, 0)
    return whole


def fold(partial, me):
    parts = partial.reshape((2, 2, partial.shape[0] // 4) + partial.shape[1:])
    core, chip = me % 2, me // 2
    theirs = lax.dynamic_index_in_dim(parts, 1 - core, 1, False)
    mine = lax.dynamic_index_in_dim(parts, core, 1, False).astype(WIDE)
    both = mine + swap(theirs.astype(LOW), 1).astype(WIDE)
    away = lax.dynamic_index_in_dim(both, 1 - chip, 0, False).astype(LOW)
    keep = lax.dynamic_index_in_dim(both, chip, 0, False)
    return keep + swap(away, 2).astype(WIDE)


def ring_steps(block, shift):
    count = len(RING)
    pairs = [(RING[i], RING[(i + shift) % count]) for i in range(count)]
    return lax.ppermute(block, "batch", pairs)


def ring_gather(block):
    count = lax.axis_size("batch")
    if count != len(RING):
        return lax.all_gather(block, "batch", axis=0, tiled=True)
    place = jnp.asarray([RING.index(i) for i in range(count)], jnp.int32)[lax.axis_index("batch")]
    order = jnp.asarray(RING, jnp.int32)
    rows = block.shape[0]
    half = rows // 2
    whole = jnp.zeros((count * rows,) + block.shape[1:], block.dtype)

    def put(whole, piece, offset, first=0):
        return lax.dynamic_update_slice_in_dim(
            whole, piece, order[(place + offset) % count] * rows + first, 0
        )

    whole = put(whole, block, 0)
    up = down = block
    for step in (1, 2, 3):
        up, down = ring_steps(up, 1), ring_steps(down, -1)
        whole = put(put(whole, up, count - step), down, step)
    whole = put(whole, ring_steps(up[:half], 1), 4)
    return put(whole, ring_steps(down[half:], -1), 4, half)


def ring_sum(partial):
    count = lax.axis_size("batch")
    if count != len(RING):
        return lax.psum_scatter(
            partial.astype(LOW), "batch", scatter_dimension=0, tiled=True
        ).astype(WIDE)
    place = jnp.asarray([RING.index(i) for i in range(count)], jnp.int32)[lax.axis_index("batch")]
    order = jnp.asarray(RING, jnp.int32)
    rows = partial.shape[0] // count
    half = rows // 2

    def part(offset, first=0, size=rows):
        start = order[(place + offset) % count] * rows + first
        return lax.dynamic_slice_in_dim(partial, start, size, 0).astype(WIDE)

    up = ring_steps(part(4, 0, half).astype(LOW), 1).astype(WIDE)
    down = ring_steps(part(4, half, half).astype(LOW), -1).astype(WIDE)
    up = part(3) + jnp.concatenate([up, jnp.zeros_like(up)], axis=0)
    down = part(5) + jnp.concatenate([jnp.zeros_like(down), down], axis=0)
    for step in (2, 1, 0):
        up = ring_steps(up.astype(LOW), 1).astype(WIDE)
        down = ring_steps(down.astype(LOW), -1).astype(WIDE)
        if step:
            up = up + part(step)
            down = down + part(count - step)
    return up + down + part(0)


def small_sum(values, axis):
    size = lax.axis_size(axis)
    if size > 8:
        return lax.psum(values, axis)
    total = values
    for shift in range(1, size):
        pairs = [(i, (i + shift) % size) for i in range(size)]
        total = total + lax.ppermute(values, axis, pairs)
    return total


def norm_forward(values):
    centre = jnp.mean(values, axis=-1, keepdims=True)
    scale = lax.rsqrt(jnp.mean(values * values, axis=-1, keepdims=True) - centre * centre + EPSILON)
    return (values - centre) * scale, scale


def norm_backward(d_out, normed, scale, gain_row):
    scaled = d_out * gain_row
    first_mean = jnp.mean(scaled, axis=-1, keepdims=True)
    second_mean = jnp.mean(scaled * normed, axis=-1, keepdims=True)
    return scale * (scaled - first_mean - normed * second_mean)


def later(series, offset):
    if offset == 0:
        return series
    return jnp.pad(series, ((offset, 0), (0, 0)))[:-offset]


def sooner(series, offset):
    if offset == 0:
        return series
    return jnp.pad(series, ((0, offset), (0, 0)))[offset:]


def causal_taps(series, taps):
    return sum(taps[j] * later(series, j) for j in range(3))


def anti_taps(grads, taps):
    return sum(taps[j] * sooner(grads, j) for j in range(3))


def tap_grads(grads, series):
    return jnp.stack([jnp.sum(grads * later(series, j), axis=0) for j in range(3)])


def spectrum(waves, series):
    length = waves.shape[1]
    both = dot(waves, series.astype(LOW), 1, 0)
    return both[:length], both[length:]


def series_of(waves, real, imag):
    both = jnp.concatenate([real.astype(LOW), imag.astype(LOW)], axis=0)
    return dot(waves, both, 0, 0) * (1.0 / waves.shape[1])


def mixer_forward(projected, short, cond, filters, mask, bucket, waves):
    channels = short.shape[-1]
    raw = [projected[:, s * channels : (s + 1) * channels].astype(WIDE) for s in range(3)]
    streams = [causal_taps(raw[s], short[s]) * mask for s in range(3)]
    chosen = jnp.where(bucket == 0, filters[:, :channels], filters[:, channels:]).astype(WIDE)
    kernel = chosen + causal_taps(streams[1], cond)
    kr, ki = spectrum(waves, kernel)
    sr, si = spectrum(waves, streams[2])
    convolved = series_of(waves, kr * sr - ki * si, kr * si + ki * sr)
    return (convolved * streams[0]).astype(LOW), (raw, streams, convolved, (kr, ki, sr, si))


def mixer_backward(d_mixed, kept, short, cond, mask, waves):
    raw, streams, convolved, (kr, ki, sr, si) = kept
    gr, gi = spectrum(waves, d_mixed * streams[0])
    d_kernel = series_of(waves, gr * sr + gi * si, gi * sr - gr * si)
    d_series = series_of(waves, gr * kr + gi * ki, gi * kr - gr * ki)
    grad_cond = tap_grads(d_kernel, streams[1])
    d_streams = (
        d_mixed * convolved * mask,
        anti_taps(d_kernel, cond) * mask,
        d_series * mask,
    )
    grad_short = jnp.concatenate([tap_grads(d_streams[s], raw[s]) for s in range(3)], axis=0)
    d_projected = jnp.concatenate(
        [anti_taps(d_streams[s], short[s]) for s in range(3)], axis=1
    ).astype(LOW)
    return d_projected, d_kernel, jnp.concatenate([grad_short, grad_cond], axis=0)


def per_device(
    tokens,
    lengths,
    buckets,
    w_in,
    long_filter,
    w_out,
    w_gu,
    w_down,
    norm_gains,
    short_taps,
    cond_taps,
    cotangent,
):
    me = lax.axis_index("chan")
    row_count, part_len, width = tokens.shape
    full_len = part_len * lax.axis_size("chan")
    channels = short_taps.shape[-1]
    hidden_count = w_down.shape[0]
    rows = range(row_count)
    gains = norm_gains.astype(WIDE)
    short = short_taps.astype(WIDE)
    cond = cond_taps.astype(WIDE)
    waves = jnp.asarray(wave_table(full_len))
    positions = jnp.arange(full_len, dtype=jnp.int32)[:, None]
    masks = [(positions < lengths[r]).astype(WIDE) for r in rows]
    own = [lax.dynamic_slice_in_dim(masks[r], me * part_len, part_len, 0) for r in rows]

    full_in = ring_gather(w_in.reshape(-1, 3 * channels))
    filters = ring_gather(jnp.concatenate([long_filter[0], long_filter[1]], axis=1))
    out_parts = jnp.concatenate(spread(w_out), axis=0)
    full_out = ring_gather(out_parts.T)
    full_gu = ring_gather(w_gu.reshape(-1, 2 * hidden_count))
    full_down = ring_gather(w_down.T)

    all_tokens = [in_order(spread(tokens[r]), me) for r in rows]
    h_first = []
    kept = []
    mixed = []
    residual = []
    for r in rows:
        normed, _ = norm_forward(all_tokens[r].astype(WIDE))
        h_first.append((normed * gains[0]).astype(LOW))
        projected = dot(h_first[r], full_in, 1, 0).astype(LOW)
        mine, keep = mixer_forward(
            projected, short, cond, filters, masks[r], buckets[r], waves
        )
        mixed.append(mine)
        kept.append(keep)
        branch = sum(
            dot(part, full_out[:, k * channels : (k + 1) * channels], 1, 1)
            for k, part in enumerate(spread(mine))
        )
        residual.append(all_tokens[r].astype(WIDE) + branch)

    d_out = [in_order(spread(cotangent[r]), me) * masks[r].astype(LOW) for r in rows]
    outputs = []
    h_second = []
    hidden = []
    d_gate_up = []
    d_residual = []
    gain_second = 0.0
    for r in rows:
        normed, _ = norm_forward(residual[r])
        h_second.append((normed * gains[1]).astype(LOW))
        gate_up = dot(h_second[r], full_gu, 1, 0)
        gate, up = gate_up[:, :hidden_count], gate_up[:, hidden_count:]
        values, pull = jax.vjp(lambda g, u: jax.nn.gelu(g) * u, gate, up)
        hidden.append(values.astype(LOW))
        d_hidden = dot(d_out[r], full_down, 1, 0)
        d_gate_up.append(jnp.concatenate(pull(d_hidden), axis=1).astype(LOW))
        d_normed = fold(dot(d_gate_up[r], full_gu, 1, 1, LOW), me)
        here = lax.dynamic_slice_in_dim(residual[r], me * part_len, part_len, 0)
        normed, scale = norm_forward(here)
        gain_second = gain_second + jnp.sum(d_normed * normed, axis=0)
        d_own = cotangent[r].astype(WIDE) * own[r]
        d_residual.append(d_own + norm_backward(d_normed, normed, scale, gains[1]))
        final = here + fold(dot(hidden[r], full_down, 1, 1, LOW), me)
        outputs.append((final * own[r]).astype(LOW))

    grad_gu = sum(dot(h_second[r], d_gate_up[r], 0, 0) for r in rows)
    grad_down = sum(dot(d_out[r], hidden[r], 0, 0) for r in rows)
    grad_gu = ring_sum(grad_gu)
    grad_down = ring_sum(grad_down)

    d_inputs = []
    grad_in = 0.0
    grad_out = 0.0
    grad_taps = 0.0
    grad_filter = 0.0
    for r in rows:
        d_branch = in_order(spread(d_residual[r].astype(LOW)), me)
        d_mixed = dot(d_branch, full_out[:, :channels], 1, 0)
        grad_out = grad_out + dot(d_branch, mixed[r], 0, 0)
        d_projected, d_kernel, taps = mixer_backward(
            d_mixed, kept[r], short, cond, masks[r], waves
        )
        grad_taps = grad_taps + taps
        first = (buckets[r] == 0).astype(WIDE)
        grad_filter = grad_filter + jnp.concatenate(
            [d_kernel * first, d_kernel * (1.0 - first)], axis=1
        )
        grad_in = grad_in + dot(h_first[r], d_projected, 0, 0)
        d_normed = fold(dot(d_projected, full_in, 1, 1, LOW), me)
        normed, scale = norm_forward(tokens[r].astype(WIDE))
        d_inputs.append(d_residual[r] + norm_backward(d_normed, normed, scale, gains[0]))

    gain_first = jnp.sum(grad_in * full_in.astype(WIDE), axis=1) / gains[0]
    grad_out = ring_sum(grad_out)
    grad_filter = ring_sum(grad_filter)
    grad_in = ring_sum(grad_in)
    packed = jnp.concatenate([gain_first, gain_second, grad_taps.reshape(-1)])
    packed = small_sum(packed.reshape(-1, 128), "batch").reshape(-1)
    grad_gains = small_sum(packed[: 2 * width].reshape(-1, 128), "chan").reshape(2, width)
    grad_taps = packed[2 * width :].reshape(12, channels)
    return (
        jnp.stack(outputs),
        jnp.stack(d_inputs),
        grad_in.reshape(-1, 3, channels),
        jnp.stack([grad_filter[:, :channels], grad_filter[:, channels:]]),
        grad_out.T,
        grad_gu.reshape(-1, 2, hidden_count),
        grad_down.T,
        grad_gains,
        grad_taps[:9].reshape(3, 3, channels),
        grad_taps[9:],
    )


def solution(mesh):
    placed = (
        P("batch", "chan", None),
        P("batch"),
        P("batch"),
        P("batch", None, "chan"),
        P(None, "batch", "chan"),
        P("chan", "batch"),
        P("batch", None, "chan"),
        P("chan", "batch"),
        P(),
        P(None, None, "chan"),
        P(None, "chan"),
        P("batch", "chan", None),
    )
    return jax.shard_map(
        per_device,
        mesh=mesh,
        in_specs=placed,
        out_specs=(
            P("batch", "chan", None),
            P("batch", "chan", None),
            P("batch", None, "chan"),
            P(None, "batch", "chan"),
            P("chan", "batch"),
            P("batch", None, "chan"),
            P("chan", "batch"),
            P(),
            P(None, None, "chan"),
            P(None, "chan"),
        ),
        check_vma=False,
    )
```

```python
import functools
import math

import jax
import jax.numpy as jnp
import numpy as np
from jax import lax
from jax.experimental import pallas as pl
from jax.experimental.pallas import tpu as pltpu
from jax.sharding import PartitionSpec as P

EPSILON = 1e-05
LOW = jnp.bfloat16
WIDE = jnp.float32
RING = (0, 2, 4, 6, 7, 5, 3, 1)
CODES = (0, 2, 1, 3)
LANES = 256


def dot(left, right, left_dim, right_dim, kind=WIDE):
    return lax.dot_general(
        left, right, (((left_dim,), (right_dim,)), ((), ())), preferred_element_type=kind
    )


@functools.lru_cache(maxsize=None)
def wave_tables(length, tiles=4):
    bins = np.arange(length, dtype=np.int64)[:, None]
    places = np.arange(length, dtype=np.int64)[None, :]
    turns = ((2 * bins + 1) * places) % (4 * length)
    angles = turns * (2.0 * math.pi / (4 * length))
    both = np.stack(
        [
            np.cos(angles).reshape(tiles, length // tiles, length),
            -np.sin(angles).reshape(tiles, length // tiles, length),
        ],
        axis=1,
    ).reshape(2 * length, length)
    return both.astype(jnp.bfloat16), np.ascontiguousarray(both.T).astype(jnp.bfloat16)


def swap(block, step):
    size = lax.axis_size("chan")
    return lax.ppermute(block, "chan", [(i, i ^ step) for i in range(size)])


def spread(block):
    far = swap(block, 2)
    near = swap(block, 1)
    return [block, far, near, swap(far, 1)]


def fold_far(keep, send):
    arrived = swap(send, 1)
    half = keep.shape[0] // 2
    away = (keep[half:] + arrived[half:].astype(WIDE)).astype(LOW)
    return arrived, swap(away, 2)


def ring_steps(block, shift):
    count = len(RING)
    pairs = [(RING[i], RING[(i + shift) % count]) for i in range(count)]
    return lax.ppermute(block, "batch", pairs)


def ring_place():
    places = jnp.asarray([RING.index(i) for i in range(len(RING))], jnp.int32)
    return places[lax.axis_index("batch")]


def place_kernel(starts, *refs):
    count = (len(refs) - 2) // 1
    pieces, whole, sems = refs[:count], refs[count], refs[count + 1]
    copies = []
    for i, piece in enumerate(pieces):
        size = piece.shape[0]
        start = pl.multiple_of(starts[i], 16)
        copies.append(
            pltpu.make_async_copy(piece, whole.at[pl.ds(start, size), :], sems.at[i])
        )
    for copy in copies:
        copy.start()
    for copy in copies:
        copy.wait()


def ring_gather(block):
    count = lax.axis_size("batch")
    if count != len(RING):
        return lax.all_gather(block, "batch", axis=0, tiled=True)
    order = jnp.asarray(RING, jnp.int32)
    place = ring_place()
    rows = block.shape[0]
    half = rows // 2
    pieces = [(block, 0, 0)]
    up = down = block
    for step in (1, 2, 3):
        up, down = ring_steps(up, 1), ring_steps(down, -1)
        pieces += [(up, count - step, 0), (down, step, 0)]
    pieces += [(ring_steps(up[:half], 1), 4, 0), (ring_steps(down[half:], -1), 4, half)]
    starts = jnp.stack([order[(place + offset) % count] * rows + first for _, offset, first in pieces])
    return pl.pallas_call(
        place_kernel,
        in_specs=[pl.BlockSpec(memory_space=pltpu.SMEM)]
        + [pl.BlockSpec(memory_space=pl.ANY)] * len(pieces),
        out_specs=pl.BlockSpec(memory_space=pl.ANY),
        out_shape=jax.ShapeDtypeStruct((count * rows,) + block.shape[1:], block.dtype),
        scratch_shapes=[pltpu.SemaphoreType.DMA((len(pieces),))],
        name="place",
    )(starts, *[piece for piece, _, _ in pieces])


def ring_sum(partial):
    count = lax.axis_size("batch")
    if count != len(RING):
        return lax.psum_scatter(
            partial.astype(LOW), "batch", scatter_dimension=0, tiled=True
        ).astype(WIDE)
    place = ring_place()
    order = jnp.asarray(RING, jnp.int32)
    rows = partial.shape[0] // count
    half = rows // 2

    def part(offset, first=0, size=rows):
        start = order[(place + offset) % count] * rows + first
        return lax.dynamic_slice_in_dim(partial, start, size, 0).astype(WIDE)

    up = ring_steps(part(4, 0, half).astype(LOW), 1).astype(WIDE)
    down = ring_steps(part(4, half, half).astype(LOW), -1).astype(WIDE)
    up = part(3) + jnp.concatenate([up, jnp.zeros_like(up)], axis=0)
    down = part(5) + jnp.concatenate([jnp.zeros_like(down), down], axis=0)
    for step in (2, 1, 0):
        up = ring_steps(up.astype(LOW), 1).astype(WIDE)
        down = ring_steps(down.astype(LOW), -1).astype(WIDE)
        if step:
            up = up + part(step)
            down = down + part(count - step)
    return up + down + part(0)


def small_sum(values, axis):
    size = lax.axis_size(axis)
    if size > 8:
        return lax.psum(values, axis)
    total = values
    for shift in range(1, size):
        pairs = [(i, (i + shift) % size) for i in range(size)]
        total = total + lax.ppermute(values, axis, pairs)
    return total


def norm_forward(values):
    centre = jnp.mean(values, axis=-1, keepdims=True)
    scale = lax.rsqrt(jnp.mean(values * values, axis=-1, keepdims=True) - centre * centre + EPSILON)
    return (values - centre) * scale, scale


def block_start(info, code, rows):
    return pl.multiple_of((info[0] ^ code) * rows, rows)


def shifted(series, offset, row):
    if offset == 0:
        return series
    length = series.shape[0]
    moved = pltpu.roll(series, offset % length, 0)
    inside = row >= offset if offset > 0 else row < length + offset
    return jnp.where(inside, moved, 0.0)


def tap_sum(series, taps, first, row, direction):
    total = taps[first : first + 1, :] * series
    for j in (1, 2):
        total = total + taps[first + j : first + j + 1, :] * shifted(series, direction * j, row)
    return total


def mixer_kernel(
    info, t0, t1, t2, t3, w_in, filters, taps, gain, waves, waves_t,
    mixed, h_first, projected, convolved, kernel_spec, series_spec,
    waves_buf, waves_t_buf, kernel_buf, series_buf, product_buf, gate_buf, sems,
):
    first_copy = pltpu.make_async_copy(waves, waves_buf, sems.at[0])
    second_copy = pltpu.make_async_copy(waves_t, waves_t_buf, sems.at[1])
    first_copy.start()
    second_copy.start()
    rows = t0.shape[0]
    for code, block in zip(CODES, (t0, t1, t2, t3)):
        normed, _ = norm_forward(block[...].astype(WIDE))
        low = (normed * gain[...]).astype(LOW)
        place = pl.ds(block_start(info, code, rows), rows)
        h_first[place, :] = low
        projected[place, :] = dot(low, w_in[...], 1, 0).astype(LOW)
    length = projected.shape[0]
    row = lax.broadcasted_iota(jnp.int32, (length, LANES), 0)
    mask = (row < info[1]).astype(WIDE)

    def stream(s):
        raw = projected[:, s * LANES : (s + 1) * LANES].astype(WIDE)
        return mask * tap_sum(raw, taps, 3 * s, row, 1)

    channels = filters.shape[1] // 2
    both = filters[...].astype(WIDE)
    chosen = jnp.where(info[2] == 0, both, pltpu.roll(both, channels, 1))[:, :LANES]
    kernel_buf[...] = (chosen + tap_sum(stream(1), taps, 9, row, 1)).astype(LOW)
    series_buf[...] = stream(2).astype(LOW)
    gate_buf[...] = stream(0)
    first_copy.wait()
    tiles = 4
    size = 2 * length // tiles
    half = size // 2
    for i in range(tiles):
        place = slice(i * size, (i + 1) * size)
        table = waves_buf[place, :]
        k = dot(table, kernel_buf[...], 1, 0)
        s = dot(table, series_buf[...], 1, 0)
        kernel_spec[place, :] = k.astype(LOW)
        series_spec[place, :] = s.astype(LOW)
        kr, ki, sr, si = k[:half], k[half:], s[:half], s[half:]
        product_buf[i * size : i * size + half, :] = (kr * sr - ki * si).astype(LOW)
        product_buf[i * size + half : (i + 1) * size, :] = (kr * si + ki * sr).astype(LOW)
    second_copy.wait()
    for i in range(2):
        place = slice(i * length // 2, (i + 1) * length // 2)
        value = dot(waves_t_buf[place, :], product_buf[...], 1, 0) * (1.0 / length)
        convolved[place, :] = value.astype(LOW)
        mixed[place, :] = (value * gate_buf[place, :]).astype(LOW)[:, : mixed.shape[1]]


def middle_kernel(
    info, t0, t1, t2, t3, c0, c1, c2, c3, m0, m1, m2, m3, o0, o1, o2, o3, gain, weights,
    h_out, grads_out, hidden_out, d_out_out, send_d, keep_d, send_o, keep_o, residual,
    weights_buf, h_buf, grads_buf, hidden_buf, d_out_buf, sems,
):
    copy = pltpu.make_async_copy(weights, weights_buf, sems.at[0])
    copy.start()
    rows, width = t0.shape
    tokens, grads, mixed, outs = (t0, t1, t2, t3), (c0, c1, c2, c3), (m0, m1, m2, m3), (o0, o1, o2, o3)
    hidden = hidden_buf.shape[1]
    leaving = []
    for tile in (1, 0):
        whole = slice(tile * 2 * rows, (tile + 1) * 2 * rows)
        for block in (2 * tile, 2 * tile + 1):
            start = block_start(info, CODES[block], rows)
            place = slice(block * rows, (block + 1) * rows)
            value = tokens[block][...].astype(WIDE)
            for part, out in zip(mixed, outs):
                value = value + dot(part[pl.ds(start, rows), :], out[...], 1, 1)
            if block == 0:
                residual[...] = value
            normed, _ = norm_forward(value)
            h_buf[place, :] = (normed * gain[...]).astype(LOW)
            row = start + lax.broadcasted_iota(jnp.int32, (rows, width), 0)
            d_out_buf[place, :] = jnp.where(row < info[1], grads[block][...].astype(WIDE), 0.0).astype(LOW)
        if tile == 1:
            copy.wait()
        for first in range(0, hidden, 256):
            gate_place = slice(first, first + 256)
            up_place = slice(hidden + first, hidden + first + 256)
            down_place = slice(2 * hidden + first, 2 * hidden + first + 256)
            gate = dot(h_buf[whole, :], weights_buf[:, gate_place], 1, 0)
            up = dot(h_buf[whole, :], weights_buf[:, up_place], 1, 0)
            d_hidden = dot(d_out_buf[whole, :], weights_buf[:, down_place], 1, 0)
            slope = math.sqrt(2.0 / math.pi)
            square = gate * gate
            bent = jnp.tanh(slope * gate * (1.0 + 0.044715 * square))
            rise = 0.5 * (1.0 + bent)
            active = gate * rise
            hidden_buf[whole, gate_place] = (active * up).astype(LOW)
            d_active = rise + 0.5 * gate * (1.0 - bent * bent) * (slope * (1.0 + 0.134145 * square))
            grads_buf[whole, gate_place] = (d_hidden * up * d_active).astype(LOW)
            grads_buf[whole, up_place] = (d_hidden * active).astype(LOW)
        moves = ((h_buf, h_out), (grads_buf, grads_out), (hidden_buf, hidden_out), (d_out_buf, d_out_out))
        for i, (source, target) in enumerate(moves):
            leave = pltpu.make_async_copy(
                source.at[whole, :], target.at[whole, :], sems.at[1 + 4 * tile + i]
            )
            leave.start()
            leaving.append(leave)
        d_normed = dot(grads_buf[whole, :], weights_buf[:, : 2 * hidden], 1, 1)
        out = dot(hidden_buf[whole, :], weights_buf[:, 2 * hidden :], 1, 1)
        if tile == 1:
            send_d[...] = d_normed.astype(LOW)
            send_o[...] = out.astype(LOW)
        else:
            keep_d[...] = d_normed
            keep_o[...] = out
    for leave in leaving:
        leave.wait()


def norm_kernel(keep, arrived, last, values, extra, gain, d_wide, d_low, gain_grad):
    rows = values.shape[0]
    d_out = keep[:rows, :] + arrived[:rows, :].astype(WIDE) + last[...].astype(WIDE)
    normed, scale = norm_forward(values[...].astype(WIDE))
    scaled = d_out * gain[...]
    first_mean = jnp.mean(scaled, axis=-1, keepdims=True)
    second_mean = jnp.mean(scaled * normed, axis=-1, keepdims=True)
    total = extra[...].astype(WIDE) + scale * (scaled - first_mean - normed * second_mean)
    d_wide[...] = total
    d_low[...] = total.astype(LOW)
    gain_grad[...] = jnp.sum(d_out * normed, axis=0, keepdims=True)


def back_kernel(
    info, b0, b1, b2, b3, w_out, w_in, mixed, projected, convolved, kernel_spec, series_spec, taps, waves, waves_t,
    d_projected, d_kernel, tap_grads, out_grad, send, keep,
    waves_buf, waves_t_buf, mix_buf, conv_buf, product_k, product_s, d_series, sems,
):
    first_copy = pltpu.make_async_copy(waves, waves_buf, sems.at[0])
    second_copy = pltpu.make_async_copy(waves_t, waves_t_buf, sems.at[1])
    first_copy.start()
    second_copy.start()
    rows = b0.shape[0]
    for i, (code, block) in enumerate(zip(CODES, (b0, b1, b2, b3))):
        place = pl.ds(block_start(info, code, rows), rows)
        mix_buf[place, :] = dot(block[...], w_out[...], 1, 0)
        part = dot(block[...], mixed[place, :], 0, 0)
        out_grad[...] = part if i == 0 else out_grad[...] + part
    length = projected.shape[0]
    row = lax.broadcasted_iota(jnp.int32, (length, LANES), 0)
    mask = (row < info[1]).astype(WIDE)

    def raw(s):
        return projected[:, s * LANES : (s + 1) * LANES].astype(WIDE)

    conv_buf[...] = (mix_buf[...] * mask * tap_sum(raw(0), taps, 0, row, 1)).astype(LOW)
    first_copy.wait()
    tiles = 4
    size = 2 * length // tiles
    half = size // 2
    for i in range(tiles):
        upper, lower = slice(i * size, i * size + half), slice(i * size + half, (i + 1) * size)
        g = dot(waves_buf[i * size : (i + 1) * size, :], conv_buf[...], 1, 0)
        gr, gi = g[:half], g[half:]
        sr, si = series_spec[upper, :].astype(WIDE), series_spec[lower, :].astype(WIDE)
        product_k[upper, :] = (gr * sr + gi * si).astype(LOW)
        product_k[lower, :] = (gi * sr - gr * si).astype(LOW)
        kr, ki = kernel_spec[upper, :].astype(WIDE), kernel_spec[lower, :].astype(WIDE)
        product_s[upper, :] = (gr * kr + gi * ki).astype(LOW)
        product_s[lower, :] = (gi * kr - gr * ki).astype(LOW)
    second_copy.wait()
    for i in range(2):
        place = slice(i * length // 2, (i + 1) * length // 2)
        d_kernel[place, :] = dot(waves_t_buf[place, :], product_k[...], 1, 0) * (1.0 / length)
        d_series[place, :] = dot(waves_t_buf[place, :], product_s[...], 1, 0) * (1.0 / length)

    def finish(s, grads):
        series = raw(s)
        for j in range(3):
            tap_grads[3 * s + j : 3 * s + j + 1, :] = jnp.sum(
                grads * shifted(series, j, row), axis=0, keepdims=True
            )
        d_projected[:, s * LANES : (s + 1) * LANES] = tap_sum(grads, taps, 3 * s, row, -1).astype(LOW)

    finish(0, mix_buf[...] * convolved[...].astype(WIDE) * mask)
    finish(2, d_series[...] * mask)
    grads = d_kernel[...]
    condition = mask * tap_sum(raw(1), taps, 3, row, 1)
    for j in range(3):
        tap_grads[9 + j : 10 + j, :] = jnp.sum(
            grads * shifted(condition, j, row), axis=0, keepdims=True
        )
    finish(1, mask * tap_sum(grads, taps, 9, row, -1))
    for i, code in enumerate(CODES):
        place = pl.ds(block_start(info, code, rows), rows)
        part = dot(d_projected[place, :], w_in[...], 1, 1)
        if i < 2:
            keep[i * rows : (i + 1) * rows, :] = part
        else:
            send[(i - 2) * rows : (i - 1) * rows, :] = part.astype(LOW)


ANY = pl.BlockSpec(memory_space=pl.ANY)
SCALARS = pl.BlockSpec(memory_space=pltpu.SMEM)
NEAR = pl.BlockSpec(memory_space=pltpu.VMEM)


def call(kernel, operands, kinds, results, result_kinds, scratch, flops, name, limit=50):
    moved = sum(x.size * x.dtype.itemsize for x in operands)
    moved += sum(math.prod(shape) * jnp.dtype(kind).itemsize for shape, kind in results)
    return pl.pallas_call(
        kernel,
        in_specs=kinds,
        out_specs=result_kinds,
        out_shape=[jax.ShapeDtypeStruct(shape, kind) for shape, kind in results],
        scratch_shapes=scratch,
        compiler_params=pltpu.CompilerParams(vmem_limit_bytes=limit * 2**20),
        cost_estimate=pl.CostEstimate(flops=flops, bytes_accessed=moved, transcendentals=0),
        name=name,
    )(*operands)


def mixer_forward(info, tokens, w_in, filters, taps, gain, tables, channels):
    rows, width = tokens[0].shape
    length = 4 * rows
    spec = ((2 * length, LANES), LOW)
    return call(
        mixer_kernel,
        [info, *tokens, w_in, filters, taps, gain, *tables],
        [SCALARS] + [NEAR] * 8 + [ANY] * 2,
        [
            ((length, channels), LOW),
            ((length, width), LOW),
            ((length, 3 * LANES), LOW),
            ((length, LANES), LOW),
            spec,
            spec,
        ],
        [NEAR] * 6,
        [
            pltpu.VMEM((2 * length, length), LOW),
            pltpu.VMEM((length, 2 * length), LOW),
            pltpu.VMEM((length, LANES), LOW),
            pltpu.VMEM((length, LANES), LOW),
            pltpu.VMEM((2 * length, LANES), LOW),
            pltpu.VMEM((length, LANES), WIDE),
            pltpu.SemaphoreType.DMA((2,)),
        ],
        2 * length * (width * 3 * LANES + 6 * length * LANES),
        "mixer",
    )


def middle(info, tokens, grads, mixed, outs, gain, weights):
    rows, width = tokens[0].shape
    length = 4 * rows
    hidden = weights.shape[1] // 3
    return call(
        middle_kernel,
        [info, *tokens, *grads, *mixed, *outs, gain, weights],
        [SCALARS] + [NEAR] * 17 + [ANY],
        [
            ((length, width), LOW),
            ((length, 2 * hidden), LOW),
            ((length, hidden), LOW),
            ((length, width), LOW),
            ((2 * rows, width), LOW),
            ((2 * rows, width), WIDE),
            ((2 * rows, width), LOW),
            ((2 * rows, width), WIDE),
            ((rows, width), WIDE),
        ],
        [ANY] * 4 + [NEAR] * 5,
        [
            pltpu.VMEM((width, 3 * hidden), LOW),
            pltpu.VMEM((length, width), LOW),
            pltpu.VMEM((length, 2 * hidden), LOW),
            pltpu.VMEM((length, hidden), LOW),
            pltpu.VMEM((length, width), LOW),
            pltpu.SemaphoreType.DMA((9,)),
        ],
        2 * length * width * (width + 6 * hidden),
        "middle",
    )


def norm_back(keep, arrived, last, values, extra, gain):
    rows, width = values.shape
    return call(
        norm_kernel,
        [keep, arrived, last, values, extra, gain],
        [NEAR] * 6,
        [((rows, width), WIDE), ((rows, width), LOW), ((1, width), WIDE)],
        [NEAR] * 3,
        [],
        20 * rows * width,
        "norm_back",
        20,
    )


def mixer_backward(info, grads, w_out, w_in, kept, taps, tables):
    rows, width = grads[0].shape
    length = 4 * rows
    mixed, projected, convolved, kernel_spec, series_spec = kept
    return call(
        back_kernel,
        [info, *grads, w_out, w_in, mixed, projected, convolved, kernel_spec, series_spec, taps, *tables],
        [SCALARS] + [NEAR] * 12 + [ANY] * 2,
        [
            ((length, 3 * LANES), LOW),
            ((length, LANES), WIDE),
            ((12, LANES), WIDE),
            ((width, mixed.shape[1]), WIDE),
            ((2 * rows, width), LOW),
            ((2 * rows, width), WIDE),
        ],
        [NEAR] * 6,
        [
            pltpu.VMEM((2 * length, length), LOW),
            pltpu.VMEM((length, 2 * length), LOW),
            pltpu.VMEM((length, LANES), WIDE),
            pltpu.VMEM((length, LANES), LOW),
            pltpu.VMEM((2 * length, LANES), LOW),
            pltpu.VMEM((2 * length, LANES), LOW),
            pltpu.VMEM((length, LANES), WIDE),
            pltpu.SemaphoreType.DMA((2,)),
        ],
        2 * length * (width * 5 * LANES + 6 * length * LANES),
        "mixer_back",
    )


def pack_mixer(w_in, long_filter, w_out):
    rows, _, channels = w_in.shape
    gap = LANES - channels
    turned = w_out.T
    pieces = []
    for s in range(3):
        pieces += [w_in[:, s], turned[:, s * gap : (s + 1) * gap]]
    both = jnp.concatenate([long_filter[0], long_filter[1]], axis=1)
    spare = both[rows:].reshape(both.shape[0] - rows, 3, -1)
    pieces += [both[:rows], spare.transpose(1, 0, 2).reshape(rows, -1)]
    return jnp.concatenate(pieces, axis=1)


def unpack_mixer(pack, rows, channels):
    gap = LANES - channels
    w_in = pack[:, : 3 * LANES]
    w_out = jnp.concatenate(
        [pack[:, s * LANES + channels : s * LANES + channels + gap] for s in range(3)], axis=1
    )
    blocks = pack[:, 3 * LANES :].reshape(-1, rows, pack.shape[1] - 3 * LANES)
    spare = blocks[:, :, 2 * channels :].reshape(blocks.shape[0], 3, rows // 3, -1)
    spare = spare.transpose(0, 2, 1, 3).reshape(blocks.shape[0], rows // 3, -1)
    filters = jnp.concatenate([blocks[:, :, : 2 * channels], spare], axis=1)
    return w_in, w_out, filters.reshape(-1, 2 * channels)


def per_device(
    tokens,
    lengths,
    buckets,
    w_in,
    long_filter,
    w_out,
    w_gu,
    w_down,
    norm_gains,
    short_taps,
    cond_taps,
    cotangent,
):
    me = lax.axis_index("chan").astype(jnp.int32)
    row_count, part_len, width = tokens.shape
    channels = short_taps.shape[-1]
    hidden = w_down.shape[0]
    shard = w_in.shape[0]
    rows = range(row_count)
    gains = norm_gains.astype(WIDE)
    taps = jnp.concatenate([short_taps.reshape(9, channels), cond_taps], axis=0).astype(WIDE)
    taps = jnp.pad(taps, ((0, 0), (0, LANES - channels)))
    tables = tuple(jnp.asarray(table) for table in wave_tables(4 * part_len))
    infos = [jnp.stack([me, lengths[r], buckets[r]]) for r in rows]
    local = me * part_len + jnp.arange(part_len, dtype=jnp.int32)[:, None]
    own = [local < lengths[r] for r in rows]

    all_tokens = [spread(tokens[r]) for r in rows]
    pack = ring_gather(pack_mixer(w_in, long_filter, w_out))
    full_in, part_out, filters = unpack_mixer(pack, shard, channels)
    outs = spread(part_out)
    weights = ring_gather(jnp.concatenate([w_gu.reshape(shard, -1), w_down.T], axis=1))

    forward = [
        mixer_forward(
            infos[r], all_tokens[r], full_in, filters, taps, gains[:1], tables, channels
        )
        for r in rows
    ]
    mixed = [spread(forward[r][0]) for r in rows]
    all_grads = [spread(cotangent[r]) for r in rows]
    centre = [
        middle(infos[r], all_tokens[r], all_grads[r], mixed[r], outs, gains[1:], weights)
        for r in rows
    ]

    d_residual = []
    gain_second = 0.0
    backward = []
    w_out_wide = jnp.pad(part_out, ((0, 0), (0, LANES - channels)))
    for r in rows:
        _, _, _, _, send_d, keep_d, _, _, residual = centre[r]
        d_own = jnp.where(own[r], cotangent[r], jnp.zeros_like(cotangent[r]))
        arrived, last = fold_far(keep_d, send_d)
        d_wide, d_low, gain_grad = norm_back(keep_d, arrived, last, residual, d_own, gains[1:])
        d_residual.append(d_wide)
        gain_second = gain_second + gain_grad
        kept = (forward[r][0],) + tuple(forward[r][2:])
        backward.append(
            mixer_backward(infos[r], spread(d_low), w_out_wide, full_in, kept, taps, tables)
        )

    grad_gu = sum(dot(centre[r][0], centre[r][1], 0, 0) for r in rows)
    grad_down = sum(dot(centre[r][3], centre[r][2], 0, 0) for r in rows)
    grad_ff = ring_sum(jnp.concatenate([grad_gu.astype(LOW), grad_down.astype(LOW)], axis=1))

    outputs = []
    d_inputs = []
    grad_in = 0.0
    grad_out = 0.0
    grad_taps = 0.0
    grad_filter = 0.0
    for r in rows:
        send_o, keep_o, residual = centre[r][6:]
        arrived, last = fold_far(keep_o, send_o)
        final = residual + keep_o[:part_len] + arrived[:part_len].astype(WIDE) + last.astype(WIDE)
        outputs.append(jnp.where(own[r], final, 0.0).astype(LOW))
        d_projected, d_kernel, tap_grads, out_grad, send, keep = backward[r]
        arrived, last = fold_far(keep, send)
        d_wide, _, _ = norm_back(keep, arrived, last, tokens[r], d_residual[r], gains[:1])
        d_inputs.append(d_wide)
        grad_in = grad_in + dot(forward[r][1], d_projected, 0, 0)
        grad_out = grad_out + out_grad
        grad_taps = grad_taps + tap_grads
        d_kernel = d_kernel[:, :channels]
        first = (buckets[r] == 0).astype(WIDE)
        grad_filter = grad_filter + jnp.concatenate(
            [d_kernel * first, d_kernel * (1.0 - first)], axis=1
        )

    gain_first = jnp.sum(grad_in * full_in.astype(WIDE), axis=1) / gains[0]
    gap = LANES - channels
    pieces = []
    for s in range(3):
        pieces += [
            grad_in[:, s * LANES : s * LANES + channels],
            grad_out[:, s * gap : (s + 1) * gap],
        ]
    grad_mixer = ring_sum(jnp.concatenate(pieces, axis=1).astype(LOW)).reshape(-1, 3, LANES)
    grad_filter = ring_sum(grad_filter.astype(LOW))
    packed = jnp.concatenate(
        [gain_first, gain_second.reshape(-1), grad_taps[:, :channels].reshape(-1)]
    )
    packed = small_sum(packed.reshape(-1, 128), "batch").reshape(-1)
    grad_gains = small_sum(packed[: 2 * width].reshape(-1, 128), "chan").reshape(2, width)
    grad_taps = packed[2 * width :].reshape(12, channels)
    return (
        jnp.stack(outputs),
        jnp.stack(d_inputs),
        grad_mixer[:, :, :channels],
        jnp.stack([grad_filter[:, :channels], grad_filter[:, channels:]]),
        jnp.concatenate([grad_mixer[:, s, channels:] for s in range(3)], axis=1).T,
        grad_ff[:, : 2 * hidden].reshape(-1, 2, hidden),
        grad_ff[:, 2 * hidden :].T,
        grad_gains,
        grad_taps[:9].reshape(3, 3, channels),
        grad_taps[9:],
    )


def solution(mesh):
    placed = (
        P("batch", "chan", None),
        P("batch"),
        P("batch"),
        P("batch", None, "chan"),
        P(None, "batch", "chan"),
        P("chan", "batch"),
        P("batch", None, "chan"),
        P("chan", "batch"),
        P(),
        P(None, None, "chan"),
        P(None, "chan"),
        P("batch", "chan", None),
    )
    return jax.shard_map(
        per_device,
        mesh=mesh,
        in_specs=placed,
        out_specs=(
            P("batch", "chan", None),
            P("batch", "chan", None),
            P("batch", None, "chan"),
            P(None, "batch", "chan"),
            P("chan", "batch"),
            P("batch", None, "chan"),
            P("chan", "batch"),
            P(),
            P(None, None, "chan"),
            P(None, "chan"),
        ),
        check_vma=False,
    )
```

```python
import functools
import math

import jax
import jax.numpy as jnp
import numpy as np
from jax import lax
from jax.experimental import pallas as pl
from jax.experimental.pallas import tpu as pltpu
from jax.sharding import PartitionSpec as P

EPSILON = 1e-05
LOW = jnp.bfloat16
WIDE = jnp.float32
RING = (0, 2, 4, 6, 7, 5, 3, 1)
CODES = (0, 2, 1, 3)
LANES = 256


def dot(left, right, left_dim, right_dim, kind=WIDE):
    return lax.dot_general(
        left, right, (((left_dim,), (right_dim,)), ((), ())), preferred_element_type=kind
    )


@functools.lru_cache(maxsize=None)
def wave_tables(length, tiles=4):
    bins = np.arange(length, dtype=np.int64)[:, None]
    places = np.arange(length, dtype=np.int64)[None, :]
    turns = ((2 * bins + 1) * places) % (4 * length)
    angles = turns * (2.0 * math.pi / (4 * length))
    both = np.stack(
        [
            np.cos(angles).reshape(tiles, length // tiles, length),
            -np.sin(angles).reshape(tiles, length // tiles, length),
        ],
        axis=1,
    ).reshape(2 * length, length)
    return both.astype(jnp.bfloat16), np.ascontiguousarray(both.T).astype(jnp.bfloat16)


def swap(block, step):
    size = lax.axis_size("chan")
    return lax.ppermute(block, "chan", [(i, i ^ step) for i in range(size)])


def spread(block):
    far = swap(block, 2)
    near = swap(block, 1)
    return [block, far, near, swap(far, 1)]


def fold_far(keep, send):
    arrived = swap(send, 1)
    half = keep.shape[0] // 2
    away = (keep[half:] + arrived[half:].astype(WIDE)).astype(LOW)
    return arrived, swap(away, 2)


def after(values, *earlier):
    return lax.optimization_barrier((values, earlier))[0]


def ring_steps(block, shift):
    count = len(RING)
    pairs = [(RING[i], RING[(i + shift) % count]) for i in range(count)]
    return lax.ppermute(block, "batch", pairs)


def ring_place():
    index = lax.axis_index("batch")
    return jnp.where(index % 2 == 0, index // 2, len(RING) - 1 - index // 2)


def ring_member(place):
    place = lax.rem(place, len(RING))
    return jnp.where(place < len(RING) // 2, 2 * place, 2 * (len(RING) - 1 - place) + 1)


OFFSETS = (0, 7, 1, 6, 2, 5, 3)


def ring_blocks(block):
    half = block.shape[0] // 2
    blocks = [block]
    up = down = block
    for _ in range(3):
        up, down = ring_steps(up, 1), ring_steps(down, -1)
        blocks += [up, down]
    return blocks + [ring_steps(up[:half], 1), ring_steps(down[half:], -1)]


def place_rows_kernel(*refs):
    blocks, whole = refs[:9], refs[9]
    rows = blocks[0].shape[0]
    half = rows // 2
    place = ring_place()
    for block, offset in zip(blocks, OFFSETS):
        start = pl.multiple_of(ring_member(place + offset) * rows, rows)
        whole[pl.ds(start, rows), :] = block[...]
    start = pl.multiple_of(ring_member(place + 4) * rows, rows)
    whole[pl.ds(start, half), :] = blocks[7][...]
    whole[pl.ds(pl.multiple_of(start + half, half), half), :] = blocks[8][...]


def place_mixer_kernel(*refs):
    blocks, (w_in, filters, w_out, joined) = refs[:9], refs[9:]
    rows = blocks[0].shape[0]
    half = rows // 2
    spare = rows // 3
    channels = filters.shape[1] // 2
    gap = LANES - channels
    place = ring_place()
    joined[:half, :] = blocks[7][...]
    joined[half:, :] = blocks[8][...]
    w_out[:, channels:] = jnp.zeros((w_out.shape[0], gap), w_out.dtype)
    for block, offset in zip((*blocks[:7], joined), (*OFFSETS, 4)):
        member = ring_member(place + offset)
        start = pl.multiple_of(member * rows, rows)
        w_in[pl.ds(start, rows), :] = block[:, : 3 * LANES]
        for s in range(3):
            w_out[pl.ds(start, rows), s * gap : (s + 1) * gap] = block[
                :, s * LANES + channels : (s + 1) * LANES
            ]
        start = pl.multiple_of(member * (rows + spare), rows + spare)
        filters[pl.ds(start, rows), :] = block[:, 3 * LANES : 3 * LANES + 2 * channels]
        start = pl.multiple_of(start + rows, spare)
        for j in range(3):
            filters[pl.ds(start, spare), j * 128 : (j + 1) * 128] = block[
                j * spare : (j + 1) * spare, 3 * LANES + 2 * channels :
            ]


def gather_rows(block):
    count = lax.axis_size("batch")
    if count != len(RING):
        return lax.all_gather(block, "batch", axis=0, tiled=True)
    blocks = ring_blocks(block)
    shape = (count * block.shape[0],) + block.shape[1:]
    return call(place_rows_kernel, blocks, [NEAR] * 9, [(shape, block.dtype)], [NEAR], [], 1, "place_rows", 16)[0]


def gather_mixer(block, channels):
    count = lax.axis_size("batch")
    rows, columns = block.shape
    if count != len(RING):
        pack = lax.all_gather(block, "batch", axis=0, tiled=True)
        return unpack_mixer(pack, rows, channels), pack
    blocks = ring_blocks(block)
    whole = call(
        place_mixer_kernel,
        blocks,
        [NEAR] * 9,
        [
            ((count * rows, 3 * LANES), block.dtype),
            ((count * (rows + rows // 3), 2 * channels), block.dtype),
            ((count * rows, LANES), block.dtype),
        ],
        [NEAR] * 3,
        [pltpu.VMEM((rows, columns), block.dtype)],
        1,
        "place_mixer",
        16,
    )
    return whole, blocks[5:7]


def ring_sum(partial):
    count = lax.axis_size("batch")
    if count != len(RING):
        return lax.psum_scatter(
            partial.astype(LOW), "batch", scatter_dimension=0, tiled=True
        ).astype(WIDE)
    place = ring_place()
    rows = partial.shape[0] // count
    half = rows // 2

    def part(offset, first=0, size=rows):
        start = ring_member(place + offset) * rows + first
        return lax.dynamic_slice_in_dim(partial, start, size, 0).astype(WIDE)

    up = ring_steps(part(4, 0, half).astype(LOW), 1).astype(WIDE)
    down = ring_steps(part(4, half, half).astype(LOW), -1).astype(WIDE)
    up = part(3) + jnp.concatenate([up, jnp.zeros_like(up)], axis=0)
    down = part(5) + jnp.concatenate([jnp.zeros_like(down), down], axis=0)
    for step in (2, 1, 0):
        up = ring_steps(up.astype(LOW), 1).astype(WIDE)
        down = ring_steps(down.astype(LOW), -1).astype(WIDE)
        if step:
            up = up + part(step)
            down = down + part(count - step)
    return up + down + part(0)


def small_sum(values, axis):
    size = lax.axis_size(axis)
    if size & (size - 1) or size > 8:
        return lax.psum(values, axis)
    step = 1
    while step < size:
        values = values + lax.ppermute(values, axis, [(i, i ^ step) for i in range(size)])
        step *= 2
    return values


def norm_forward(values):
    centre = jnp.mean(values, axis=-1, keepdims=True)
    scale = lax.rsqrt(jnp.mean(values * values, axis=-1, keepdims=True) - centre * centre + EPSILON)
    return (values - centre) * scale, scale


def block_start(code, rows):
    return pl.multiple_of((lax.axis_index("chan") ^ code) * rows, rows)


def shifted(series, offset, row):
    if offset == 0:
        return series
    length = series.shape[0]
    moved = pltpu.roll(series, offset % length, 0)
    inside = row >= offset if offset > 0 else row < length + offset
    return jnp.where(inside, moved, 0.0)


def tap_sum(series, taps, first, row, direction):
    total = taps[first : first + 1, :] * series
    for j in (1, 2):
        total = total + taps[first + j : first + j + 1, :] * shifted(series, direction * j, row)
    return total


def mixer_kernel(
    index, lengths, buckets, t0, t1, t2, t3, w_in, filters, taps, gain, waves, waves_t,
    mixed, h_first, projected, convolved, kernel_spec, series_spec,
    waves_buf, waves_t_buf, kernel_buf, series_buf, product_buf, gate_buf, sems,
):
    first_copy = pltpu.make_async_copy(waves, waves_buf, sems.at[0])
    second_copy = pltpu.make_async_copy(waves_t, waves_t_buf, sems.at[1])
    first_copy.start()
    second_copy.start()
    rows = t0.shape[1]
    for code, block in zip(CODES, (t0, t1, t2, t3)):
        normed, _ = norm_forward(block[0].astype(WIDE))
        low = (normed * gain[...]).astype(LOW)
        place = pl.ds(block_start(code, rows), rows)
        h_first[place, :] = low
        projected[place, :] = dot(low, w_in[...], 1, 0).astype(LOW)
    length = projected.shape[0]
    row = lax.broadcasted_iota(jnp.int32, (length, LANES), 0)
    mask = (row < lengths[index]).astype(WIDE)

    def stream(s):
        raw = projected[:, s * LANES : (s + 1) * LANES].astype(WIDE)
        return mask * tap_sum(raw, taps, 3 * s, row, 1)

    channels = filters.shape[1] // 2
    both = filters[...].astype(WIDE)
    chosen = jnp.where(buckets[index] == 0, both, pltpu.roll(both, channels, 1))[:, :LANES]
    kernel_buf[...] = (chosen + tap_sum(stream(1), taps, 9, row, 1)).astype(LOW)
    series_buf[...] = stream(2).astype(LOW)
    gate_buf[...] = stream(0)
    first_copy.wait()
    tiles = 4
    size = 2 * length // tiles
    half = size // 2
    for i in range(tiles):
        place = slice(i * size, (i + 1) * size)
        table = waves_buf[place, :]
        k = dot(table, kernel_buf[...], 1, 0)
        s = dot(table, series_buf[...], 1, 0)
        kernel_spec[place, :] = k.astype(LOW)
        series_spec[place, :] = s.astype(LOW)
        kr, ki, sr, si = k[:half], k[half:], s[:half], s[half:]
        product_buf[i * size : i * size + half, :] = (kr * sr - ki * si).astype(LOW)
        product_buf[i * size + half : (i + 1) * size, :] = (kr * si + ki * sr).astype(LOW)
    second_copy.wait()
    for i in range(2):
        place = slice(i * length // 2, (i + 1) * length // 2)
        value = dot(waves_t_buf[place, :], product_buf[...], 1, 0) * (1.0 / length)
        convolved[place, :] = value.astype(LOW)
        mixed[place, :] = (value * gate_buf[place, :]).astype(LOW)


def middle_kernel(
    index, lengths, t0, t1, t2, t3, c0, c1, c2, c3, m0, m1, m2, m3, o0, o1, o2, o3, gain, weights,
    h_out, grads_out, hidden_out, d_out_out, send_d, keep_d, send_o, keep_o, residual,
    weights_buf, h_buf, grads_buf, hidden_buf, d_out_buf, sems,
):
    copy = pltpu.make_async_copy(weights, weights_buf, sems.at[0])
    copy.start()
    _, rows, width = t0.shape
    tokens, grads, mixed, outs = (t0, t1, t2, t3), (c0, c1, c2, c3), (m0, m1, m2, m3), (o0, o1, o2, o3)
    hidden = hidden_buf.shape[1]
    leaving = []
    for tile in (1, 0):
        whole = slice(tile * 2 * rows, (tile + 1) * 2 * rows)
        for block in (2 * tile, 2 * tile + 1):
            start = block_start(CODES[block], rows)
            place = slice(block * rows, (block + 1) * rows)
            value = tokens[block][0].astype(WIDE)
            for part, out in zip(mixed, outs):
                value = value + dot(part[pl.ds(start, rows), :], out[...], 1, 1)
            if block == 0:
                residual[...] = value
            normed, _ = norm_forward(value)
            h_buf[place, :] = (normed * gain[...]).astype(LOW)
            row = start + lax.broadcasted_iota(jnp.int32, (rows, width), 0)
            d_out_buf[place, :] = jnp.where(row < lengths[index], grads[block][0].astype(WIDE), 0.0).astype(LOW)
        if tile == 1:
            copy.wait()
        for first in range(0, hidden, 256):
            gate_place = slice(first, first + 256)
            up_place = slice(hidden + first, hidden + first + 256)
            down_place = slice(2 * hidden + first, 2 * hidden + first + 256)
            gate = dot(h_buf[whole, :], weights_buf[:, gate_place], 1, 0)
            up = dot(h_buf[whole, :], weights_buf[:, up_place], 1, 0)
            d_hidden = dot(d_out_buf[whole, :], weights_buf[:, down_place], 1, 0)
            slope = math.sqrt(2.0 / math.pi)
            square = gate * gate
            bent = jnp.tanh(slope * gate * (1.0 + 0.044715 * square))
            rise = 0.5 * (1.0 + bent)
            active = gate * rise
            hidden_buf[whole, gate_place] = (active * up).astype(LOW)
            d_active = rise + 0.5 * gate * (1.0 - bent * bent) * (slope * (1.0 + 0.134145 * square))
            grads_buf[whole, gate_place] = (d_hidden * up * d_active).astype(LOW)
            grads_buf[whole, up_place] = (d_hidden * active).astype(LOW)
        moves = ((h_buf, h_out), (grads_buf, grads_out), (hidden_buf, hidden_out), (d_out_buf, d_out_out))
        for i, (source, target) in enumerate(moves):
            leave = pltpu.make_async_copy(
                source.at[whole, :], target.at[whole, :], sems.at[1 + 4 * tile + i]
            )
            leave.start()
            leaving.append(leave)
        d_normed = dot(grads_buf[whole, :], weights_buf[:, : 2 * hidden], 1, 1)
        out = dot(hidden_buf[whole, :], weights_buf[:, 2 * hidden :], 1, 1)
        if tile == 1:
            send_d[...] = d_normed.astype(LOW)
            send_o[...] = out.astype(LOW)
        else:
            keep_d[...] = d_normed
            keep_o[...] = out
    for leave in leaving:
        leave.wait()


def norm_kernel(keep, arrived, last, values, extra, gain, d_wide, d_low, gain_grad):
    d_out = keep[...] + arrived[...].astype(WIDE) + last[...].astype(WIDE)
    normed, scale = norm_forward(values[...].reshape(d_out.shape).astype(WIDE))
    scaled = d_out * gain[...]
    first_mean = jnp.mean(scaled, axis=-1, keepdims=True)
    second_mean = jnp.mean(scaled * normed, axis=-1, keepdims=True)
    total = extra[...].astype(WIDE) + scale * (scaled - first_mean - normed * second_mean)
    d_wide[...] = total
    d_low[...] = total.astype(LOW)
    gain_grad[...] = jnp.sum(d_out * normed, axis=0, keepdims=True)


def back_kernel(
    index, lengths, b0, b1, b2, b3, w_out, w_in, mixed, projected, convolved, kernel_spec, series_spec, taps, waves, waves_t,
    d_projected, d_kernel, tap_grads, out_grad, send, keep,
    waves_buf, waves_t_buf, mix_buf, conv_buf, product_k, product_s, d_series, sems,
):
    first_copy = pltpu.make_async_copy(waves, waves_buf, sems.at[0])
    second_copy = pltpu.make_async_copy(waves_t, waves_t_buf, sems.at[1])
    first_copy.start()
    second_copy.start()
    rows = b0.shape[0]
    for i, (code, block) in enumerate(zip(CODES, (b0, b1, b2, b3))):
        place = pl.ds(block_start(code, rows), rows)
        mix_buf[place, :] = dot(block[...], w_out[...], 1, 0)
        part = dot(block[...], mixed[place, :], 0, 0)
        out_grad[...] = part if i == 0 else out_grad[...] + part
    length = projected.shape[0]
    row = lax.broadcasted_iota(jnp.int32, (length, LANES), 0)
    mask = (row < lengths[index]).astype(WIDE)

    def raw(s):
        return projected[:, s * LANES : (s + 1) * LANES].astype(WIDE)

    conv_buf[...] = (mix_buf[...] * mask * tap_sum(raw(0), taps, 0, row, 1)).astype(LOW)
    first_copy.wait()
    tiles = 4
    size = 2 * length // tiles
    half = size // 2
    for i in range(tiles):
        upper, lower = slice(i * size, i * size + half), slice(i * size + half, (i + 1) * size)
        g = dot(waves_buf[i * size : (i + 1) * size, :], conv_buf[...], 1, 0)
        gr, gi = g[:half], g[half:]
        sr, si = series_spec[upper, :].astype(WIDE), series_spec[lower, :].astype(WIDE)
        product_k[upper, :] = (gr * sr + gi * si).astype(LOW)
        product_k[lower, :] = (gi * sr - gr * si).astype(LOW)
        kr, ki = kernel_spec[upper, :].astype(WIDE), kernel_spec[lower, :].astype(WIDE)
        product_s[upper, :] = (gr * kr + gi * ki).astype(LOW)
        product_s[lower, :] = (gi * kr - gr * ki).astype(LOW)
    second_copy.wait()
    for i in range(2):
        place = slice(i * length // 2, (i + 1) * length // 2)
        d_kernel[place, :] = dot(waves_t_buf[place, :], product_k[...], 1, 0) * (1.0 / length)
        d_series[place, :] = dot(waves_t_buf[place, :], product_s[...], 1, 0) * (1.0 / length)

    def finish(s, grads):
        series = raw(s)
        for j in range(3):
            tap_grads[3 * s + j : 3 * s + j + 1, :] = jnp.sum(
                grads * shifted(series, j, row), axis=0, keepdims=True
            )
        d_projected[:, s * LANES : (s + 1) * LANES] = tap_sum(grads, taps, 3 * s, row, -1).astype(LOW)

    finish(0, mix_buf[...] * convolved[...].astype(WIDE) * mask)
    finish(2, d_series[...] * mask)
    grads = d_kernel[...]
    condition = mask * tap_sum(raw(1), taps, 3, row, 1)
    for j in range(3):
        tap_grads[9 + j : 10 + j, :] = jnp.sum(
            grads * shifted(condition, j, row), axis=0, keepdims=True
        )
    finish(1, mask * tap_sum(grads, taps, 9, row, -1))
    for i, code in enumerate(CODES):
        place = pl.ds(block_start(code, rows), rows)
        part = dot(d_projected[place, :], w_in[...], 1, 1)
        if i < 2:
            keep[i * rows : (i + 1) * rows, :] = part
        else:
            send[(i - 2) * rows : (i - 1) * rows, :] = part.astype(LOW)


def tail_kernel(packed, channels, buckets, h0, h1, p0, p1, g0, g1, k0, k1, w_in, gain, grads, gain_grad, filters):
    gap = LANES - channels
    width = w_in.shape[0]
    out_grad = g0[...] + g1[...]
    lane = lax.broadcasted_iota(jnp.int32, (width, LANES), 1)
    total = jnp.zeros((width, 1), WIDE)
    for s in range(3):
        place = slice(s * LANES, (s + 1) * LANES)
        grad = dot(h0[...], p0[:, place], 0, 0) + dot(h1[...], p1[:, place], 0, 0)
        total = total + jnp.sum(grad * w_in[:, place].astype(WIDE), axis=1, keepdims=True)
        behind = pltpu.roll(out_grad, channels - s * gap, 1)
        grads[:, place] = jnp.where(lane < channels, grad, behind).astype(LOW)
    gain_grad[...] = total / gain[...]
    first = [jnp.where(buckets[r] == 0, 1.0, 0.0) for r in range(2)]
    parts = [k0[...], k1[...]]
    zeros = jnp.zeros((k0.shape[0], 2 * channels - LANES), WIDE)
    sums = [
        jnp.concatenate([parts[0] * a + parts[1] * b, zeros], axis=1)
        for a, b in (first, [1.0 - first[0], 1.0 - first[1]])
    ]
    filters[...] = (sums[0] + pltpu.roll(sums[1], channels, 1)).astype(filters.dtype)
    if packed:
        rows = width // len(RING)
        spare = rows // 3
        for i in range(len(RING)):
            start = i * (rows + spare)
            place = slice(i * rows, (i + 1) * rows)
            grads[place, 3 * LANES : 3 * LANES + 2 * channels] = filters[start : start + rows, :].astype(LOW)
            for j in range(3):
                place = slice(i * rows + j * spare, i * rows + (j + 1) * spare)
                grads[place, 3 * LANES + 2 * channels :] = filters[
                    start + rows : start + rows + spare, j * 128 : (j + 1) * 128
                ].astype(LOW)


ANY = pl.BlockSpec(memory_space=pl.ANY)
SCALARS = pl.BlockSpec(memory_space=pltpu.SMEM)
NEAR = pl.BlockSpec(memory_space=pltpu.VMEM)


def call(kernel, operands, kinds, results, result_kinds, scratch, flops, name, limit=50):
    moved = sum(x.size * x.dtype.itemsize for x in operands)
    moved += sum(math.prod(shape) * jnp.dtype(kind).itemsize for shape, kind in results)
    return pl.pallas_call(
        kernel,
        grid=(1,),
        in_specs=kinds,
        out_specs=result_kinds,
        out_shape=[jax.ShapeDtypeStruct(shape, kind) for shape, kind in results],
        scratch_shapes=scratch,
        compiler_params=pltpu.CompilerParams(vmem_limit_bytes=limit * 2**20),
        cost_estimate=pl.CostEstimate(flops=flops, bytes_accessed=moved, transcendentals=0),
        name=name,
    )(*operands)


def row_block(index, array):
    return pl.BlockSpec((1,) + array.shape[1:], lambda _: (index, 0, 0))


def first_rows(rows, array):
    return pl.BlockSpec((rows, array.shape[1]), lambda _: (0, 0))


def mixer_forward(index, scalars, tokens, w_in, filters, taps, gain, tables):
    _, rows, width = tokens[0].shape
    length = 4 * rows
    spec = ((2 * length, LANES), LOW)
    return call(
        functools.partial(mixer_kernel, index),
        [*scalars, *tokens, w_in, filters, taps, gain, *tables],
        [SCALARS] * 2 + [row_block(index, tokens[0])] * 4 + [NEAR] * 4 + [ANY] * 2,
        [
            ((length, LANES), LOW),
            ((length, width), LOW),
            ((length, 3 * LANES), LOW),
            ((length, LANES), LOW),
            spec,
            spec,
        ],
        [NEAR] * 6,
        [
            pltpu.VMEM((2 * length, length), LOW),
            pltpu.VMEM((length, 2 * length), LOW),
            pltpu.VMEM((length, LANES), LOW),
            pltpu.VMEM((length, LANES), LOW),
            pltpu.VMEM((2 * length, LANES), LOW),
            pltpu.VMEM((length, LANES), WIDE),
            pltpu.SemaphoreType.DMA((2,)),
        ],
        15 * 10**9,
        "mixer",
    )


def middle(index, lengths, tokens, grads, mixed, outs, gain, weights):
    _, rows, width = tokens[0].shape
    length = 4 * rows
    hidden = weights.shape[1] // 3
    return call(
        functools.partial(middle_kernel, index),
        [lengths, *tokens, *grads, *mixed, *outs, gain, weights],
        [SCALARS] + [row_block(index, tokens[0])] * 8 + [NEAR] * 9 + [ANY],
        [
            ((length, width), LOW),
            ((length, 2 * hidden), LOW),
            ((length, hidden), LOW),
            ((length, width), LOW),
            ((2 * rows, width), LOW),
            ((2 * rows, width), WIDE),
            ((2 * rows, width), LOW),
            ((2 * rows, width), WIDE),
            ((rows, width), WIDE),
        ],
        [ANY] * 4 + [NEAR] * 5,
        [
            pltpu.VMEM((width, 3 * hidden), LOW),
            pltpu.VMEM((length, width), LOW),
            pltpu.VMEM((length, 2 * hidden), LOW),
            pltpu.VMEM((length, hidden), LOW),
            pltpu.VMEM((length, width), LOW),
            pltpu.SemaphoreType.DMA((9,)),
        ],
        19 * 10**9,
        "middle",
    )


def norm_back(keep, arrived, last, values, value_kind, extra, gain):
    rows, width = last.shape
    return call(
        norm_kernel,
        [keep, arrived, last, values, extra, gain],
        [first_rows(rows, keep), first_rows(rows, arrived), NEAR, value_kind, first_rows(rows, extra), NEAR],
        [((rows, width), WIDE), ((rows, width), LOW), ((1, width), WIDE)],
        [NEAR] * 3,
        [],
        2 * 10**9,
        "norm_back",
        20,
    )


def mixer_backward(index, lengths, grads, w_out, w_in, kept, taps, tables):
    rows, width = grads[0].shape
    length = 4 * rows
    mixed, projected, convolved, kernel_spec, series_spec = kept
    return call(
        functools.partial(back_kernel, index),
        [lengths, *grads, w_out, w_in, mixed, projected, convolved, kernel_spec, series_spec, taps, *tables],
        [SCALARS] + [NEAR] * 12 + [ANY] * 2,
        [
            ((length, 3 * LANES), LOW),
            ((length, LANES), WIDE),
            ((12, LANES), WIDE),
            ((width, LANES), WIDE),
            ((2 * rows, width), LOW),
            ((2 * rows, width), WIDE),
        ],
        [NEAR] * 6,
        [
            pltpu.VMEM((2 * length, length), LOW),
            pltpu.VMEM((length, 2 * length), LOW),
            pltpu.VMEM((length, LANES), WIDE),
            pltpu.VMEM((length, LANES), LOW),
            pltpu.VMEM((2 * length, LANES), LOW),
            pltpu.VMEM((2 * length, LANES), LOW),
            pltpu.VMEM((length, LANES), WIDE),
            pltpu.SemaphoreType.DMA((2,)),
        ],
        19 * 10**9,
        "mixer_back",
    )


def tail(packed, channels, buckets, h_first, d_projected, out_grads, d_kernels, w_in, gain):
    length, width = h_first[0].shape
    extra = 2 * channels + 128 if packed else 0
    return call(
        functools.partial(tail_kernel, packed, channels),
        [buckets, *h_first, *d_projected, *out_grads, *d_kernels, w_in, gain],
        [SCALARS] + [NEAR] * 10,
        [
            ((width, 3 * LANES + extra), LOW),
            ((width, 1), WIDE),
            ((length, 2 * channels), WIDE),
        ],
        [NEAR] * 3,
        [],
        6 * 10**9,
        "tail",
    )


def pack_mixer(w_in, long_filter, w_out):
    rows, _, channels = w_in.shape
    gap = LANES - channels
    turned = w_out.T
    pieces = []
    for s in range(3):
        pieces += [w_in[:, s], turned[:, s * gap : (s + 1) * gap]]
    both = jnp.concatenate([long_filter[0], long_filter[1]], axis=1)
    spare = both[rows:].reshape(both.shape[0] - rows, 3, -1)
    pieces += [both[:rows], spare.transpose(1, 0, 2).reshape(rows, -1)]
    return jnp.concatenate(pieces, axis=1)


def unpack_rows(blocks, channels):
    count, rows, _ = blocks.shape
    spare = blocks[:, :, 2 * channels :].reshape(count, 3, rows // 3, -1)
    spare = spare.transpose(0, 2, 1, 3).reshape(count, rows // 3, -1)
    return jnp.concatenate([blocks[:, :, : 2 * channels], spare], axis=1)


def unpack_out(pack, channels):
    gap = LANES - channels
    return jnp.concatenate(
        [pack[:, s * LANES + channels : s * LANES + channels + gap] for s in range(3)], axis=1
    )


def unpack_mixer(pack, rows, channels):
    w_out = jnp.pad(unpack_out(pack, channels), ((0, 0), (0, LANES - channels)))
    blocks = pack[:, 3 * LANES :].reshape(-1, rows, pack.shape[1] - 3 * LANES)
    filters = unpack_rows(blocks, channels).reshape(-1, 2 * channels)
    return pack[:, : 3 * LANES], filters, w_out


def per_device(
    tokens,
    lengths,
    buckets,
    w_in,
    long_filter,
    w_out,
    w_gu,
    w_down,
    norm_gains,
    short_taps,
    cond_taps,
    cotangent,
):
    me = lax.axis_index("chan")
    row_count, part_len, width = tokens.shape
    channels = short_taps.shape[-1]
    hidden = w_down.shape[0]
    shard = w_in.shape[0]
    rows = range(row_count)
    gains = norm_gains.astype(WIDE)
    taps = jnp.concatenate([short_taps.reshape(9, channels), cond_taps], axis=0).astype(WIDE)
    taps = jnp.pad(taps, ((0, 0), (0, LANES - channels)))
    tables = tuple(jnp.asarray(table) for table in wave_tables(4 * part_len))
    local = me * part_len + jnp.arange(part_len, dtype=jnp.int32)[:, None]
    own = [local < lengths[r] for r in rows]

    all_tokens = spread(tokens)
    (full_in, filters, part_out), packed_last = gather_mixer(
        pack_mixer(w_in, long_filter, w_out), channels
    )
    outs = spread(part_out)
    w_ff = jnp.concatenate([w_gu.reshape(shard, -1), w_down.T], axis=1)
    weights = gather_rows(after(w_ff, packed_last))

    forward = [
        mixer_forward(r, (lengths, buckets), all_tokens, full_in, filters, taps, gains[:1], tables)
        for r in rows
    ]
    all_grads = spread(after(cotangent, all_tokens))
    mixed = [spread(forward[r][0]) for r in rows]
    centre = [
        middle(r, lengths, all_tokens, all_grads, mixed[r], outs, gains[1:], weights) for r in rows
    ]

    d_residual = []
    gain_second = 0.0
    backward = []
    folded = [fold_far(centre[r][5], centre[r][4]) for r in rows]
    for r in rows:
        d_out, keep_d, residual = centre[r][3], centre[r][5], centre[r][8]
        arrived, last = folded[r]
        d_wide, d_low, gain_grad = norm_back(
            keep_d, arrived, last, residual, NEAR, d_out, gains[1:]
        )
        d_residual.append(d_wide)
        gain_second = gain_second + gain_grad
        kept = (forward[r][0],) + tuple(forward[r][2:])
        d_spread = spread(d_low)
        backward.append(
            mixer_backward(r, lengths, d_spread, part_out, full_in, kept, taps, tables)
        )

    kept_ff = after([centre[r][:4] for r in rows], [folded[r][0] for r in rows])
    grad_gu = sum(dot(kept_ff[r][0], kept_ff[r][1], 0, 0) for r in rows)
    grad_down = sum(dot(kept_ff[r][3], kept_ff[r][2], 0, 0) for r in rows)
    grad_ff = lax.psum_scatter(
        jnp.concatenate([grad_gu.astype(LOW), grad_down.astype(LOW)], axis=1),
        "batch",
        scatter_dimension=0,
        tiled=True,
    ).astype(WIDE)

    outputs = []
    d_inputs = []
    for r in rows:
        send_o, keep_o, residual = centre[r][6:]
        arrived, last = fold_far(keep_o, after(send_o, d_spread))
        final = residual + keep_o[:part_len] + arrived[:part_len].astype(WIDE) + last.astype(WIDE)
        outputs.append(jnp.where(own[r], final, 0.0).astype(LOW))
        send, keep = backward[r][4:]
        arrived, last = fold_far(keep, send)
        d_wide, _, _ = norm_back(
            keep, arrived, last, tokens, row_block(r, tokens), d_residual[r], gains[:1]
        )
        d_inputs.append(d_wide)

    packed = lax.axis_size("batch") == len(RING)
    grad_mixer, gain_first, grad_filter = tail(
        packed,
        channels,
        buckets,
        [forward[r][1] for r in rows],
        [backward[r][0] for r in rows],
        [backward[r][3] for r in rows],
        [backward[r][1] for r in rows],
        full_in,
        gains[0][:, None],
    )
    grad_mixer = ring_sum(grad_mixer)
    if packed:
        grad_filter = unpack_rows(grad_mixer[None, :, 3 * LANES :], channels)[0]
    else:
        grad_filter = ring_sum(grad_filter)
    grad_in = grad_mixer[:, : 3 * LANES].reshape(-1, 3, LANES)[:, :, :channels]
    grad_taps = sum(backward[r][2] for r in rows)[:, :channels]
    smalls = jnp.concatenate(
        [gain_first.reshape(-1), gain_second.reshape(-1), grad_taps.reshape(-1)]
    )
    smalls = small_sum(smalls.reshape(-1, 128), "batch").reshape(-1)
    grad_gains = small_sum(smalls[: 2 * width].reshape(-1, 128), "chan").reshape(2, width)
    grad_taps = smalls[2 * width :].reshape(12, channels)
    return (
        jnp.stack(outputs),
        jnp.stack(d_inputs),
        grad_in,
        jnp.stack([grad_filter[:, :channels], grad_filter[:, channels:]]),
        unpack_out(grad_mixer, channels).T,
        grad_ff[:, : 2 * hidden].reshape(-1, 2, hidden),
        grad_ff[:, 2 * hidden :].T,
        grad_gains,
        grad_taps[:9].reshape(3, 3, channels),
        grad_taps[9:],
    )


def solution(mesh):
    placed = (
        P("batch", "chan", None),
        P("batch"),
        P("batch"),
        P("batch", None, "chan"),
        P(None, "batch", "chan"),
        P("chan", "batch"),
        P("batch", None, "chan"),
        P("chan", "batch"),
        P(),
        P(None, None, "chan"),
        P(None, "chan"),
        P("batch", "chan", None),
    )
    return jax.shard_map(
        per_device,
        mesh=mesh,
        in_specs=placed,
        out_specs=(
            P("batch", "chan", None),
            P("batch", "chan", None),
            P("batch", None, "chan"),
            P(None, "batch", "chan"),
            P("chan", "batch"),
            P("batch", None, "chan"),
            P("chan", "batch"),
            P(),
            P(None, None, "chan"),
            P(None, "chan"),
        ),
        check_vma=False,
    )
```

```python
import functools
import math

import jax
import jax.numpy as jnp
import numpy as np
from jax import lax
from jax.experimental import pallas as pl
from jax.experimental.pallas import tpu as pltpu
from jax.sharding import PartitionSpec as P

EPSILON = 1e-05
LOW = jnp.bfloat16
WIDE = jnp.float32
RING = (0, 2, 4, 6, 7, 5, 3, 1)
CODES = (0, 2, 1, 3)
LANES = 256


def dot(left, right, left_dim, right_dim, kind=WIDE):
    return lax.dot_general(
        left, right, (((left_dim,), (right_dim,)), ((), ())), preferred_element_type=kind
    )


@functools.lru_cache(maxsize=None)
def wave_tables(length, tiles=4):
    bins = np.arange(length, dtype=np.int64)[:, None]
    places = np.arange(length, dtype=np.int64)[None, :]
    turns = ((2 * bins + 1) * places) % (4 * length)
    angles = turns * (2.0 * math.pi / (4 * length))
    both = np.stack(
        [
            np.cos(angles).reshape(tiles, length // tiles, length),
            -np.sin(angles).reshape(tiles, length // tiles, length),
        ],
        axis=1,
    ).reshape(2 * length, length)
    return both.astype(jnp.bfloat16), np.ascontiguousarray(both.T).astype(jnp.bfloat16)


def swap(block, step):
    size = lax.axis_size("chan")
    return lax.ppermute(block, "chan", [(i, i ^ step) for i in range(size)])


def after(values, *earlier):
    return lax.optimization_barrier((values, earlier))[0]


def spread(block, gate=None):
    far = swap(block, 2)
    near = swap(block, 1)
    return [block, far, near, swap(far if gate is None else after(far, gate), 1)]


def fold_near(send):
    return swap(send, 1)


def fold_far(keep, arrived):
    half = keep.shape[0] // 2
    return swap((keep[half:] + arrived[half:].astype(WIDE)).astype(LOW), 2)


def ring_steps(block, shift):
    count = len(RING)
    pairs = [(RING[i], RING[(i + shift) % count]) for i in range(count)]
    return lax.ppermute(block, "batch", pairs)


def ring_place():
    index = lax.axis_index("batch")
    return jnp.where(index % 2 == 0, index // 2, len(RING) - 1 - index // 2)


def ring_member(place):
    place = lax.rem(place, len(RING))
    return jnp.where(place < len(RING) // 2, 2 * place, 2 * (len(RING) - 1 - place) + 1)


OFFSETS = (0, 7, 1, 6, 2, 5, 3)


def ring_blocks(block):
    half = block.shape[0] // 2
    blocks = [block]
    up = down = block
    for _ in range(3):
        up, down = ring_steps(up, 1), ring_steps(down, -1)
        blocks += [up, down]
    return blocks + [ring_steps(up[:half], 1), ring_steps(down[half:], -1)]


def place_rows_kernel(*refs):
    blocks, whole = refs[:9], refs[9]
    rows = blocks[0].shape[0]
    half = rows // 2
    place = ring_place()
    for block, offset in zip(blocks, OFFSETS):
        start = pl.multiple_of(ring_member(place + offset) * rows, rows)
        whole[pl.ds(start, rows), :] = block[...]
    start = pl.multiple_of(ring_member(place + 4) * rows, rows)
    whole[pl.ds(start, half), :] = blocks[7][...]
    whole[pl.ds(pl.multiple_of(start + half, half), half), :] = blocks[8][...]


def place_mixer_kernel(*refs):
    blocks, (w_in, filters, w_out, joined) = refs[:9], refs[9:]
    rows = blocks[0].shape[0]
    half = rows // 2
    spare = rows // 3
    channels = filters.shape[1] // 2
    gap = LANES - channels
    place = ring_place()
    joined[:half, :] = blocks[7][...]
    joined[half:, :] = blocks[8][...]
    w_out[:, channels:] = jnp.zeros((w_out.shape[0], gap), w_out.dtype)
    for block, offset in zip((*blocks[:7], joined), (*OFFSETS, 4)):
        member = ring_member(place + offset)
        start = pl.multiple_of(member * rows, rows)
        w_in[pl.ds(start, rows), :] = block[:, : 3 * LANES]
        for s in range(3):
            w_out[pl.ds(start, rows), s * gap : (s + 1) * gap] = block[
                :, s * LANES + channels : (s + 1) * LANES
            ]
        start = pl.multiple_of(member * (rows + spare), rows + spare)
        filters[pl.ds(start, rows), :] = block[:, 3 * LANES : 3 * LANES + 2 * channels]
        start = pl.multiple_of(start + rows, spare)
        for j in range(3):
            filters[pl.ds(start, spare), j * 128 : (j + 1) * 128] = block[
                j * spare : (j + 1) * spare, 3 * LANES + 2 * channels :
            ]


def gather_rows(block):
    count = lax.axis_size("batch")
    if count != len(RING):
        return lax.all_gather(block, "batch", axis=0, tiled=True)
    blocks = ring_blocks(block)
    shape = (count * block.shape[0],) + block.shape[1:]
    return call(place_rows_kernel, blocks, [NEAR] * 9, [(shape, block.dtype)], [NEAR], [], 1, "place_rows")[0]


def gather_mixer(block, channels):
    count = lax.axis_size("batch")
    rows, columns = block.shape
    if count != len(RING):
        pack = lax.all_gather(block, "batch", axis=0, tiled=True)
        return unpack_mixer(pack, rows, channels), pack
    blocks = ring_blocks(block)
    whole = call(
        place_mixer_kernel,
        blocks,
        [NEAR] * 9,
        [
            ((count * rows, 3 * LANES), block.dtype),
            ((count * (rows + rows // 3), 2 * channels), block.dtype),
            ((count * rows, LANES), block.dtype),
        ],
        [NEAR] * 3,
        [pltpu.VMEM((rows, columns), block.dtype)],
        1,
        "place_mixer",
    )
    return whole, blocks[7:]


def ring_sums(partial):
    count = lax.axis_size("batch")
    if count != len(RING):
        total = lax.psum_scatter(partial.astype(LOW), "batch", scatter_dimension=0, tiled=True)
        for _ in range(4):
            gate = yield total
            if gate is not None:
                total = after(total, gate)
        yield total.astype(WIDE)
        return
    place = ring_place()
    rows = partial.shape[0] // count
    half = rows // 2

    def part(offset, first=0, size=rows):
        start = ring_member(place + offset) * rows + first
        return lax.dynamic_slice_in_dim(partial, start, size, 0).astype(WIDE)

    up, down = part(4, 0, half).astype(LOW), part(4, half, half).astype(LOW)
    gate = yield up, down
    if gate is not None:
        up, down = after((up, down), gate)
    up, down = ring_steps(up, 1).astype(WIDE), ring_steps(down, -1).astype(WIDE)
    up = part(3) + jnp.concatenate([up, jnp.zeros_like(up)], axis=0)
    down = part(5) + jnp.concatenate([jnp.zeros_like(down), down], axis=0)
    for step in (2, 1, 0):
        up, down = up.astype(LOW), down.astype(LOW)
        gate = yield up, down
        if gate is not None:
            up, down = after((up, down), gate)
        up, down = ring_steps(up, 1).astype(WIDE), ring_steps(down, -1).astype(WIDE)
        if step:
            up = up + part(step)
            down = down + part(count - step)
    yield up + down + part(0)


def small_sums(values, axis):
    size = lax.axis_size(axis)
    if size & (size - 1) or size > 8:
        values = lax.psum(values, axis)
        yield values
        yield values
        return
    step = 1
    while step < size:
        gate = yield values
        if gate is not None:
            values = after(values, gate)
        values = values + lax.ppermute(values, axis, [(i, i ^ step) for i in range(size)])
        step *= 2
    yield values


def norm_forward(values):
    centre = jnp.mean(values, axis=-1, keepdims=True)
    scale = lax.rsqrt(jnp.mean(values * values, axis=-1, keepdims=True) - centre * centre + EPSILON)
    return (values - centre) * scale, scale


def block_start(code, rows):
    return pl.multiple_of((lax.axis_index("chan") ^ code) * rows, rows)


def shifted(series, offset, row):
    if offset == 0:
        return series
    length = series.shape[0]
    moved = pltpu.roll(series, offset % length, 0)
    inside = row >= offset if offset > 0 else row < length + offset
    return jnp.where(inside, moved, 0.0)


def tap_sum(series, taps, first, row, direction):
    total = taps[first : first + 1, :] * series
    for j in (1, 2):
        total = total + taps[first + j : first + j + 1, :] * shifted(series, direction * j, row)
    return total


def mixer_kernel(
    index, lengths, buckets, t0, t1, t2, t3, w_in, filters, taps, gain, waves, waves_t,
    mixed, h_first, projected, convolved, kernel_spec, series_spec,
    waves_buf, waves_t_buf, kernel_buf, series_buf, product_buf, gate_buf, sems,
):
    first_copy = pltpu.make_async_copy(waves, waves_buf, sems.at[0])
    second_copy = pltpu.make_async_copy(waves_t, waves_t_buf, sems.at[1])
    first_copy.start()
    second_copy.start()
    rows = t0.shape[1]
    for code, block in zip(CODES, (t0, t1, t2, t3)):
        normed, _ = norm_forward(block[0].astype(WIDE))
        low = (normed * gain[...]).astype(LOW)
        place = pl.ds(block_start(code, rows), rows)
        h_first[place, :] = low
        projected[place, :] = dot(low, w_in[...], 1, 0).astype(LOW)
    length = projected.shape[0]
    row = lax.broadcasted_iota(jnp.int32, (length, LANES), 0)
    mask = (row < lengths[index]).astype(WIDE)

    def stream(s):
        raw = projected[:, s * LANES : (s + 1) * LANES].astype(WIDE)
        return mask * tap_sum(raw, taps, 3 * s, row, 1)

    channels = filters.shape[1] // 2
    both = filters[...].astype(WIDE)
    chosen = jnp.where(buckets[index] == 0, both, pltpu.roll(both, channels, 1))[:, :LANES]
    kernel_buf[...] = (chosen + tap_sum(stream(1), taps, 9, row, 1)).astype(LOW)
    series_buf[...] = stream(2).astype(LOW)
    gate_buf[...] = stream(0)
    first_copy.wait()
    tiles = 4
    size = 2 * length // tiles
    half = size // 2
    for i in range(tiles):
        place = slice(i * size, (i + 1) * size)
        table = waves_buf[place, :]
        k = dot(table, kernel_buf[...], 1, 0)
        s = dot(table, series_buf[...], 1, 0)
        kernel_spec[place, :] = k.astype(LOW)
        series_spec[place, :] = s.astype(LOW)
        kr, ki, sr, si = k[:half], k[half:], s[:half], s[half:]
        product_buf[i * size : i * size + half, :] = (kr * sr - ki * si).astype(LOW)
        product_buf[i * size + half : (i + 1) * size, :] = (kr * si + ki * sr).astype(LOW)
    second_copy.wait()
    for i in range(2):
        place = slice(i * length // 2, (i + 1) * length // 2)
        value = dot(waves_t_buf[place, :], product_buf[...], 1, 0) * (1.0 / length)
        convolved[place, :] = value.astype(LOW)
        mixed[place, :] = (value * gate_buf[place, :]).astype(LOW)


def middle_kernel(
    index, tile, lengths, t0, t1, c0, c1, m0, m1, m2, m3, o0, o1, o2, o3, gain, weights, gate_in,
    h_buf, grads_buf, hidden_buf, d_out_buf, *refs,
):
    del gate_in
    d_normed, out_sum = refs[:2]
    weights_buf, sems = refs[-2:]
    copy = pltpu.make_async_copy(weights, weights_buf, sems.at[0])
    copy.start()
    _, rows, width = t0.shape
    mixed, outs = (m0, m1, m2, m3), (o0, o1, o2, o3)
    hidden = hidden_buf.shape[1]
    for i, (tokens, grads) in enumerate(((t0, c0), (t1, c1))):
        start = block_start(CODES[2 * tile + i], rows)
        place = slice(i * rows, (i + 1) * rows)
        value = tokens[0].astype(WIDE)
        for part, out in zip(mixed, outs):
            value = value + dot(part[pl.ds(start, rows), :], out[...], 1, 1)
        if tile == 0 and i == 0:
            refs[2][...] = value
        normed, _ = norm_forward(value)
        h_buf[place, :] = (normed * gain[...]).astype(LOW)
        row = start + lax.broadcasted_iota(jnp.int32, (rows, width), 0)
        d_out_buf[place, :] = jnp.where(row < lengths[index], grads[0].astype(WIDE), 0.0).astype(LOW)
    copy.wait()
    for first in range(0, hidden, 256):
        gate_place = slice(first, first + 256)
        up_place = slice(hidden + first, hidden + first + 256)
        down_place = slice(2 * hidden + first, 2 * hidden + first + 256)
        gate = dot(h_buf[...], weights_buf[:, gate_place], 1, 0)
        up = dot(h_buf[...], weights_buf[:, up_place], 1, 0)
        d_hidden = dot(d_out_buf[...], weights_buf[:, down_place], 1, 0)
        slope = math.sqrt(2.0 / math.pi)
        square = gate * gate
        bent = jnp.tanh(slope * gate * (1.0 + 0.044715 * square))
        rise = 0.5 * (1.0 + bent)
        active = gate * rise
        hidden_buf[:, gate_place] = (active * up).astype(LOW)
        d_active = rise + 0.5 * gate * (1.0 - bent * bent) * (slope * (1.0 + 0.134145 * square))
        grads_buf[:, gate_place] = (d_hidden * up * d_active).astype(LOW)
        grads_buf[:, up_place] = (d_hidden * active).astype(LOW)
    d_normed[...] = dot(grads_buf[...], weights_buf[:, : 2 * hidden], 1, 1).astype(d_normed.dtype)
    out_sum[...] = dot(hidden_buf[...], weights_buf[:, 2 * hidden :], 1, 1).astype(out_sum.dtype)


def norm_step(d_out, values, extra, gain):
    normed, scale = norm_forward(values)
    scaled = d_out * gain
    first_mean = jnp.mean(scaled, axis=-1, keepdims=True)
    second_mean = jnp.mean(scaled * normed, axis=-1, keepdims=True)
    return extra + scale * (scaled - first_mean - normed * second_mean), normed


def norm_kernel(keep, arrived, last, values, extra, gain, d_wide, d_low, gain_grad):
    d_out = keep[...] + arrived[...].astype(WIDE) + last[...].astype(WIDE)
    total, normed = norm_step(d_out, values[...], extra[...].astype(WIDE), gain[...])
    d_wide[...] = total
    d_low[...] = total.astype(LOW)
    gain_grad[...] = jnp.sum(d_out * normed, axis=0, keepdims=True)


def finish_kernel(k0, k1, a0, a1, l0, l1, tokens, e0, e1, gain, result):
    for r, (keep, arrived, last, extra) in enumerate(((k0, a0, l0, e0), (k1, a1, l1, e1))):
        d_out = keep[...] + arrived[...].astype(WIDE) + last[...].astype(WIDE)
        result[r], _ = norm_step(d_out, tokens[r].astype(WIDE), extra[...], gain[...])


def output_kernel(lengths, k0, k1, a0, a1, l0, l1, r0, r1, result):
    for r, (keep, arrived, last, residual) in enumerate(((k0, a0, l0, r0), (k1, a1, l1, r1))):
        value = residual[...] + keep[...] + arrived[...].astype(WIDE) + last[...].astype(WIDE)
        row = block_start(0, value.shape[0]) + lax.broadcasted_iota(jnp.int32, value.shape, 0)
        result[r] = jnp.where(row < lengths[r], value, 0.0).astype(LOW)


def back_kernel(
    index, lengths, b0, b1, b2, b3, w_out, w_in, mixed, projected, convolved, kernel_spec, series_spec, taps, waves, waves_t,
    d_projected, d_kernel, tap_grads, out_grad, send, keep,
    waves_buf, waves_t_buf, mix_buf, conv_buf, product_k, product_s, d_series, sems,
):
    first_copy = pltpu.make_async_copy(waves, waves_buf, sems.at[0])
    second_copy = pltpu.make_async_copy(waves_t, waves_t_buf, sems.at[1])
    first_copy.start()
    second_copy.start()
    rows = b0.shape[0]
    for i, (code, block) in enumerate(zip(CODES, (b0, b1, b2, b3))):
        place = pl.ds(block_start(code, rows), rows)
        mix_buf[place, :] = dot(block[...], w_out[...], 1, 0)
        part = dot(block[...], mixed[place, :], 0, 0)
        out_grad[...] = part if i == 0 else out_grad[...] + part
    length = projected.shape[0]
    row = lax.broadcasted_iota(jnp.int32, (length, LANES), 0)
    mask = (row < lengths[index]).astype(WIDE)

    def raw(s):
        return projected[:, s * LANES : (s + 1) * LANES].astype(WIDE)

    conv_buf[...] = (mix_buf[...] * mask * tap_sum(raw(0), taps, 0, row, 1)).astype(LOW)
    first_copy.wait()
    tiles = 4
    size = 2 * length // tiles
    half = size // 2
    for i in range(tiles):
        upper, lower = slice(i * size, i * size + half), slice(i * size + half, (i + 1) * size)
        g = dot(waves_buf[i * size : (i + 1) * size, :], conv_buf[...], 1, 0)
        gr, gi = g[:half], g[half:]
        sr, si = series_spec[upper, :].astype(WIDE), series_spec[lower, :].astype(WIDE)
        product_k[upper, :] = (gr * sr + gi * si).astype(LOW)
        product_k[lower, :] = (gi * sr - gr * si).astype(LOW)
        kr, ki = kernel_spec[upper, :].astype(WIDE), kernel_spec[lower, :].astype(WIDE)
        product_s[upper, :] = (gr * kr + gi * ki).astype(LOW)
        product_s[lower, :] = (gi * kr - gr * ki).astype(LOW)
    second_copy.wait()
    for i in range(2):
        place = slice(i * length // 2, (i + 1) * length // 2)
        d_kernel[place, :] = dot(waves_t_buf[place, :], product_k[...], 1, 0) * (1.0 / length)
        d_series[place, :] = dot(waves_t_buf[place, :], product_s[...], 1, 0) * (1.0 / length)

    def finish(s, grads):
        series = raw(s)
        for j in range(3):
            tap_grads[3 * s + j : 3 * s + j + 1, :] = jnp.sum(
                grads * shifted(series, j, row), axis=0, keepdims=True
            )
        d_projected[:, s * LANES : (s + 1) * LANES] = tap_sum(grads, taps, 3 * s, row, -1).astype(LOW)

    finish(0, mix_buf[...] * convolved[...].astype(WIDE) * mask)
    finish(2, d_series[...] * mask)
    grads = d_kernel[...]
    condition = mask * tap_sum(raw(1), taps, 3, row, 1)
    for j in range(3):
        tap_grads[9 + j : 10 + j, :] = jnp.sum(
            grads * shifted(condition, j, row), axis=0, keepdims=True
        )
    finish(1, mask * tap_sum(grads, taps, 9, row, -1))
    for i, code in enumerate(CODES):
        place = pl.ds(block_start(code, rows), rows)
        part = dot(d_projected[place, :], w_in[...], 1, 1)
        if i < 2:
            keep[i * rows : (i + 1) * rows, :] = part
        else:
            send[(i - 2) * rows : (i - 1) * rows, :] = part.astype(LOW)


def tail_kernel(packed, channels, buckets, grad_in, g0, g1, k0, k1, w_in, gain, grads, gain_grad, filters):
    gap = LANES - channels
    width = w_in.shape[0]
    out_grad = g0[...] + g1[...]
    lane = lax.broadcasted_iota(jnp.int32, (width, LANES), 1)
    total = jnp.zeros((width, 1), WIDE)
    for s in range(3):
        place = slice(s * LANES, (s + 1) * LANES)
        grad = grad_in[:, place]
        total = total + jnp.sum(grad * w_in[:, place].astype(WIDE), axis=1, keepdims=True)
        behind = pltpu.roll(out_grad, channels - s * gap, 1)
        grads[:, place] = jnp.where(lane < channels, grad, behind).astype(LOW)
    gain_grad[...] = total / gain[...]
    first = [jnp.where(buckets[r] == 0, 1.0, 0.0) for r in range(2)]
    parts = [k0[...], k1[...]]
    zeros = jnp.zeros((k0.shape[0], 2 * channels - LANES), WIDE)
    sums = [
        jnp.concatenate([parts[0] * a + parts[1] * b, zeros], axis=1)
        for a, b in (first, [1.0 - first[0], 1.0 - first[1]])
    ]
    filters[...] = (sums[0] + pltpu.roll(sums[1], channels, 1)).astype(filters.dtype)
    if packed:
        rows = width // len(RING)
        spare = rows // 3
        for i in range(len(RING)):
            start = i * (rows + spare)
            place = slice(i * rows, (i + 1) * rows)
            grads[place, 3 * LANES : 3 * LANES + 2 * channels] = filters[start : start + rows, :].astype(LOW)
            for j in range(3):
                place = slice(i * rows + j * spare, i * rows + (j + 1) * spare)
                grads[place, 3 * LANES + 2 * channels :] = filters[
                    start + rows : start + rows + spare, j * 128 : (j + 1) * 128
                ].astype(LOW)


ANY = pl.BlockSpec(memory_space=pl.ANY)
SCALARS = pl.BlockSpec(memory_space=pltpu.SMEM)
NEAR = pl.BlockSpec(memory_space=pltpu.VMEM)


def call(kernel, operands, kinds, results, result_kinds, scratch, flops, name, limit=60):
    moved = sum(x.size * x.dtype.itemsize for x in operands)
    moved += sum(math.prod(shape) * jnp.dtype(kind).itemsize for shape, kind in results)
    return pl.pallas_call(
        kernel,
        grid=(1,),
        in_specs=kinds,
        out_specs=result_kinds,
        out_shape=[jax.ShapeDtypeStruct(shape, kind) for shape, kind in results],
        scratch_shapes=scratch,
        compiler_params=pltpu.CompilerParams(vmem_limit_bytes=limit * 2**20),
        cost_estimate=pl.CostEstimate(flops=flops, bytes_accessed=moved, transcendentals=0),
        name=name,
    )(*operands)


def row_block(index, array):
    return pl.BlockSpec((1,) + array.shape[1:], lambda _: (index, 0, 0))


def first_rows(rows, array):
    return pl.BlockSpec((rows, array.shape[1]), lambda _: (0, 0))


def mixer_forward(index, scalars, tokens, w_in, filters, taps, gain, tables):
    _, rows, width = tokens[0].shape
    length = 4 * rows
    spec = ((2 * length, LANES), LOW)
    return call(
        functools.partial(mixer_kernel, index),
        [*scalars, *tokens, w_in, filters, taps, gain, *tables],
        [SCALARS] * 2 + [row_block(index, tokens[0])] * 4 + [NEAR] * 4 + [ANY] * 2,
        [
            ((length, LANES), LOW),
            ((length, width), LOW),
            ((length, 3 * LANES), LOW),
            ((length, LANES), LOW),
            spec,
            spec,
        ],
        [NEAR] * 6,
        [
            pltpu.VMEM((2 * length, length), LOW),
            pltpu.VMEM((length, 2 * length), LOW),
            pltpu.VMEM((length, LANES), LOW),
            pltpu.VMEM((length, LANES), LOW),
            pltpu.VMEM((2 * length, LANES), LOW),
            pltpu.VMEM((length, LANES), WIDE),
            pltpu.SemaphoreType.DMA((2,)),
        ],
        15 * 10**9,
        "mixer",
    )


def middle(index, tile, lengths, tokens, grads, mixed, outs, gain, weights, gate):
    _, rows, width = tokens[0].shape
    length = 2 * rows
    hidden = weights.shape[1] // 3
    kind = LOW if tile else WIDE
    results = [
        ((length, width), LOW),
        ((length, 2 * hidden), LOW),
        ((length, hidden), LOW),
        ((length, width), LOW),
        ((length, width), kind),
        ((length, width), kind),
    ]
    if tile == 0:
        results.append(((rows, width), WIDE))
    half = slice(2 * tile, 2 * tile + 2)
    return call(
        functools.partial(middle_kernel, index, tile),
        [lengths, *tokens[half], *grads[half], *mixed, *outs, gain, weights, gate],
        [SCALARS] + [row_block(index, tokens[0])] * 4 + [NEAR] * 9 + [ANY] * 2,
        results,
        [NEAR] * len(results),
        [
            pltpu.VMEM((width, 3 * hidden), LOW),
            pltpu.SemaphoreType.DMA((1,)),
        ],
        10**10,
        "middle",
    )


def norm_back(keep, arrived, last, values, extra, gain):
    rows, width = last.shape
    return call(
        norm_kernel,
        [keep, arrived, last, values, extra, gain],
        [first_rows(rows, keep), first_rows(rows, arrived), NEAR, NEAR, first_rows(rows, extra), NEAR],
        [((rows, width), WIDE), ((rows, width), LOW), ((1, width), WIDE)],
        [NEAR] * 3,
        [],
        2 * 10**9,
        "norm_back",
        24,
    )


def finish(keeps, arrived, lasts, tokens, extras, gain):
    rows, width = lasts[0].shape
    return call(
        finish_kernel,
        [*keeps, *arrived, *lasts, tokens, *extras, gain],
        [first_rows(rows, keeps[0])] * 4 + [NEAR] * 6,
        [((2, rows, width), WIDE)],
        [NEAR],
        [],
        3 * 10**9,
        "finish",
        24,
    )[0]


def output(lengths, keeps, arrived, lasts, residuals):
    rows, width = lasts[0].shape
    return call(
        output_kernel,
        [lengths, *keeps, *arrived, *lasts, *residuals],
        [SCALARS] + [first_rows(rows, keeps[0])] * 4 + [NEAR] * 4,
        [((2, rows, width), LOW)],
        [NEAR],
        [],
        3 * 10**9,
        "output",
        24,
    )[0]


def mixer_backward(index, lengths, grads, w_out, w_in, kept, taps, tables):
    rows, width = grads[0].shape
    length = 4 * rows
    mixed, projected, convolved, kernel_spec, series_spec = kept
    return call(
        functools.partial(back_kernel, index),
        [lengths, *grads, w_out, w_in, mixed, projected, convolved, kernel_spec, series_spec, taps, *tables],
        [SCALARS] + [NEAR] * 12 + [ANY] * 2,
        [
            ((length, 3 * LANES), LOW),
            ((length, LANES), WIDE),
            ((12, LANES), WIDE),
            ((width, LANES), WIDE),
            ((2 * rows, width), LOW),
            ((2 * rows, width), WIDE),
        ],
        [NEAR] * 6,
        [
            pltpu.VMEM((2 * length, length), LOW),
            pltpu.VMEM((length, 2 * length), LOW),
            pltpu.VMEM((length, LANES), WIDE),
            pltpu.VMEM((length, LANES), LOW),
            pltpu.VMEM((2 * length, LANES), LOW),
            pltpu.VMEM((2 * length, LANES), LOW),
            pltpu.VMEM((length, LANES), WIDE),
            pltpu.SemaphoreType.DMA((2,)),
        ],
        19 * 10**9,
        "mixer_back",
    )


def tail(packed, channels, buckets, grad_in, out_grads, d_kernels, w_in, gain):
    width = w_in.shape[0]
    length = d_kernels[0].shape[0]
    extra = 2 * channels + 128 if packed else 0
    return call(
        functools.partial(tail_kernel, packed, channels),
        [buckets, grad_in, *out_grads, *d_kernels, w_in, gain],
        [SCALARS] + [NEAR] * 7,
        [
            ((width, 3 * LANES + extra), LOW),
            ((width, 1), WIDE),
            ((length, 2 * channels), WIDE),
        ],
        [NEAR] * 3,
        [],
        4 * 10**9,
        "tail",
    )


def pack_mixer(w_in, long_filter, w_out):
    rows, _, channels = w_in.shape
    gap = LANES - channels
    turned = w_out.T
    pieces = []
    for s in range(3):
        pieces += [w_in[:, s], turned[:, s * gap : (s + 1) * gap]]
    both = jnp.concatenate([long_filter[0], long_filter[1]], axis=1)
    spare = both[rows:].reshape(both.shape[0] - rows, 3, -1)
    pieces += [both[:rows], spare.transpose(1, 0, 2).reshape(rows, -1)]
    return jnp.concatenate(pieces, axis=1)


def unpack_rows(blocks, channels):
    count, rows, _ = blocks.shape
    spare = blocks[:, :, 2 * channels :].reshape(count, 3, rows // 3, -1)
    spare = spare.transpose(0, 2, 1, 3).reshape(count, rows // 3, -1)
    return jnp.concatenate([blocks[:, :, : 2 * channels], spare], axis=1)


def unpack_out(pack, channels):
    gap = LANES - channels
    return jnp.concatenate(
        [pack[:, s * LANES + channels : s * LANES + channels + gap] for s in range(3)], axis=1
    )


def unpack_mixer(pack, rows, channels):
    w_out = jnp.pad(unpack_out(pack, channels), ((0, 0), (0, LANES - channels)))
    blocks = pack[:, 3 * LANES :].reshape(-1, rows, pack.shape[1] - 3 * LANES)
    filters = unpack_rows(blocks, channels).reshape(-1, 2 * channels)
    return pack[:, : 3 * LANES], filters, w_out


def per_device(
    tokens,
    lengths,
    buckets,
    w_in,
    long_filter,
    w_out,
    w_gu,
    w_down,
    norm_gains,
    short_taps,
    cond_taps,
    cotangent,
):
    row_count, part_len, width = tokens.shape
    channels = short_taps.shape[-1]
    hidden = w_down.shape[0]
    shard = w_in.shape[0]
    rows = range(row_count)
    gains = norm_gains.astype(WIDE)
    taps = jnp.concatenate([short_taps.reshape(9, channels), cond_taps], axis=0).astype(WIDE)
    taps = jnp.pad(taps, ((0, 0), (0, LANES - channels)))
    tables = tuple(jnp.asarray(table) for table in wave_tables(4 * part_len))

    all_tokens = spread(tokens)
    (full_in, filters, part_out), packed_last = gather_mixer(
        pack_mixer(w_in, long_filter, w_out), channels
    )
    w_ff = jnp.concatenate([w_gu.reshape(shard, -1), w_down.T], axis=1)
    weights = gather_rows(after(w_ff, packed_last))

    forward = [
        mixer_forward(r, (lengths, buckets), all_tokens, full_in, filters, taps, gains[:1], tables)
        for r in rows
    ]
    first_mixed = forward[0][0]
    second_mixed = forward[1][0]
    all_grads = spread(after(cotangent, all_tokens[1]), second_mixed)
    outs = spread(after(part_out, all_grads[1]), second_mixed)
    inputs = (lengths, all_tokens, all_grads)
    centre = []
    arrived_d = []
    last_d = []
    gate = first_mixed
    for r in rows:
        mixed = spread(forward[r][0], gate if r else None)
        leaving = middle(r, 1, *inputs, mixed, outs, gains[1:], weights, gate)
        arrived_d.append(fold_near(leaving[4]))
        staying = middle(r, 0, *inputs, mixed, outs, gains[1:], weights, leaving[4])
        last_d.append(fold_far(staying[4], arrived_d[r]))
        centre.append((staying, leaving))
        gate = staying[4]

    d_residual = []
    gain_second = 0.0
    d_low = []
    for r in rows:
        staying = centre[r][0]
        d_wide, low, gain_grad = norm_back(
            staying[4], arrived_d[r], last_d[r], staying[6], staying[3], gains[1:]
        )
        d_residual.append(d_wide)
        gain_second = gain_second + gain_grad
        d_low.append(low)

    kept_ff = after([[half[:4] for half in centre[r]] for r in rows], arrived_d)
    grad_gu = sum(dot(half[0], half[1], 0, 0) for kept in kept_ff for half in kept)
    grad_down = sum(dot(half[3], half[2], 0, 0) for kept in kept_ff for half in kept)
    grad_gu, grad_down = after((grad_gu.astype(LOW), grad_down.astype(LOW)), last_d)
    ff_steps = ring_sums(jnp.concatenate([grad_gu, grad_down], axis=1))
    ff_sums = [next(ff_steps)]

    arrived_o = [fold_near(after(centre[r][1][5], d_low)) for r in rows]
    backward = []
    arrived_h = []
    gate = None
    for r in rows:
        kept = (forward[r][0],) + tuple(forward[r][2:])
        spread_d = spread(d_low[r], gate)
        if r:
            ff_sums.append(next(ff_steps))
            spread_d[3] = after(spread_d[3], ff_sums[1])
        else:
            spread_d[3] = after(spread_d[3], d_low[1])
        back = mixer_backward(r, lengths, spread_d, part_out, full_in, kept, taps, tables)
        backward.append(back)
        arrived_h.append(fold_near(back[4]))
        gate = back[4]
    last_o = [
        fold_far(centre[r][0][5], after(arrived_o[r], spread_d[1], backward[0][4])) for r in rows
    ]
    last_h = [fold_far(backward[r][5], arrived_h[r]) for r in rows]

    packed = lax.axis_size("batch") == len(RING)
    ff_sums.append(next(ff_steps))
    d_projected = after([back[0] for back in backward], arrived_h, ff_sums[2])
    grad_in = sum(dot(forward[r][1], d_projected[r], 0, 0) for r in rows)
    grad_mixer, gain_first, grad_filter = tail(
        packed,
        channels,
        buckets,
        grad_in,
        [backward[r][3] for r in rows],
        [backward[r][1] for r in rows],
        full_in,
        gains[0][:, None],
    )
    mixer_steps = ring_sums(grad_mixer)
    mixer_sums = [next(mixer_steps)]
    ff_sums.append(next(ff_steps))
    grad_ff = ff_steps.send(mixer_sums[0])
    mixer_sums.append(next(mixer_steps))
    mixer_sums.append(next(mixer_steps))
    mixer_sums.append(next(mixer_steps))
    grad_mixer = next(mixer_steps)
    outputs = output(
        after(lengths, mixer_sums[1]),
        [centre[r][0][5] for r in rows],
        arrived_o,
        last_o,
        [centre[r][0][6] for r in rows],
    )
    d_inputs = finish(
        [backward[r][5] for r in rows],
        arrived_h,
        last_h,
        tokens,
        d_residual,
        after(gains[:1], mixer_sums[2]),
    )
    if packed:
        grad_filter = unpack_rows(grad_mixer[None, :, 3 * LANES :], channels)[0]
    else:
        grad_filter = list(ring_sums(grad_filter))[-1]
    grad_in = grad_mixer[:, : 3 * LANES].reshape(-1, 3, LANES)[:, :, :channels]
    grad_taps = sum(backward[r][2] for r in rows)[:, :channels]
    smalls = jnp.concatenate(
        [gain_first.reshape(-1), gain_second.reshape(-1), grad_taps.reshape(-1)]
    )
    small_steps = small_sums(after(smalls, mixer_sums[0]).reshape(-1, 128), "batch")
    smalls = next(small_steps)
    for smalls in small_steps:
        pass
    smalls = smalls.reshape(-1)
    small_steps = small_sums(smalls[: 2 * width].reshape(-1, 128), "chan")
    grad_gains = list(small_steps)[-1].reshape(2, width)
    grad_taps = smalls[2 * width :].reshape(12, channels)
    return (
        outputs,
        d_inputs,
        grad_in,
        jnp.stack([grad_filter[:, :channels], grad_filter[:, channels:]]),
        unpack_out(grad_mixer, channels).T,
        grad_ff[:, : 2 * hidden].reshape(-1, 2, hidden),
        grad_ff[:, 2 * hidden :].T,
        grad_gains,
        grad_taps[:9].reshape(3, 3, channels),
        grad_taps[9:],
    )


def solution(mesh):
    placed = (
        P("batch", "chan", None),
        P("batch"),
        P("batch"),
        P("batch", None, "chan"),
        P(None, "batch", "chan"),
        P("chan", "batch"),
        P("batch", None, "chan"),
        P("chan", "batch"),
        P(),
        P(None, None, "chan"),
        P(None, "chan"),
        P("batch", "chan", None),
    )
    return jax.shard_map(
        per_device,
        mesh=mesh,
        in_specs=placed,
        out_specs=(
            P("batch", "chan", None),
            P("batch", "chan", None),
            P("batch", None, "chan"),
            P(None, "batch", "chan"),
            P("chan", "batch"),
            P("batch", None, "chan"),
            P("chan", "batch"),
            P(),
            P(None, None, "chan"),
            P(None, "chan"),
        ),
        check_vma=False,
    )
```

```python
import functools
import math

import jax
import jax.numpy as jnp
import numpy as np
from jax import lax
from jax.experimental import pallas as pl
from jax.experimental.pallas import tpu as pltpu
from jax.sharding import PartitionSpec as P

EPSILON = 1e-05
LOW = jnp.bfloat16
WIDE = jnp.float32
RING = (0, 2, 4, 6, 7, 5, 3, 1)
CODES = (0, 2, 1, 3)
LANES = 256


def dot(left, right, left_dim, right_dim, kind=WIDE):
    return lax.dot_general(
        left, right, (((left_dim,), (right_dim,)), ((), ())), preferred_element_type=kind
    )


TILES = 2


@functools.lru_cache(maxsize=None)
def wave_tables(length):
    half = length // 2
    bins = np.arange(half, dtype=np.int64)[:, None]
    places = np.arange(length, dtype=np.int64)
    places = np.concatenate([places[::2], places[1::2]])[None, :]
    turns = ((2 * bins + 1) * places) % (4 * length)
    angles = turns * (2.0 * math.pi / (4 * length))
    shape = (TILES, half // TILES, length)
    both = np.stack([np.cos(angles).reshape(shape), -np.sin(angles).reshape(shape)], axis=1)
    both = both.reshape(length, length)
    return both.astype(jnp.bfloat16), np.ascontiguousarray(both.T).astype(jnp.bfloat16)


def swap(block, step):
    size = lax.axis_size("chan")
    return lax.ppermute(block, "chan", [(i, i ^ step) for i in range(size)])


def after(values, *earlier):
    return lax.optimization_barrier((values, earlier))[0]


def spread(block, gate=None):
    far = swap(block, 2)
    near = swap(block, 1)
    return [block, far, near, swap(far if gate is None else after(far, gate), 1)]


def fold_near(send):
    return swap(send, 1)


def fold_far(keep, arrived):
    half = keep.shape[0] // 2
    return swap((keep[half:].astype(WIDE) + arrived[half:].astype(WIDE)).astype(LOW), 2)


def ring_steps(block, shift):
    count = len(RING)
    pairs = [(RING[i], RING[(i + shift) % count]) for i in range(count)]
    return lax.ppermute(block, "batch", pairs)


def ring_place():
    index = lax.axis_index("batch")
    return jnp.where(index % 2 == 0, index // 2, len(RING) - 1 - index // 2)


def ring_member(place):
    place = lax.rem(place, len(RING))
    return jnp.where(place < len(RING) // 2, 2 * place, 2 * (len(RING) - 1 - place) + 1)


OFFSETS = (0, 7, 1, 6, 2, 5, 3)


def ring_blocks(block):
    half = block.shape[0] // 2
    blocks = [block]
    up = down = block
    for _ in range(3):
        up, down = ring_steps(up, 1), ring_steps(down, -1)
        blocks += [up, down]
    return blocks + [ring_steps(up[:half], 1), ring_steps(down[half:], -1)]


def place_mixer_kernel(get, outs, leave, joined):
    w_in, filters, w_out = outs
    blocks = [get(i) for i in range(9)]
    rows = blocks[0].shape[0]
    half = rows // 2
    spare = rows // 3
    channels = filters.shape[1] // 2
    gap = LANES - channels
    place = ring_place()
    joined[:half, :] = blocks[7][...]
    joined[half:, :] = blocks[8][...]
    w_out[:, channels:] = jnp.zeros((w_out.shape[0], gap), w_out.dtype)
    for block, offset in zip((*blocks[:7], joined), (*OFFSETS, 4)):
        member = ring_member(place + offset)
        start = pl.multiple_of(member * rows, rows)
        w_in[pl.ds(start, rows), :] = block[:, : 3 * LANES]
        for s in range(3):
            w_out[pl.ds(start, rows), s * gap : (s + 1) * gap] = block[
                :, s * LANES + channels : (s + 1) * LANES
            ]
        start = pl.multiple_of(member * (rows + spare), rows + spare)
        filters[pl.ds(start, rows), :] = block[:, 3 * LANES : 3 * LANES + 2 * channels]
        start = pl.multiple_of(start + rows, spare)
        for j in range(3):
            filters[pl.ds(start, spare), j * 128 : (j + 1) * 128] = block[
                j * spare : (j + 1) * spare, 3 * LANES + 2 * channels :
            ]
    for i in range(3):
        leave(i)


def gather_rows(block):
    if lax.axis_size("batch") != len(RING):
        return [lax.all_gather(block, "batch", axis=0, tiled=True)]
    return ring_blocks(block)


def gather_mixer(block, channels):
    count = lax.axis_size("batch")
    rows, columns = block.shape
    if count != len(RING):
        pack = lax.all_gather(block, "batch", axis=0, tiled=True)
        return unpack_mixer(pack, rows, channels), pack
    blocks = ring_blocks(block)
    whole = call(
        place_mixer_kernel,
        [],
        blocks,
        [
            ((count * rows, 3 * LANES), block.dtype),
            ((count * (rows + rows // 3), 2 * channels), block.dtype),
            ((count * rows, LANES), block.dtype),
        ],
        [pltpu.VMEM((rows, columns), block.dtype)],
        2 * 10**9,
        "place_mixer",
    )
    return whole, blocks[7:]


def ring_sums(partial):
    count = lax.axis_size("batch")
    if count != len(RING):
        total = lax.psum_scatter(partial.astype(LOW), "batch", scatter_dimension=0, tiled=True)
        for _ in range(5):
            gate = yield total
            if gate is not None:
                total = after(total, gate)
        yield total.astype(WIDE)
        return
    place = ring_place()
    rows = partial.shape[0] // count
    half = rows // 2

    def part(offset, first=0, size=rows):
        start = ring_member(place + offset) * rows + first
        return lax.dynamic_slice_in_dim(partial, start, size, 0).astype(WIDE)

    up, down = part(4, 0, half).astype(LOW), part(4, half, half).astype(LOW)
    gate = yield up, down
    if gate is not None:
        up, down = after((up, down), gate)
    up, down = ring_steps(up, 1).astype(WIDE), ring_steps(down, -1).astype(WIDE)
    up = part(3) + jnp.concatenate([up, jnp.zeros_like(up)], axis=0)
    down = part(5) + jnp.concatenate([jnp.zeros_like(down), down], axis=0)
    for step in (2, 1, 0):
        up, down = up.astype(LOW), down.astype(LOW)
        gate = yield up, down
        if gate is not None:
            up, down = after((up, down), gate)
        up, down = ring_steps(up, 1).astype(WIDE), ring_steps(down, -1).astype(WIDE)
        if step:
            up = up + part(step)
            down = down + part(count - step)
    gate = yield up, down
    if gate is not None:
        up, down = after((up, down), gate)
    yield up + down + part(0)


def small_sums(values, axis):
    size = lax.axis_size(axis)
    if size & (size - 1) or size > 8:
        values = lax.psum(values, axis)
        yield values
        yield values
        return
    step = 1
    while step < size:
        gate = yield values
        if gate is not None:
            values = after(values, gate)
        values = values + lax.ppermute(values, axis, [(i, i ^ step) for i in range(size)])
        step *= 2
    yield values


def norm_forward(values):
    centre = jnp.mean(values, axis=-1, keepdims=True)
    scale = lax.rsqrt(jnp.mean(values * values, axis=-1, keepdims=True) - centre * centre + EPSILON)
    return (values - centre) * scale, scale


def block_start(code, rows):
    return pl.multiple_of((lax.axis_index("chan") ^ code) * rows, rows)


def shifted(series, offset, row):
    if offset == 0:
        return series
    length = series.shape[0]
    moved = pltpu.roll(series, offset % length, 0)
    inside = row >= offset if offset > 0 else row < length + offset
    return jnp.where(inside, moved, 0.0)


def tap_sum(series, taps, first, row, direction):
    total = taps[first : first + 1, :] * series
    for j in (1, 2):
        total = total + taps[first + j : first + j + 1, :] * shifted(series, direction * j, row)
    return total


def split_places(value, halves, even, odd):
    half = value.shape[0] // 2
    for i in range(2):
        lanes = slice(i * 128, (i + 1) * 128)
        halves[i] = value[:, lanes]
        even[:, lanes] = halves[i, pl.ds(0, half, stride=2), :].astype(LOW)
        odd[:, lanes] = halves[i, pl.ds(1, half, stride=2), :].astype(LOW)


def mirrored(table, even, odd):
    half = table.shape[1] // 2
    first = dot(table[:, :half], even[...], 1, 0)
    second = dot(table[:, half:], odd[...], 1, 0)
    total, rest = first + second, first - second
    size = table.shape[0] // 2
    return total[:size], total[size:], rest[:size], rest[size:]


def join_places(waves_t, even, odd, halves):
    length = waves_t.shape[0]
    half = length // 2
    for start, source in enumerate((even, odd)):
        part = dot(waves_t[start * half : (start + 1) * half, :], source[...], 1, 0) * (1.0 / length)
        for i in range(2):
            halves[i, pl.ds(start, half, stride=2), :] = part[:, i * 128 : (i + 1) * 128]
    return jnp.concatenate([halves[0], halves[1]], axis=1)


def mixer_kernel(
    index, lengths, buckets, get, outs, leave,
    wide_buf, series_wide, gate_buf, kernel_even, kernel_odd, series_even, series_odd, even_buf, odd_buf,
):
    mixed, h_first, projected, convolved, kernel_spec, series_spec = outs
    gain, w_in = get(1), None
    for i, code in enumerate(CODES):
        block = get((0, 3, 4, 5)[i])
        normed, _ = norm_forward(block[...].astype(WIDE))
        low = (normed * gain[...]).astype(LOW)
        rows = block.shape[0]
        place = pl.ds(block_start(code, rows), rows)
        h_first[place, :] = low
        leave(1, place)
        w_in = get(2)
        projected[place, :] = dot(low, w_in[...], 1, 0).astype(LOW)
        leave(2, place)
    length = projected.shape[0]
    row = lax.broadcasted_iota(jnp.int32, (length, LANES), 0)
    mask = (row < lengths[index]).astype(WIDE)
    filters, taps = get(6), get(7)

    def stream(s):
        raw = projected[:, s * LANES : (s + 1) * LANES].astype(WIDE)
        return mask * tap_sum(raw, taps, 3 * s, row, 1)

    channels = filters.shape[1] // 2
    both = filters[...].astype(WIDE)
    chosen = jnp.where(buckets[index] == 0, both, pltpu.roll(both, channels, 1))[:, :LANES]
    kernel = chosen + tap_sum(stream(1), taps, 9, row, 1)
    split_places(kernel, wide_buf, kernel_even, kernel_odd)
    split_places(stream(2), series_wide, series_even, series_odd)
    gate_buf[...] = stream(0)
    waves = get(8)
    size = length // TILES
    half = size // 2
    for i in range(TILES):
        table = waves[i * size : (i + 1) * size, :]
        k = mirrored(table, kernel_even, kernel_odd)
        s = mirrored(table, series_even, series_odd)
        for j in range(4):
            place = slice((2 * i + j // 2) * size + (j % 2) * half, (2 * i + j // 2) * size + (j % 2 + 1) * half)
            kernel_spec[place, :] = k[j].astype(LOW)
            series_spec[place, :] = s[j].astype(LOW)
        place = slice(2 * i * size, 2 * (i + 1) * size)
        leave(4, place)
        leave(5, place)
        real, imag = k[0] * s[0] - k[1] * s[1], k[0] * s[1] + k[1] * s[0]
        real_rest, imag_rest = k[2] * s[2] - k[3] * s[3], k[2] * s[3] + k[3] * s[2]
        upper, lower = slice(i * size, i * size + half), slice(i * size + half, (i + 1) * size)
        even_buf[upper, :] = (real + real_rest).astype(LOW)
        even_buf[lower, :] = (imag + imag_rest).astype(LOW)
        odd_buf[upper, :] = (real - real_rest).astype(LOW)
        odd_buf[lower, :] = (imag - imag_rest).astype(LOW)
    value = join_places(get(9), even_buf, odd_buf, wide_buf)
    mixed[...] = (value * gate_buf[...]).astype(LOW)
    leave(0)
    convolved[...] = value.astype(LOW)
    leave(3)


def middle_kernel(index, tile, pieces, lengths, get, outs, leave, *scratch):
    h_out, grads_out, hidden_out, d_out_out, d_normed, out_sum = outs[:6]
    outs_first, mixed_first = 5, 9
    rows, width = get(0).shape
    hidden = hidden_out.shape[1]
    gain = get(4)
    for i in range(2):
        start = block_start(CODES[2 * tile + i], rows)
        place = slice(i * rows, (i + 1) * rows)
        value = get(i)[...].astype(WIDE)
        for j in range(4):
            value = value + dot(get(mixed_first + 4 * i + j)[...], get(outs_first + j)[...], 1, 1)
        if tile == 0 and i == 0:
            outs[6][...] = value
            leave(6)
        normed, _ = norm_forward(value)
        h_out[place, :] = (normed * gain[...]).astype(LOW)
        row = start + lax.broadcasted_iota(jnp.int32, (rows, width), 0)
        grads = get(2 + i)[...].astype(WIDE)
        d_out_out[place, :] = jnp.where(row < lengths[index], grads, 0.0).astype(LOW)
    leave(0)
    leave(3)
    if pieces:
        weights = outs[-1]
        for i in range(9):
            get(17 + i)
        leave(len(outs) - 1)
    else:
        weights = get(17)
    for first in range(0, hidden, 256):
        gate_place = slice(first, first + 256)
        up_place = slice(hidden + first, hidden + first + 256)
        down_place = slice(2 * hidden + first, 2 * hidden + first + 256)
        gate = dot(h_out[...], weights[:, gate_place], 1, 0)
        up = dot(h_out[...], weights[:, up_place], 1, 0)
        d_hidden = dot(d_out_out[...], weights[:, down_place], 1, 0)
        slope = math.sqrt(2.0 / math.pi)
        square = gate * gate
        bent = jnp.tanh(slope * gate * (1.0 + 0.044715 * square))
        rise = 0.5 * (1.0 + bent)
        active = gate * rise
        hidden_out[:, gate_place] = (active * up).astype(LOW)
        d_active = rise + 0.5 * gate * (1.0 - bent * bent) * (slope * (1.0 + 0.134145 * square))
        grads_out[:, gate_place] = (d_hidden * up * d_active).astype(LOW)
        grads_out[:, up_place] = (d_hidden * active).astype(LOW)
    leave(1)
    leave(2)
    d_normed[...] = dot(grads_out[...], weights[:, : 2 * hidden], 1, 1).astype(d_normed.dtype)
    leave(4)
    out_sum[...] = dot(hidden_out[...], weights[:, 2 * hidden :], 1, 1).astype(out_sum.dtype)
    leave(5)


def norm_step(d_out, values, extra, gain):
    normed, scale = norm_forward(values)
    scaled = d_out * gain
    first_mean = jnp.mean(scaled, axis=-1, keepdims=True)
    second_mean = jnp.mean(scaled * normed, axis=-1, keepdims=True)
    return extra + scale * (scaled - first_mean - normed * second_mean), normed


def norm_kernel(get, outs, leave):
    keep, arrived, last, values, extra, gain = (get(i) for i in range(6))
    d_wide, d_low, gain_grad = outs
    d_out = keep[...].astype(WIDE) + arrived[...].astype(WIDE) + last[...].astype(WIDE)
    total, normed = norm_step(d_out, values[...], extra[...].astype(WIDE), gain[...])
    d_low[...] = total.astype(LOW)
    leave(1)
    d_wide[...] = total
    leave(0)
    gain_grad[...] = jnp.sum(d_out * normed, axis=0, keepdims=True)
    leave(2)


def finish_kernel(get, outs, leave):
    gain = get(0)
    for r in range(2):
        keep, arrived, last, tokens, extra = (get(1 + 5 * r + i) for i in range(5))
        d_out = keep[...].astype(WIDE) + arrived[...].astype(WIDE) + last[...].astype(WIDE)
        outs[0][r], _ = norm_step(d_out, tokens[...].astype(WIDE), extra[...], gain[...])
        leave(0, r)


def output_kernel(lengths, get, outs, leave):
    for r in range(2):
        keep, arrived, last, residual = (get(4 * r + i) for i in range(4))
        value = residual[...] + keep[...].astype(WIDE) + arrived[...].astype(WIDE) + last[...].astype(WIDE)
        row = block_start(0, value.shape[0]) + lax.broadcasted_iota(jnp.int32, value.shape, 0)
        outs[0][r] = jnp.where(row < lengths[r], value, 0.0).astype(LOW)
        leave(0, r)


def back_kernel(
    index, lengths, get, outs, leave,
    mix_buf, conv_buf, series_halves, kernel_halves, conv_even, conv_odd, kernel_even, kernel_odd, series_even, series_odd,
):
    d_projected, kernel_out, tap_grads, out_grad, send, keep, gain_grad = outs
    w_out = get(0)
    for i, code in enumerate(CODES):
        block = get(1 + i)
        rows = block.shape[0]
        mix_buf[pl.ds(block_start(code, rows), rows), :] = dot(block[...], w_out[...], 1, 0)
    projected, taps = get(5), get(6)
    length = projected.shape[0]
    row = lax.broadcasted_iota(jnp.int32, (length, LANES), 0)
    mask = (row < lengths[index]).astype(WIDE)

    def raw(s):
        return projected[:, s * LANES : (s + 1) * LANES].astype(WIDE)

    d_conv = mix_buf[...] * mask * tap_sum(raw(0), taps, 0, row, 1)
    split_places(d_conv, conv_buf, conv_even, conv_odd)
    waves, series_spec, kernel_spec = get(7), get(8), get(9)
    size = length // TILES
    half = size // 2
    for i in range(TILES):
        g = mirrored(waves[i * size : (i + 1) * size, :], conv_even, conv_odd)
        upper, lower = slice(i * size, i * size + half), slice(i * size + half, (i + 1) * size)
        for spec, even, odd in (
            (series_spec, kernel_even, kernel_odd),
            (kernel_spec, series_even, series_odd),
        ):
            start = 2 * i * size
            a = [spec[start + j * half : start + (j + 1) * half, :].astype(WIDE) for j in range(4)]
            real, imag = g[0] * a[0] + g[1] * a[1], g[1] * a[0] - g[0] * a[1]
            real_rest, imag_rest = g[2] * a[2] + g[3] * a[3], g[3] * a[2] - g[2] * a[3]
            even[upper, :] = (real + real_rest).astype(LOW)
            even[lower, :] = (imag + imag_rest).astype(LOW)
            odd[upper, :] = (real - real_rest).astype(LOW)
            odd[lower, :] = (imag - imag_rest).astype(LOW)
    waves_t = get(10)
    d_kernel = join_places(waves_t, kernel_even, kernel_odd, kernel_halves)
    kernel_out[...] = d_kernel.astype(LOW)
    leave(1)
    d_series = join_places(waves_t, series_even, series_odd, series_halves)

    def finish(s, grads):
        series = raw(s)
        for j in range(3):
            tap_grads[3 * s + j : 3 * s + j + 1, :] = jnp.sum(
                grads * shifted(series, j, row), axis=0, keepdims=True
            )
        d_projected[:, s * LANES : (s + 1) * LANES] = tap_sum(grads, taps, 3 * s, row, -1).astype(LOW)

    finish(2, d_series * mask)
    grads = d_kernel
    condition = mask * tap_sum(raw(1), taps, 3, row, 1)
    for j in range(3):
        tap_grads[9 + j : 10 + j, :] = jnp.sum(
            grads * shifted(condition, j, row), axis=0, keepdims=True
        )
    finish(1, mask * tap_sum(grads, taps, 9, row, -1))
    convolved = get(11)
    finish(0, mix_buf[...] * convolved[...].astype(WIDE) * mask)
    leave(0)
    leave(2)
    w_in, h_first = get(12), get(14)
    gain_sum = 0.0
    for i in (2, 3, 0, 1):
        place = pl.ds(block_start(CODES[i], rows), rows)
        part = dot(d_projected[place, :], w_in[...], 1, 1)
        gain_sum = gain_sum + jnp.sum(part * h_first[place, :].astype(WIDE), axis=0, keepdims=True)
        if i < 2:
            keep[i * rows : (i + 1) * rows, :] = part.astype(LOW)
        else:
            send[(i - 2) * rows : (i - 1) * rows, :] = part.astype(LOW)
        if i == 3:
            leave(4)
    leave(5)
    gain_grad[...] = gain_sum
    leave(6)
    mixed = get(13)
    total = None
    for i, code in enumerate(CODES):
        place = pl.ds(block_start(code, rows), rows)
        part = dot(get(1 + i)[...], mixed[place, :], 0, 0)
        total = part if total is None else total + part
    out_grad[...] = total.astype(LOW)
    leave(3)


def tail_kernel(packed, channels, buckets, get, outs, leave):
    grad_in, g0, g1, k0, k1 = (get(i) for i in range(5))
    grads, filters = outs
    gap = LANES - channels
    width = grad_in.shape[0]
    out_grad = g0[...].astype(WIDE) + g1[...].astype(WIDE)
    lane = lax.broadcasted_iota(jnp.int32, (width, LANES), 1)
    for s in range(3):
        place = slice(s * LANES, (s + 1) * LANES)
        grad = grad_in[:, place].astype(WIDE)
        behind = pltpu.roll(out_grad, channels - s * gap, 1)
        grads[:, place] = jnp.where(lane < channels, grad, behind).astype(LOW)
    first = [jnp.where(buckets[r] == 0, 1.0, 0.0) for r in range(2)]
    parts = [k0[...].astype(WIDE), k1[...].astype(WIDE)]
    zeros = jnp.zeros((k0.shape[0], 2 * channels - LANES), WIDE)
    sums = [
        jnp.concatenate([parts[0] * a + parts[1] * b, zeros], axis=1)
        for a, b in (first, [1.0 - first[0], 1.0 - first[1]])
    ]
    filters[...] = (sums[0] + pltpu.roll(sums[1], channels, 1)).astype(filters.dtype)
    if packed:
        rows = width // len(RING)
        spare = rows // 3
        for i in range(len(RING)):
            start = i * (rows + spare)
            place = slice(i * rows, (i + 1) * rows)
            grads[place, 3 * LANES : 3 * LANES + 2 * channels] = filters[start : start + rows, :].astype(LOW)
            for j in range(3):
                place = slice(i * rows + j * spare, i * rows + (j + 1) * spare)
                grads[place, 3 * LANES + 2 * channels :] = filters[
                    start + rows : start + rows + spare, j * 128 : (j + 1) * 128
                ].astype(LOW)
    else:
        leave(1)
    leave(0)


ANY = pl.BlockSpec(memory_space=pl.ANY)
SCALARS = pl.BlockSpec(memory_space=pltpu.SMEM)


def call(kernel, scalars, operands, results, scratch, flops, name, limit=60, pieces=()):
    operands = [x if isinstance(x, tuple) else (x, None, x.shape) for x in operands]
    count, first_piece = len(operands), len(operands)
    blocks = [block for block, _ in pieces]
    buffers = [pltpu.VMEM(shape, x.dtype) for x, _, shape in operands]
    finals = [pltpu.VMEM(shape, kind) for shape, kind in results]
    taken = len(scalars) + count + len(blocks)
    spare = 4 * len(results) + 8

    def body(*refs):
        outside, ours = refs[: taken + len(results)], refs[taken + len(results) :]
        left, ours = outside[taken:], ours
        inside, outs = ours[:count], ours[count : count + len(finals)]
        extra, sems = ours[count + len(finals) : -1], ours[-1]
        copies = []
        for i, (_, view, _) in enumerate(operands):
            source = outside[len(scalars) + i]
            source = source if view is None else view(source)
            copies.append(pltpu.make_async_copy(source, inside[i], sems.at[i]))
        for i, (block, start) in enumerate(pieces):
            size = block.shape[0]
            place = pl.ds(pl.multiple_of(start(), 16), size)
            copies.append(
                pltpu.make_async_copy(
                    outside[len(scalars) + count + i], outs[-1].at[place, :], sems.at[count + i]
                )
            )
        for copy in copies:
            copy.start()
        waited = set()
        leaving = []

        def get(i):
            if i not in waited:
                copies[i].wait()
                waited.add(i)
            return inside[i] if i < first_piece else None

        def leave(i, place=None):
            source, target = outs[i], left[i]
            if isinstance(place, int):
                source, target = source.at[place], target.at[place]
            elif place is not None:
                source, target = source.at[place, :], target.at[place, :]
            sem = sems.at[len(copies) + len(leaving)]
            leaving.append(pltpu.make_async_copy(source, target, sem))
            leaving[-1].start()

        kernel(*outside[: len(scalars)], get, outs, leave, *extra)
        for i in range(len(copies)):
            get(i)
        for copy in leaving:
            copy.wait()

    moved = sum(math.prod(shape) * x.dtype.itemsize for x, _, shape in operands)
    moved += sum(math.prod(shape) * jnp.dtype(kind).itemsize for shape, kind in results)
    return pl.pallas_call(
        body,
        in_specs=[SCALARS] * len(scalars) + [ANY] * (count + len(blocks)),
        out_specs=[ANY] * len(results),
        out_shape=[jax.ShapeDtypeStruct(shape, kind) for shape, kind in results],
        scratch_shapes=[
            *buffers,
            *finals,
            *scratch,
            pltpu.SemaphoreType.DMA((count + len(blocks) + spare,)),
        ],
        compiler_params=pltpu.CompilerParams(vmem_limit_bytes=limit * 2**20),
        cost_estimate=pl.CostEstimate(flops=flops, bytes_accessed=moved, transcendentals=0),
        name=name,
    )(*scalars, *[x for x, _, _ in operands], *blocks)


def of_row(index, array):
    return array, lambda ref: ref.at[index], array.shape[1:]


def first_rows(rows, array):
    return array, lambda ref: ref.at[pl.ds(0, rows), :], (rows,) + array.shape[1:]


def block_rows(code, rows, array):
    view = lambda ref: ref.at[pl.ds(block_start(code, rows), rows), :]
    return array, view, (rows,) + array.shape[1:]


def mixer_forward(index, scalars, tokens, w_in, filters, taps, gain, tables):
    _, rows, width = tokens[0].shape
    length = 4 * rows
    spec = ((2 * length, LANES), LOW)
    blocks = [of_row(index, block) for block in tokens]
    return call(
        functools.partial(mixer_kernel, index),
        scalars,
        [blocks[0], gain, w_in, *blocks[1:], filters, taps, *tables],
        [
            ((length, LANES), LOW),
            ((length, width), LOW),
            ((length, 3 * LANES), LOW),
            ((length, LANES), LOW),
            spec,
            spec,
        ],
        [pltpu.VMEM((2, length, 128), WIDE)] * 2
        + [pltpu.VMEM((length, LANES), WIDE)]
        + [pltpu.VMEM((length // 2, LANES), LOW)] * 4
        + [pltpu.VMEM((length, LANES), LOW)] * 2,
        10**10,
        "mixer",
    )


def middle(index, tile, lengths, tokens, grads, mixed, outs, gain, weights, gate):
    _, rows, width = tokens[0].shape
    length = 2 * rows
    hidden = weights[0].shape[1] // 3
    results = [
        ((length, width), LOW),
        ((length, 2 * hidden), LOW),
        ((length, hidden), LOW),
        ((length, width), LOW),
        ((length, width), LOW),
        ((length, width), LOW),
    ]
    if tile == 0:
        results.append(((rows, width), WIDE))
    half = slice(2 * tile, 2 * tile + 2)
    codes = CODES[half]
    pieces = []
    if len(weights) > 1:
        size = weights[0].shape[0]

        def start(offset, first=0):
            return lambda: ring_member(ring_place() + offset) * size + first

        offsets = [(offset, 0) for offset in OFFSETS] + [(4, 0), (4, size // 2)]
        pieces = [(block, start(*where)) for block, where in zip(weights, offsets)]
        results.append(((width, 3 * hidden), LOW))
    return call(
        functools.partial(middle_kernel, index, tile, bool(pieces)),
        [lengths],
        [
            *[of_row(index, block) for block in tokens[half]],
            *[of_row(index, block) for block in grads[half]],
            after(gain, gate),
            *outs,
            *[block_rows(code, rows, part) for code in codes for part in mixed],
            *([] if pieces else weights),
        ],
        results,
        [],
        9 * 10**9,
        "middle",
        60,
        pieces,
    )


def norm_back(keep, arrived, last, values, extra, gain):
    rows, width = last.shape
    return call(
        norm_kernel,
        [],
        [first_rows(rows, keep), first_rows(rows, arrived), last, values, first_rows(rows, extra), gain],
        [((rows, width), WIDE), ((rows, width), LOW), ((1, width), WIDE)],
        [],
        2 * 10**9,
        "norm_back",
        24,
    )


def finish(keeps, arrived, lasts, tokens, extras, gain):
    rows, width = lasts[0].shape
    operands = [gain]
    for r in range(2):
        operands += [first_rows(rows, keeps[r]), first_rows(rows, arrived[r]), lasts[r]]
        operands += [of_row(r, tokens), extras[r]]
    return call(finish_kernel, [], operands, [((2, rows, width), WIDE)], [], 3 * 10**9, "finish", 24)[0]


def output(lengths, keeps, arrived, lasts, residuals):
    rows, width = lasts[0].shape
    operands = []
    for r in range(2):
        operands += [first_rows(rows, keeps[r]), first_rows(rows, arrived[r]), lasts[r], residuals[r]]
    return call(
        output_kernel, [lengths], operands, [((2, rows, width), LOW)], [], 3 * 10**9, "output", 24
    )[0]


def mixer_backward(index, lengths, grads, w_out, w_in, kept, taps, tables):
    rows, width = grads[0].shape
    length = 4 * rows
    mixed, h_first, projected, convolved, kernel_spec, series_spec = kept
    return call(
        functools.partial(back_kernel, index),
        [lengths],
        [
            w_out,
            *grads,
            projected,
            taps,
            tables[0],
            series_spec,
            kernel_spec,
            tables[1],
            convolved,
            w_in,
            mixed,
            h_first,
        ],
        [
            ((length, 3 * LANES), LOW),
            ((length, LANES), LOW),
            ((12, LANES), WIDE),
            ((width, LANES), LOW),
            ((2 * rows, width), LOW),
            ((2 * rows, width), LOW),
            ((1, width), WIDE),
        ],
        [pltpu.VMEM((length, LANES), WIDE)]
        + [pltpu.VMEM((2, length, 128), WIDE)] * 3
        + [pltpu.VMEM((length // 2, LANES), LOW)] * 2
        + [pltpu.VMEM((length, LANES), LOW)] * 4,
        14 * 10**9,
        "mixer_back",
    )


def tail(packed, channels, buckets, grad_in, out_grads, d_kernels):
    width = grad_in.shape[0]
    length = d_kernels[0].shape[0]
    extra = 2 * channels + 128 if packed else 0
    return call(
        functools.partial(tail_kernel, packed, channels),
        [buckets],
        [grad_in, *out_grads, *d_kernels],
        [
            ((width, 3 * LANES + extra), LOW),
            ((length, 2 * channels), WIDE),
        ],
        [],
        4 * 10**9,
        "tail",
    )


def pack_mixer(w_in, long_filter, w_out):
    rows, _, channels = w_in.shape
    gap = LANES - channels
    turned = w_out.T
    pieces = []
    for s in range(3):
        pieces += [w_in[:, s], turned[:, s * gap : (s + 1) * gap]]
    both = jnp.concatenate([long_filter[0], long_filter[1]], axis=1)
    spare = both[rows:].reshape(both.shape[0] - rows, 3, -1)
    pieces += [both[:rows], spare.transpose(1, 0, 2).reshape(rows, -1)]
    return jnp.concatenate(pieces, axis=1)


def unpack_rows(blocks, channels):
    count, rows, _ = blocks.shape
    spare = blocks[:, :, 2 * channels :].reshape(count, 3, rows // 3, -1)
    spare = spare.transpose(0, 2, 1, 3).reshape(count, rows // 3, -1)
    return jnp.concatenate([blocks[:, :, : 2 * channels], spare], axis=1)


def unpack_out(pack, channels):
    gap = LANES - channels
    return jnp.concatenate(
        [pack[:, s * LANES + channels : s * LANES + channels + gap] for s in range(3)], axis=1
    )


def unpack_mixer(pack, rows, channels):
    w_out = jnp.pad(unpack_out(pack, channels), ((0, 0), (0, LANES - channels)))
    blocks = pack[:, 3 * LANES :].reshape(-1, rows, pack.shape[1] - 3 * LANES)
    filters = unpack_rows(blocks, channels).reshape(-1, 2 * channels)
    return pack[:, : 3 * LANES], filters, w_out


def per_device(
    tokens,
    lengths,
    buckets,
    w_in,
    long_filter,
    w_out,
    w_gu,
    w_down,
    norm_gains,
    short_taps,
    cond_taps,
    cotangent,
):
    row_count, part_len, width = tokens.shape
    channels = short_taps.shape[-1]
    hidden = w_down.shape[0]
    shard = w_in.shape[0]
    rows = range(row_count)
    gains = norm_gains.astype(WIDE)
    taps = jnp.concatenate([short_taps.reshape(9, channels), cond_taps], axis=0).astype(WIDE)
    taps = jnp.pad(taps, ((0, 0), (0, LANES - channels)))
    tables = tuple(jnp.asarray(table) for table in wave_tables(4 * part_len))

    all_tokens = spread(tokens)
    (full_in, filters, part_out), packed_last = gather_mixer(
        pack_mixer(w_in, long_filter, w_out), channels
    )
    w_ff = jnp.concatenate([w_gu.reshape(shard, -1), w_down.T], axis=1)
    weights = gather_rows(after(w_ff, packed_last))

    forward = [
        mixer_forward(r, (lengths, buckets), all_tokens, full_in, filters, taps, gains[:1], tables)
        for r in rows
    ]
    first_mixed = forward[0][0]
    second_mixed = forward[1][0]
    all_grads = spread(after(cotangent, all_tokens[1]), second_mixed)
    outs = spread(after(part_out, all_grads[1]), second_mixed)
    inputs = (lengths, all_tokens, all_grads)
    centre = []
    arrived_d = []
    last_d = []
    gate = first_mixed
    for r in rows:
        mixed = spread(forward[r][0], gate if r else None)
        leaving = middle(r, 1, *inputs, mixed, outs, gains[1:], weights, gate)
        if len(weights) > 1:
            weights = [leaving[-1]]
        arrived_d.append(fold_near(leaving[4]))
        staying = middle(r, 0, *inputs, mixed, outs, gains[1:], weights, leaving[4])
        last_d.append(fold_far(staying[4], arrived_d[r]))
        centre.append((staying, leaving))
        gate = staying[4]

    d_residual = []
    gain_second = 0.0
    d_low = []
    for r in rows:
        staying = centre[r][0]
        d_wide, low, gain_grad = norm_back(
            staying[4], arrived_d[r], last_d[r], staying[6], staying[3], gains[1:]
        )
        d_residual.append(d_wide)
        gain_second = gain_second + gain_grad
        d_low.append(low)

    kept_ff = after([[half[:4] for half in centre[r]] for r in rows], arrived_d)
    grad_gu = sum(dot(half[0], half[1], 0, 0) for kept in kept_ff for half in kept)
    grad_down = sum(dot(half[3], half[2], 0, 0) for kept in kept_ff for half in kept)
    grad_gu, grad_down = after((grad_gu.astype(LOW), grad_down.astype(LOW)), last_d)
    ff_steps = ring_sums(jnp.concatenate([grad_gu, grad_down], axis=1))
    ff_sums = [next(ff_steps)]

    arrived_o = [fold_near(after(centre[r][1][5], d_low)) for r in rows]
    backward = []
    arrived_h = []
    gate = None
    for r in rows:
        spread_d = spread(d_low[r], gate)
        if r == 0:
            spread_d[3] = after(spread_d[3], d_low[1])
            beside = ()
        else:
            last_o = [fold_far(centre[i][0][5], after(arrived_o[i], spread_d[1])) for i in rows]
            spread_d[3] = after(spread_d[3], ff_sums[1])
            beside = last_o
        back = mixer_backward(r, lengths, spread_d, part_out, full_in, forward[r], taps, tables)
        ff_sums.append(next(ff_steps))
        back = after(back, ff_sums[-1], beside)
        backward.append(back)
        arrived_h.append(fold_near(back[4]))
        gate = back[4]
    last_h = [fold_far(backward[r][5], arrived_h[r]) for r in rows]

    packed = lax.axis_size("batch") == len(RING)
    ff_sums.append(next(ff_steps))
    ff_sums.append(next(ff_steps))
    grad_taps = sum(backward[r][2] for r in rows)[:, :channels]
    gain_first = sum(backward[r][6] for r in rows) / gains[:1]
    smalls = jnp.concatenate(
        [gain_first.reshape(-1), gain_second.reshape(-1), grad_taps.reshape(-1)]
    )
    small_steps = small_sums(smalls.reshape(-1, 128), "batch")
    smalls = [next(small_steps), next(small_steps)]
    grad_in = sum(dot(forward[r][1], backward[r][0], 0, 0) for r in rows)
    grad_in = after(grad_in.astype(LOW), smalls[1], arrived_h)
    grad_mixer, grad_filter = tail(
        packed,
        channels,
        buckets,
        grad_in,
        [backward[r][3] for r in rows],
        [backward[r][1] for r in rows],
    )
    smalls += list(small_steps)
    grad_mixer, grad_filter = after((grad_mixer, grad_filter), smalls[min(2, len(smalls) - 1)], last_h)
    mixer_steps = ring_sums(grad_mixer)
    mixer_sums = [next(mixer_steps)]
    mixer_sums.append(next(mixer_steps))
    outputs = output(
        after(lengths, mixer_sums[0]),
        [centre[r][0][5] for r in rows],
        arrived_o,
        last_o,
        [centre[r][0][6] for r in rows],
    )
    mixer_sums[1], outputs = after((mixer_sums[1], outputs), ff_sums[4])
    mixer_sums.append(mixer_steps.send(outputs))
    grad_ff = ff_steps.send(mixer_sums[1])
    d_inputs = finish(
        [backward[r][5] for r in rows],
        arrived_h,
        last_h,
        tokens,
        d_residual,
        after(gains[:1], mixer_sums[1]),
    )
    mixer_sums.append(mixer_steps.send(d_inputs))
    next(mixer_steps)
    grad_mixer = next(mixer_steps)
    if packed:
        grad_filter = unpack_rows(grad_mixer[None, :, 3 * LANES :], channels)[0]
    else:
        grad_filter = list(ring_sums(grad_filter))[-1]
    grad_in = grad_mixer[:, : 3 * LANES].reshape(-1, 3, LANES)[:, :, :channels]
    smalls = smalls[-1].reshape(-1)
    small_steps = small_sums(smalls[: 2 * width].reshape(-1, 128), "chan")
    grad_gains = list(small_steps)[-1].reshape(2, width)
    grad_taps = smalls[2 * width :].reshape(12, channels)
    return (
        outputs,
        d_inputs,
        grad_in,
        jnp.stack([grad_filter[:, :channels], grad_filter[:, channels:]]),
        unpack_out(grad_mixer, channels).T,
        grad_ff[:, : 2 * hidden].reshape(-1, 2, hidden),
        grad_ff[:, 2 * hidden :].T,
        grad_gains,
        grad_taps[:9].reshape(3, 3, channels),
        grad_taps[9:],
    )


def solution(mesh):
    placed = (
        P("batch", "chan", None),
        P("batch"),
        P("batch"),
        P("batch", None, "chan"),
        P(None, "batch", "chan"),
        P("chan", "batch"),
        P("batch", None, "chan"),
        P("chan", "batch"),
        P(),
        P(None, None, "chan"),
        P(None, "chan"),
        P("batch", "chan", None),
    )
    return jax.shard_map(
        per_device,
        mesh=mesh,
        in_specs=placed,
        out_specs=(
            P("batch", "chan", None),
            P("batch", "chan", None),
            P("batch", None, "chan"),
            P(None, "batch", "chan"),
            P("chan", "batch"),
            P("batch", None, "chan"),
            P("chan", "batch"),
            P(),
            P(None, None, "chan"),
            P(None, "chan"),
        ),
        check_vma=False,
    )
```

```python
import functools
import math

import jax
import jax.numpy as jnp
import numpy as np
from jax import lax
from jax.experimental import pallas as pl
from jax.experimental.pallas import tpu as pltpu
from jax.sharding import PartitionSpec as P

EPSILON = 1e-05
LOW = jnp.bfloat16
WIDE = jnp.float32
RING = (0, 2, 4, 6, 7, 5, 3, 1)
CODES = (0, 2, 1, 3)
LANES = 256


def dot(left, right, left_dim, right_dim, kind=WIDE):
    return lax.dot_general(
        left, right, (((left_dim,), (right_dim,)), ((), ())), preferred_element_type=kind
    )


TILES = 2


@functools.lru_cache(maxsize=None)
def wave_tables(length):
    half = length // 2
    bins = np.arange(half, dtype=np.int64)[:, None]
    places = np.arange(length, dtype=np.int64)
    places = np.concatenate([places[::2], places[1::2]])[None, :]
    turns = ((2 * bins + 1) * places) % (4 * length)
    angles = turns * (2.0 * math.pi / (4 * length))
    shape = (TILES, half // TILES, length)
    both = np.stack([np.cos(angles).reshape(shape), -np.sin(angles).reshape(shape)], axis=1)
    both = both.reshape(length, length)
    return both.astype(jnp.bfloat16), np.ascontiguousarray(both.T).astype(jnp.bfloat16)


def swap(block, step):
    size = lax.axis_size("chan")
    return lax.ppermute(block, "chan", [(i, i ^ step) for i in range(size)])


def after(values, *earlier):
    return lax.optimization_barrier((values, earlier))[0]


def spread(block, gate=None, near_gate=None):
    far = swap(block, 2)
    near = swap(block if near_gate is None else after(block, near_gate), 1)
    return [block, far, near, swap(far if gate is None else after(far, gate), 1)]


def fold_near(send):
    return swap(send, 1)


def fold_away(keep, arrived):
    half = keep.shape[0] // 2
    return (keep[half:].astype(WIDE) + arrived[half:].astype(WIDE)).astype(LOW)


def fold_far(keep, arrived):
    return swap(fold_away(keep, arrived), 2)


def ring_steps(block, shift):
    count = len(RING)
    pairs = [(RING[i], RING[(i + shift) % count]) for i in range(count)]
    return lax.ppermute(block, "batch", pairs)


def ring_place():
    index = lax.axis_index("batch")
    return jnp.where(index % 2 == 0, index // 2, len(RING) - 1 - index // 2)


def ring_member(place):
    place = lax.rem(place, len(RING))
    return jnp.where(place < len(RING) // 2, 2 * place, 2 * (len(RING) - 1 - place) + 1)


OFFSETS = (0, 7, 1, 6, 2, 5, 3)


def ring_blocks(block):
    if lax.axis_size("batch") != len(RING):
        whole = [lax.all_gather(block, "batch", axis=0, tiled=True)]
        for _ in range(5):
            yield whole
        return
    half = block.shape[0] // 2
    blocks = [block]
    up = down = block
    for step in range(4):
        gate = yield blocks
        if gate is not None:
            up, down = after((up, down), gate)
        if step == 3:
            up, down = up[:half], down[half:]
        up, down = ring_steps(up, 1), ring_steps(down, -1)
        blocks = [*blocks, up, down]
    yield blocks


def place_mixer_kernel(get, outs, leave, joined):
    w_in, filters, w_out = outs
    blocks = [get(i) for i in range(9)]
    rows = blocks[0].shape[0]
    half = rows // 2
    spare = rows // 3
    channels = filters.shape[1] // 2
    gap = LANES - channels
    place = ring_place()
    joined[:half, :] = blocks[7][...]
    joined[half:, :] = blocks[8][...]
    w_out[:, channels:] = jnp.zeros((w_out.shape[0], gap), w_out.dtype)
    for block, offset in zip((*blocks[:7], joined), (*OFFSETS, 4)):
        member = ring_member(place + offset)
        start = pl.multiple_of(member * rows, rows)
        w_in[pl.ds(start, rows), :] = block[:, : 3 * LANES]
        for s in range(3):
            w_out[pl.ds(start, rows), s * gap : (s + 1) * gap] = block[
                :, s * LANES + channels : (s + 1) * LANES
            ]
        start = pl.multiple_of(member * (rows + spare), rows + spare)
        filters[pl.ds(start, rows), :] = block[:, 3 * LANES : 3 * LANES + 2 * channels]
        start = pl.multiple_of(start + rows, spare)
        for j in range(3):
            filters[pl.ds(start, spare), j * 128 : (j + 1) * 128] = block[
                j * spare : (j + 1) * spare, 3 * LANES + 2 * channels :
            ]
    for i in range(3):
        leave(i)


def gather_mixer(block, channels):
    count = lax.axis_size("batch")
    rows, columns = block.shape
    if count != len(RING):
        pack = lax.all_gather(block, "batch", axis=0, tiled=True)
        return unpack_mixer(pack, rows, channels), [pack]
    blocks = list(ring_blocks(block))[-1]
    whole = call(
        place_mixer_kernel,
        [],
        blocks,
        [
            ((count * rows, 3 * LANES), block.dtype),
            ((count * (rows + rows // 3), 2 * channels), block.dtype),
            ((count * rows, LANES), block.dtype),
        ],
        [pltpu.VMEM((rows, columns), block.dtype)],
        2 * 10**9,
        "place_mixer",
    )
    return whole, blocks[7:]


def ring_sums(partial):
    count = lax.axis_size("batch")
    if count != len(RING):
        total = lax.psum_scatter(partial.astype(LOW), "batch", scatter_dimension=0, tiled=True)
        for _ in range(5):
            gate, _ = (yield total) or (None, None)
            if gate is not None:
                total = after(total, gate)
        yield total.astype(WIDE)
        return
    place = ring_place()
    rows = partial.shape[0] // count
    half = rows // 2

    def part(offset, first=0, size=rows):
        start = ring_member(place + offset) * rows + first
        return lax.dynamic_slice_in_dim(partial, start, size, 0).astype(WIDE)

    up, down = part(4, 0, half).astype(LOW), part(4, half, half).astype(LOW)
    gate, _ = (yield up, down) or (None, None)
    if gate is not None:
        up, down = after((up, down), gate)
    up, down = ring_steps(up, 1).astype(WIDE), ring_steps(down, -1).astype(WIDE)
    up = part(3) + jnp.concatenate([up, jnp.zeros_like(up)], axis=0)
    down = part(5) + jnp.concatenate([jnp.zeros_like(down), down], axis=0)
    for step in (2, 1, 0):
        up, down = up.astype(LOW), down.astype(LOW)
        gate, behind = (yield up, down) or (None, None)
        if gate is not None:
            up, down = after((up, down), gate)
        up, down = ring_steps(up, 1), ring_steps(down, -1)
        if behind is not None:
            up, down = after((up, down), behind)
        if step:
            up = up.astype(WIDE) + part(step)
            down = down.astype(WIDE) + part(count - step)
    gate, _ = (yield up, down) or (None, None)
    if gate is not None:
        up, down = after((up, down), gate)
    yield up.astype(WIDE) + down.astype(WIDE) + part(0)


def small_sums(values, axis):
    size = lax.axis_size(axis)
    if size & (size - 1) or size > 8:
        values = lax.psum(values, axis)
        yield values
        yield values
        return
    step = 1
    while step < size:
        gate = yield values
        if gate is not None:
            values = after(values, gate)
        values = values + lax.ppermute(values, axis, [(i, i ^ step) for i in range(size)])
        step *= 2
    yield values


def norm_forward(values):
    centre = jnp.mean(values, axis=-1, keepdims=True)
    scale = lax.rsqrt(jnp.mean(values * values, axis=-1, keepdims=True) - centre * centre + EPSILON)
    return (values - centre) * scale, scale


def block_start(code, rows):
    return pl.multiple_of((lax.axis_index("chan") ^ code) * rows, rows)


def shifted(series, offset, row):
    if offset == 0:
        return series
    length = series.shape[0]
    moved = pltpu.roll(series, offset % length, 0)
    inside = row >= offset if offset > 0 else row < length + offset
    return jnp.where(inside, moved, 0.0)


def tap_sum(series, taps, first, row, direction):
    total = taps[first : first + 1, :] * series
    for j in (1, 2):
        total = total + taps[first + j : first + j + 1, :] * shifted(series, direction * j, row)
    return total


def split_places(value, halves, even, odd):
    half = value.shape[0] // 2
    for i in range(2):
        lanes = slice(i * 128, (i + 1) * 128)
        halves[i] = value[:, lanes]
        even[:, lanes] = halves[i, pl.ds(0, half, stride=2), :].astype(LOW)
        odd[:, lanes] = halves[i, pl.ds(1, half, stride=2), :].astype(LOW)


def mirrored(table, even, odd):
    half = table.shape[1] // 2
    first = dot(table[:, :half], even[...], 1, 0)
    second = dot(table[:, half:], odd[...], 1, 0)
    total, rest = first + second, first - second
    size = table.shape[0] // 2
    return total[:size], total[size:], rest[:size], rest[size:]


def join_places(waves_t, even, odd, halves):
    length = waves_t.shape[0]
    half = length // 2
    for start, source in enumerate((even, odd)):
        part = dot(waves_t[start * half : (start + 1) * half, :], source[...], 1, 0) * (1.0 / length)
        for i in range(2):
            halves[i, pl.ds(start, half, stride=2), :] = part[:, i * 128 : (i + 1) * 128]
    return jnp.concatenate([halves[0], halves[1]], axis=1)


def mixer_kernel(
    index, lengths, buckets, get, outs, leave,
    wide_buf, series_wide, gate_buf, kernel_even, kernel_odd, series_even, series_odd, even_buf, odd_buf,
):
    mixed, h_first, projected, convolved, kernel_spec, series_spec = outs
    gain, w_in = get(1), None
    for i, code in enumerate(CODES):
        block = get((0, 3, 4, 5)[i])
        normed, _ = norm_forward(block[...].astype(WIDE))
        low = (normed * gain[...]).astype(LOW)
        rows = block.shape[0]
        place = pl.ds(block_start(code, rows), rows)
        h_first[place, :] = low
        leave(1, place)
        w_in = get(2)
        projected[place, :] = dot(low, w_in[...], 1, 0).astype(LOW)
        leave(2, place)
    length = projected.shape[0]
    row = lax.broadcasted_iota(jnp.int32, (length, LANES), 0)
    mask = (row < lengths[index]).astype(WIDE)
    filters, taps = get(6), get(7)

    def stream(s):
        raw = projected[:, s * LANES : (s + 1) * LANES].astype(WIDE)
        return mask * tap_sum(raw, taps, 3 * s, row, 1)

    channels = filters.shape[1] // 2
    both = filters[...].astype(WIDE)
    chosen = jnp.where(buckets[index] == 0, both, pltpu.roll(both, channels, 1))[:, :LANES]
    kernel = chosen + tap_sum(stream(1), taps, 9, row, 1)
    split_places(kernel, wide_buf, kernel_even, kernel_odd)
    split_places(stream(2), series_wide, series_even, series_odd)
    gate_buf[...] = stream(0)
    waves = get(8)
    size = length // TILES
    half = size // 2
    for i in range(TILES):
        table = waves[i * size : (i + 1) * size, :]
        k = mirrored(table, kernel_even, kernel_odd)
        s = mirrored(table, series_even, series_odd)
        for j in range(4):
            place = slice((2 * i + j // 2) * size + (j % 2) * half, (2 * i + j // 2) * size + (j % 2 + 1) * half)
            kernel_spec[place, :] = k[j].astype(LOW)
            series_spec[place, :] = s[j].astype(LOW)
        place = slice(2 * i * size, 2 * (i + 1) * size)
        leave(4, place)
        leave(5, place)
        real, imag = k[0] * s[0] - k[1] * s[1], k[0] * s[1] + k[1] * s[0]
        real_rest, imag_rest = k[2] * s[2] - k[3] * s[3], k[2] * s[3] + k[3] * s[2]
        upper, lower = slice(i * size, i * size + half), slice(i * size + half, (i + 1) * size)
        even_buf[upper, :] = (real + real_rest).astype(LOW)
        even_buf[lower, :] = (imag + imag_rest).astype(LOW)
        odd_buf[upper, :] = (real - real_rest).astype(LOW)
        odd_buf[lower, :] = (imag - imag_rest).astype(LOW)
    value = join_places(get(9), even_buf, odd_buf, wide_buf)
    mixed[...] = (value * gate_buf[...]).astype(LOW)
    leave(0)
    convolved[...] = value.astype(LOW)
    leave(3)


def middle_kernel(index, pieces, lengths, get, outs, leave):
    h_out, grads_out, hidden_out, d_out_out, send_d, send_o, keep_d, keep_o, residual = outs[:9]
    hidden = hidden_out.shape[1]
    gain, outs_first, tile_first, weights_first = get(0), 1, 5, 29
    for tile in (1, 0):
        operands = tile_first + 12 * (1 - tile)
        rows, width = get(operands).shape
        whole = slice(2 * tile * rows, 2 * (tile + 1) * rows)
        for i in range(2):
            block = 2 * tile + i
            start = block_start(CODES[block], rows)
            place = slice(block * rows, (block + 1) * rows)
            value = get(operands + 6 * i)[...].astype(WIDE)
            for j in range(4):
                value = value + dot(get(operands + 6 * i + 1 + j)[...], get(outs_first + j)[...], 1, 1)
            if block == 0:
                residual[...] = value
                leave(8)
            normed, _ = norm_forward(value)
            h_out[place, :] = (normed * gain[...]).astype(LOW)
            row = start + lax.broadcasted_iota(jnp.int32, (rows, width), 0)
            grads = get(operands + 6 * i + 5)[...].astype(WIDE)
            d_out_out[place, :] = jnp.where(row < lengths[index], grads, 0.0).astype(LOW)
        leave(0, whole)
        leave(3, whole)
        if not pieces:
            weights = get(weights_first)
        elif tile == 1:
            weights = outs[9]
            for i in range(9):
                get(weights_first + i)
            leave(9)
        for first in range(0, hidden, 256):
            gate_place = slice(first, first + 256)
            up_place = slice(hidden + first, hidden + first + 256)
            down_place = slice(2 * hidden + first, 2 * hidden + first + 256)
            gate = dot(h_out[whole, :], weights[:, gate_place], 1, 0)
            up = dot(h_out[whole, :], weights[:, up_place], 1, 0)
            d_hidden = dot(d_out_out[whole, :], weights[:, down_place], 1, 0)
            slope = math.sqrt(2.0 / math.pi)
            square = gate * gate
            bent = jnp.tanh(slope * gate * (1.0 + 0.044715 * square))
            rise = 0.5 * (1.0 + bent)
            active = gate * rise
            hidden_out[whole, gate_place] = (active * up).astype(LOW)
            d_active = rise + 0.5 * gate * (1.0 - bent * bent) * (slope * (1.0 + 0.134145 * square))
            grads_out[whole, gate_place] = (d_hidden * up * d_active).astype(LOW)
            grads_out[whole, up_place] = (d_hidden * active).astype(LOW)
        leave(1, whole)
        leave(2, whole)
        d_normed = dot(grads_out[whole, :], weights[:, : 2 * hidden], 1, 1)
        (send_d if tile else keep_d)[...] = d_normed.astype(LOW)
        leave(4 if tile else 6)
        out = dot(hidden_out[whole, :], weights[:, 2 * hidden :], 1, 1)
        (send_o if tile else keep_o)[...] = out.astype(LOW)
        leave(5 if tile else 7)


def norm_step(d_out, values, extra, gain):
    normed, scale = norm_forward(values)
    scaled = d_out * gain
    first_mean = jnp.mean(scaled, axis=-1, keepdims=True)
    second_mean = jnp.mean(scaled * normed, axis=-1, keepdims=True)
    return extra + scale * (scaled - first_mean - normed * second_mean), normed


def norm_kernel(get, outs, leave):
    keep, arrived, last, values, extra, gain = (get(i) for i in range(6))
    d_wide, d_low, gain_grad = outs
    d_out = keep[...].astype(WIDE) + arrived[...].astype(WIDE) + last[...].astype(WIDE)
    total, normed = norm_step(d_out, values[...], extra[...].astype(WIDE), gain[...])
    d_low[...] = total.astype(LOW)
    leave(1)
    d_wide[...] = total
    leave(0)
    gain_grad[...] = jnp.sum(d_out * normed, axis=0, keepdims=True)
    leave(2)


def finish_kernel(get, outs, leave):
    gain = get(0)
    for r in range(2):
        keep, arrived, last, tokens, extra = (get(1 + 5 * r + i) for i in range(5))
        d_out = keep[...].astype(WIDE) + arrived[...].astype(WIDE) + last[...].astype(WIDE)
        outs[0][r], _ = norm_step(d_out, tokens[...].astype(WIDE), extra[...], gain[...])
        leave(0, r)


def output_kernel(lengths, get, outs, leave):
    for r in range(2):
        keep, arrived, last, residual = (get(4 * r + i) for i in range(4))
        value = residual[...] + keep[...].astype(WIDE) + arrived[...].astype(WIDE) + last[...].astype(WIDE)
        row = block_start(0, value.shape[0]) + lax.broadcasted_iota(jnp.int32, value.shape, 0)
        outs[0][r] = jnp.where(row < lengths[r], value, 0.0).astype(LOW)
        leave(0, r)


def back_kernel(
    index, lengths, get, outs, leave,
    mix_buf, conv_buf, series_halves, kernel_halves, conv_even, conv_odd, kernel_even, kernel_odd, series_even, series_odd,
):
    d_projected, kernel_out, tap_grads, out_grad, send, keep, gain_grad = outs
    w_out = get(0)
    for i, code in enumerate(CODES):
        block = get(1 + i)
        rows = block.shape[0]
        mix_buf[pl.ds(block_start(code, rows), rows), :] = dot(block[...], w_out[...], 1, 0)
    projected, taps = get(5), get(6)
    length = projected.shape[0]
    row = lax.broadcasted_iota(jnp.int32, (length, LANES), 0)
    mask = (row < lengths[index]).astype(WIDE)

    def raw(s):
        return projected[:, s * LANES : (s + 1) * LANES].astype(WIDE)

    d_conv = mix_buf[...] * mask * tap_sum(raw(0), taps, 0, row, 1)
    split_places(d_conv, conv_buf, conv_even, conv_odd)
    waves, series_spec, kernel_spec = get(7), get(8), get(9)
    size = length // TILES
    half = size // 2
    for i in range(TILES):
        g = mirrored(waves[i * size : (i + 1) * size, :], conv_even, conv_odd)
        upper, lower = slice(i * size, i * size + half), slice(i * size + half, (i + 1) * size)
        for spec, even, odd in (
            (series_spec, kernel_even, kernel_odd),
            (kernel_spec, series_even, series_odd),
        ):
            start = 2 * i * size
            a = [spec[start + j * half : start + (j + 1) * half, :].astype(WIDE) for j in range(4)]
            real, imag = g[0] * a[0] + g[1] * a[1], g[1] * a[0] - g[0] * a[1]
            real_rest, imag_rest = g[2] * a[2] + g[3] * a[3], g[3] * a[2] - g[2] * a[3]
            even[upper, :] = (real + real_rest).astype(LOW)
            even[lower, :] = (imag + imag_rest).astype(LOW)
            odd[upper, :] = (real - real_rest).astype(LOW)
            odd[lower, :] = (imag - imag_rest).astype(LOW)
    waves_t = get(10)
    d_kernel = join_places(waves_t, kernel_even, kernel_odd, kernel_halves)
    kernel_out[...] = d_kernel.astype(LOW)
    leave(1)
    d_series = join_places(waves_t, series_even, series_odd, series_halves)

    def finish(s, grads):
        series = raw(s)
        for j in range(3):
            tap_grads[3 * s + j : 3 * s + j + 1, :] = jnp.sum(
                grads * shifted(series, j, row), axis=0, keepdims=True
            )
        d_projected[:, s * LANES : (s + 1) * LANES] = tap_sum(grads, taps, 3 * s, row, -1).astype(LOW)

    finish(2, d_series * mask)
    grads = d_kernel
    condition = mask * tap_sum(raw(1), taps, 3, row, 1)
    for j in range(3):
        tap_grads[9 + j : 10 + j, :] = jnp.sum(
            grads * shifted(condition, j, row), axis=0, keepdims=True
        )
    finish(1, mask * tap_sum(grads, taps, 9, row, -1))
    convolved = get(11)
    finish(0, mix_buf[...] * convolved[...].astype(WIDE) * mask)
    leave(0)
    leave(2)
    w_in, h_first = get(12), get(14)
    gain_sum = 0.0
    for i in (2, 3, 0, 1):
        place = pl.ds(block_start(CODES[i], rows), rows)
        part = dot(d_projected[place, :], w_in[...], 1, 1)
        gain_sum = gain_sum + jnp.sum(part * h_first[place, :].astype(WIDE), axis=0, keepdims=True)
        if i < 2:
            keep[i * rows : (i + 1) * rows, :] = part.astype(LOW)
        else:
            send[(i - 2) * rows : (i - 1) * rows, :] = part.astype(LOW)
        if i == 3:
            leave(4)
    leave(5)
    gain_grad[...] = gain_sum
    leave(6)
    mixed = get(13)
    total = None
    for i, code in enumerate(CODES):
        place = pl.ds(block_start(code, rows), rows)
        part = dot(get(1 + i)[...], mixed[place, :], 0, 0)
        total = part if total is None else total + part
    out_grad[...] = total.astype(LOW)
    leave(3)


def tail_kernel(packed, channels, buckets, get, outs, leave):
    grad_in, g0, g1, k0, k1 = (get(i) for i in range(5))
    grads, filters = outs
    gap = LANES - channels
    width = grad_in.shape[0]
    out_grad = g0[...].astype(WIDE) + g1[...].astype(WIDE)
    lane = lax.broadcasted_iota(jnp.int32, (width, LANES), 1)
    for s in range(3):
        place = slice(s * LANES, (s + 1) * LANES)
        grad = grad_in[:, place].astype(WIDE)
        behind = pltpu.roll(out_grad, channels - s * gap, 1)
        grads[:, place] = jnp.where(lane < channels, grad, behind).astype(LOW)
    first = [jnp.where(buckets[r] == 0, 1.0, 0.0) for r in range(2)]
    parts = [k0[...].astype(WIDE), k1[...].astype(WIDE)]
    zeros = jnp.zeros((k0.shape[0], 2 * channels - LANES), WIDE)
    sums = [
        jnp.concatenate([parts[0] * a + parts[1] * b, zeros], axis=1)
        for a, b in (first, [1.0 - first[0], 1.0 - first[1]])
    ]
    filters[...] = (sums[0] + pltpu.roll(sums[1], channels, 1)).astype(filters.dtype)
    if packed:
        rows = width // len(RING)
        spare = rows // 3
        for i in range(len(RING)):
            start = i * (rows + spare)
            place = slice(i * rows, (i + 1) * rows)
            grads[place, 3 * LANES : 3 * LANES + 2 * channels] = filters[start : start + rows, :].astype(LOW)
            for j in range(3):
                place = slice(i * rows + j * spare, i * rows + (j + 1) * spare)
                grads[place, 3 * LANES + 2 * channels :] = filters[
                    start + rows : start + rows + spare, j * 128 : (j + 1) * 128
                ].astype(LOW)
    else:
        leave(1)
    leave(0)


ANY = pl.BlockSpec(memory_space=pl.ANY)
SCALARS = pl.BlockSpec(memory_space=pltpu.SMEM)


def call(kernel, scalars, operands, results, scratch, flops, name, limit=60, pieces=()):
    operands = [x if isinstance(x, tuple) else (x, None, x.shape) for x in operands]
    count, first_piece = len(operands), len(operands)
    blocks = [block for block, _ in pieces]
    buffers = [pltpu.VMEM(shape, x.dtype) for x, _, shape in operands]
    finals = [pltpu.VMEM(shape, kind) for shape, kind in results]
    taken = len(scalars) + count + len(blocks)
    spare = 2 * len(results) + 12

    def body(*refs):
        outside, ours = refs[: taken + len(results)], refs[taken + len(results) :]
        left, ours = outside[taken:], ours
        inside, outs = ours[:count], ours[count : count + len(finals)]
        extra, sems = ours[count + len(finals) : -1], ours[-1]
        copies = []
        for i, (_, view, _) in enumerate(operands):
            source = outside[len(scalars) + i]
            source = source if view is None else view(source)
            copies.append(pltpu.make_async_copy(source, inside[i], sems.at[i]))
        for i, (block, start) in enumerate(pieces):
            size = block.shape[0]
            place = pl.ds(pl.multiple_of(start(), 16), size)
            copies.append(
                pltpu.make_async_copy(
                    outside[len(scalars) + count + i], outs[-1].at[place, :], sems.at[count + i]
                )
            )
        for copy in copies:
            copy.start()
        waited = set()
        leaving = []

        def get(i):
            if i not in waited:
                copies[i].wait()
                waited.add(i)
            return inside[i] if i < first_piece else None

        def leave(i, place=None):
            source, target = outs[i], left[i]
            if isinstance(place, int):
                source, target = source.at[place], target.at[place]
            elif place is not None:
                source, target = source.at[place, :], target.at[place, :]
            sem = sems.at[len(copies) + len(leaving)]
            leaving.append(pltpu.make_async_copy(source, target, sem))
            leaving[-1].start()

        kernel(*outside[: len(scalars)], get, outs, leave, *extra)
        for i in range(len(copies)):
            get(i)
        for copy in leaving:
            copy.wait()

    moved = sum(math.prod(shape) * x.dtype.itemsize for x, _, shape in operands)
    moved += sum(math.prod(shape) * jnp.dtype(kind).itemsize for shape, kind in results)
    return pl.pallas_call(
        body,
        in_specs=[SCALARS] * len(scalars) + [ANY] * (count + len(blocks)),
        out_specs=[ANY] * len(results),
        out_shape=[jax.ShapeDtypeStruct(shape, kind) for shape, kind in results],
        scratch_shapes=[
            *buffers,
            *finals,
            *scratch,
            pltpu.SemaphoreType.DMA((count + len(blocks) + spare,)),
        ],
        compiler_params=pltpu.CompilerParams(vmem_limit_bytes=limit * 2**20),
        cost_estimate=pl.CostEstimate(flops=flops, bytes_accessed=moved, transcendentals=0),
        name=name,
    )(*scalars, *[x for x, _, _ in operands], *blocks)


def of_row(index, array):
    return array, lambda ref: ref.at[index], array.shape[1:]


def first_rows(rows, array):
    return array, lambda ref: ref.at[pl.ds(0, rows), :], (rows,) + array.shape[1:]


def block_rows(code, rows, array):
    view = lambda ref: ref.at[pl.ds(block_start(code, rows), rows), :]
    return array, view, (rows,) + array.shape[1:]


def mixer_forward(index, scalars, tokens, w_in, filters, taps, gain, tables):
    _, rows, width = tokens[0].shape
    length = 4 * rows
    spec = ((2 * length, LANES), LOW)
    blocks = [of_row(index, block) for block in tokens]
    return call(
        functools.partial(mixer_kernel, index),
        scalars,
        [blocks[0], gain, w_in, *blocks[1:], filters, taps, *tables],
        [
            ((length, LANES), LOW),
            ((length, width), LOW),
            ((length, 3 * LANES), LOW),
            ((length, LANES), LOW),
            spec,
            spec,
        ],
        [pltpu.VMEM((2, length, 128), WIDE)] * 2
        + [pltpu.VMEM((length, LANES), WIDE)]
        + [pltpu.VMEM((length // 2, LANES), LOW)] * 4
        + [pltpu.VMEM((length, LANES), LOW)] * 2,
        10**10,
        "mixer",
    )


def middle(index, lengths, tokens, grads, mixed, outs, gain, weights, gate):
    _, rows, width = tokens[0].shape
    length = 4 * rows
    hidden = weights[0].shape[1] // 3
    results = [
        ((length, width), LOW),
        ((length, 2 * hidden), LOW),
        ((length, hidden), LOW),
        ((length, width), LOW),
        *[((2 * rows, width), LOW)] * 4,
        ((rows, width), WIDE),
    ]
    operands = [after(gain, gate), *outs]
    for block in (2, 3, 0, 1):
        operands.append(of_row(index, tokens[block]))
        operands += [block_rows(CODES[block], rows, part) for part in mixed]
        operands.append(of_row(index, grads[block]))
    pieces = []
    if len(weights) > 1:
        size = weights[0].shape[0]

        def start(offset, first=0):
            return lambda: ring_member(ring_place() + offset) * size + first

        offsets = [(offset, 0) for offset in OFFSETS] + [(4, 0), (4, size // 2)]
        pieces = [(block, start(*where)) for block, where in zip(weights, offsets)]
        results.append(((width, 3 * hidden), LOW))
    else:
        operands += weights
    return call(
        functools.partial(middle_kernel, index, bool(pieces)),
        [lengths],
        operands,
        results,
        [],
        16 * 10**9,
        "middle",
        60,
        pieces,
    )


def norm_back(keep, arrived, last, values, extra, gain):
    rows, width = last.shape
    return call(
        norm_kernel,
        [],
        [first_rows(rows, keep), first_rows(rows, arrived), last, values, first_rows(rows, extra), gain],
        [((rows, width), WIDE), ((rows, width), LOW), ((1, width), WIDE)],
        [],
        2 * 10**9,
        "norm_back",
        24,
    )


def finish(keeps, arrived, lasts, tokens, extras, gain):
    rows, width = lasts[0].shape
    operands = [gain]
    for r in range(2):
        operands += [first_rows(rows, keeps[r]), first_rows(rows, arrived[r]), lasts[r]]
        operands += [of_row(r, tokens), extras[r]]
    return call(finish_kernel, [], operands, [((2, rows, width), WIDE)], [], 3 * 10**9, "finish", 24)[0]


def output(lengths, keeps, arrived, lasts, residuals):
    rows, width = lasts[0].shape
    operands = []
    for r in range(2):
        operands += [first_rows(rows, keeps[r]), first_rows(rows, arrived[r]), lasts[r], residuals[r]]
    return call(
        output_kernel, [lengths], operands, [((2, rows, width), LOW)], [], 3 * 10**9, "output", 24
    )[0]


def mixer_backward(index, lengths, grads, w_out, w_in, kept, taps, tables):
    rows, width = grads[0].shape
    length = 4 * rows
    mixed, h_first, projected, convolved, kernel_spec, series_spec = kept
    return call(
        functools.partial(back_kernel, index),
        [lengths],
        [
            w_out,
            *grads,
            projected,
            taps,
            tables[0],
            series_spec,
            kernel_spec,
            tables[1],
            convolved,
            w_in,
            mixed,
            h_first,
        ],
        [
            ((length, 3 * LANES), LOW),
            ((length, LANES), LOW),
            ((12, LANES), WIDE),
            ((width, LANES), LOW),
            ((2 * rows, width), LOW),
            ((2 * rows, width), LOW),
            ((1, width), WIDE),
        ],
        [pltpu.VMEM((length, LANES), WIDE)]
        + [pltpu.VMEM((2, length, 128), WIDE)] * 3
        + [pltpu.VMEM((length // 2, LANES), LOW)] * 2
        + [pltpu.VMEM((length, LANES), LOW)] * 4,
        14 * 10**9,
        "mixer_back",
    )


def tail(packed, channels, buckets, grad_in, out_grads, d_kernels):
    width = grad_in.shape[0]
    length = d_kernels[0].shape[0]
    extra = 2 * channels + 128 if packed else 0
    return call(
        functools.partial(tail_kernel, packed, channels),
        [buckets],
        [grad_in, *out_grads, *d_kernels],
        [
            ((width, 3 * LANES + extra), LOW),
            ((length, 2 * channels), WIDE),
        ],
        [],
        4 * 10**9,
        "tail",
    )


def pack_mixer(w_in, long_filter, w_out):
    rows, _, channels = w_in.shape
    gap = LANES - channels
    turned = w_out.T
    pieces = []
    for s in range(3):
        pieces += [w_in[:, s], turned[:, s * gap : (s + 1) * gap]]
    both = jnp.concatenate([long_filter[0], long_filter[1]], axis=1)
    spare = both[rows:].reshape(both.shape[0] - rows, 3, -1)
    pieces += [both[:rows], spare.transpose(1, 0, 2).reshape(rows, -1)]
    return jnp.concatenate(pieces, axis=1)


def unpack_rows(blocks, channels):
    count, rows, _ = blocks.shape
    spare = blocks[:, :, 2 * channels :].reshape(count, 3, rows // 3, -1)
    spare = spare.transpose(0, 2, 1, 3).reshape(count, rows // 3, -1)
    return jnp.concatenate([blocks[:, :, : 2 * channels], spare], axis=1)


def unpack_out(pack, channels):
    gap = LANES - channels
    return jnp.concatenate(
        [pack[:, s * LANES + channels : s * LANES + channels + gap] for s in range(3)], axis=1
    )


def unpack_mixer(pack, rows, channels):
    w_out = jnp.pad(unpack_out(pack, channels), ((0, 0), (0, LANES - channels)))
    blocks = pack[:, 3 * LANES :].reshape(-1, rows, pack.shape[1] - 3 * LANES)
    filters = unpack_rows(blocks, channels).reshape(-1, 2 * channels)
    return pack[:, : 3 * LANES], filters, w_out


def per_device(
    tokens,
    lengths,
    buckets,
    w_in,
    long_filter,
    w_out,
    w_gu,
    w_down,
    norm_gains,
    short_taps,
    cond_taps,
    cotangent,
):
    row_count, part_len, width = tokens.shape
    channels = short_taps.shape[-1]
    hidden = w_down.shape[0]
    shard = w_in.shape[0]
    rows = range(row_count)
    gains = norm_gains.astype(WIDE)
    taps = jnp.concatenate([short_taps.reshape(9, channels), cond_taps], axis=0).astype(WIDE)
    taps = jnp.pad(taps, ((0, 0), (0, LANES - channels)))
    tables = tuple(jnp.asarray(table) for table in wave_tables(4 * part_len))

    all_tokens = spread(tokens)
    (full_in, filters, part_out), packed_last = gather_mixer(
        pack_mixer(w_in, long_filter, w_out), channels
    )
    w_ff = jnp.concatenate([w_gu.reshape(shard, -1), w_down.T], axis=1)
    ff_blocks = ring_blocks(after(w_ff, packed_last))
    for _ in range(3):
        arrived_ff = next(ff_blocks)

    first = mixer_forward(0, (lengths, buckets), all_tokens, full_in, filters, taps, gains[:1], tables)
    first = after(first, arrived_ff[-2:])
    arrived_ff = ff_blocks.send(first[0])
    second = mixer_forward(
        1, (lengths, buckets), all_tokens, full_in, filters, taps, after(gains[:1], first[0]), tables
    )
    second = after(second, arrived_ff[-2:])
    cotangent = after(cotangent, all_tokens[1])
    all_grads = spread(cotangent, second[0], second[0])
    outs = spread(after(part_out, all_grads[1]), second[0], second[0])
    weights = ff_blocks.send(second[0])
    forward = [first, second]
    first_mixed = first[0]
    inputs = (lengths, all_tokens, all_grads)
    centre = []
    arrived_d = []
    gate = first_mixed
    for r in rows:
        mixed = spread(forward[r][0], gate if r else None)
        centre.append(middle(r, *inputs, mixed, outs, gains[1:], weights, gate))
        if len(weights) > 1:
            weights = [centre[r][9]]
        arrived_d.append(fold_near(centre[r][4]))
        gate = centre[r][4]
    away_d = [fold_away(centre[r][6], arrived_d[r]) for r in rows]
    last_d = [swap(away_d[r], 2) for r in rows]

    d_residual = []
    gain_second = 0.0
    d_low = []
    for r in rows:
        keep_d, residual, d_out = centre[r][6], centre[r][8], centre[r][3]
        d_wide, low, gain_grad = norm_back(
            keep_d, arrived_d[r], after(last_d[r], away_d), residual, d_out, gains[1:]
        )
        d_residual.append(d_wide)
        gain_second = gain_second + gain_grad
        d_low.append(low)

    kept_ff = [after(centre[0][:4], away_d[0]), after(centre[1][:4], away_d)]
    arrived_o = [fold_near(after(centre[r][5], away_d)) for r in rows]
    grad_gu = sum(dot(kept[0], kept[1], 0, 0) for kept in kept_ff)
    grad_down = sum(dot(kept[3], kept[2], 0, 0) for kept in kept_ff)
    grad_gu, grad_down = after((grad_gu.astype(LOW), grad_down.astype(LOW)), last_d, arrived_o)
    ff_steps = ring_sums(jnp.concatenate([grad_gu, grad_down], axis=1))
    ff_sums = [next(ff_steps)]

    backward = []
    arrived_h = []
    gate = None
    for r in rows:
        spread_d = spread(d_low[r], gate)
        if r == 0:
            spread_d[3] = after(spread_d[3], d_low[1])
            beside = ()
        else:
            last_o = [fold_far(centre[i][7], after(arrived_o[i], spread_d[1])) for i in rows]
            spread_d[3] = after(spread_d[3], ff_sums[1])
            beside = last_o
        back = mixer_backward(r, lengths, spread_d, part_out, full_in, forward[r], taps, tables)
        ff_sums.append(next(ff_steps))
        back = after(back, ff_sums[-1], beside)
        backward.append(back)
        arrived_h.append(fold_near(back[4]))
        gate = back[4]
    away_h = [fold_away(backward[r][5], arrived_h[r]) for r in rows]
    last_h = [swap(away_h[r], 2) for r in rows]

    packed = lax.axis_size("batch") == len(RING)
    d_projected = [after(backward[0][0], away_h[0]), after(backward[1][0], arrived_h)]
    grads_in = [dot(forward[r][1], d_projected[r], 0, 0) for r in rows]
    ff_sums.append(ff_steps.send((None, grads_in[0])))
    ff_sums.append(next(ff_steps))
    grad_taps = sum(backward[r][2] for r in rows)[:, :channels]
    gain_first = sum(backward[r][6] for r in rows) / gains[:1]
    smalls = jnp.concatenate(
        [gain_first.reshape(-1), gain_second.reshape(-1), grad_taps.reshape(-1)]
    )
    grad_in = grads_in[0] + grads_in[1]
    grad_in = after(grad_in.astype(LOW), away_h)
    grad_mixer, grad_filter = tail(
        packed,
        channels,
        buckets,
        grad_in,
        [backward[r][3] for r in rows],
        [backward[r][1] for r in rows],
    )
    grad_mixer, grad_filter = after((grad_mixer, grad_filter), last_h)
    smalls = list(small_sums(after(smalls.reshape(-1, 128), grad_mixer), "batch"))
    mixer_steps = ring_sums(grad_mixer)
    mixer_sums = [next(mixer_steps)]
    mixer_sums.append(next(mixer_steps))
    outputs = output(
        after(lengths, mixer_sums[0]),
        [centre[r][7] for r in rows],
        arrived_o,
        last_o,
        [centre[r][8] for r in rows],
    )
    mixer_sums[1], outputs = after((mixer_sums[1], outputs), ff_sums[4], smalls[1])
    mixer_sums.append(mixer_steps.send((outputs, None)))
    grad_ff = ff_steps.send((mixer_sums[1], None))
    d_inputs = finish(
        [backward[r][5] for r in rows],
        arrived_h,
        last_h,
        tokens,
        d_residual,
        after(gains[:1], mixer_sums[1]),
    )
    mixer_sums.append(mixer_steps.send(((d_inputs, smalls[min(2, len(smalls) - 1)]), None)))
    next(mixer_steps)
    grad_mixer = next(mixer_steps)
    if packed:
        grad_filter = unpack_rows(grad_mixer[None, :, 3 * LANES :], channels)[0]
    else:
        grad_filter = list(ring_sums(grad_filter))[-1]
    grad_in = grad_mixer[:, : 3 * LANES].reshape(-1, 3, LANES)[:, :, :channels]
    smalls = smalls[-1].reshape(-1)
    small_steps = small_sums(smalls[: 2 * width].reshape(-1, 128), "chan")
    grad_gains = list(small_steps)[-1].reshape(2, width)
    grad_taps = smalls[2 * width :].reshape(12, channels)
    return (
        outputs,
        d_inputs,
        grad_in,
        jnp.stack([grad_filter[:, :channels], grad_filter[:, channels:]]),
        unpack_out(grad_mixer, channels).T,
        grad_ff[:, : 2 * hidden].reshape(-1, 2, hidden),
        grad_ff[:, 2 * hidden :].T,
        grad_gains,
        grad_taps[:9].reshape(3, 3, channels),
        grad_taps[9:],
    )


def solution(mesh):
    placed = (
        P("batch", "chan", None),
        P("batch"),
        P("batch"),
        P("batch", None, "chan"),
        P(None, "batch", "chan"),
        P("chan", "batch"),
        P("batch", None, "chan"),
        P("chan", "batch"),
        P(),
        P(None, None, "chan"),
        P(None, "chan"),
        P("batch", "chan", None),
    )
    return jax.shard_map(
        per_device,
        mesh=mesh,
        in_specs=placed,
        out_specs=(
            P("batch", "chan", None),
            P("batch", "chan", None),
            P("batch", None, "chan"),
            P(None, "batch", "chan"),
            P("chan", "batch"),
            P("batch", None, "chan"),
            P("chan", "batch"),
            P(),
            P(None, None, "chan"),
            P(None, "chan"),
        ),
        check_vma=False,
    )
```

```python
import functools
import math

import jax
import jax.numpy as jnp
import numpy as np
from jax import lax
from jax.experimental import pallas as pl
from jax.experimental.pallas import tpu as pltpu
from jax.sharding import PartitionSpec as P

EPSILON = 1e-05
LOW = jnp.bfloat16
WIDE = jnp.float32
RING = (0, 2, 4, 6, 7, 5, 3, 1)
CODES = (0, 2, 1, 3)
LANES = 256


def dot(left, right, left_dim, right_dim, kind=WIDE):
    return lax.dot_general(
        left, right, (((left_dim,), (right_dim,)), ((), ())), preferred_element_type=kind
    )


TILES = 2


@functools.lru_cache(maxsize=None)
def wave_tables(length):
    half = length // 2
    bins = np.arange(half, dtype=np.int64)[:, None]
    places = np.arange(length, dtype=np.int64)
    places = np.concatenate([places[::2], places[1::2]])[None, :]
    turns = ((2 * bins + 1) * places) % (4 * length)
    angles = turns * (2.0 * math.pi / (4 * length))
    shape = (TILES, half // TILES, length)
    both = np.stack([np.cos(angles).reshape(shape), -np.sin(angles).reshape(shape)], axis=1)
    both = both.reshape(length, length)
    return both.astype(jnp.bfloat16), np.ascontiguousarray(both.T).astype(jnp.bfloat16)


def swap(block, step):
    size = lax.axis_size("chan")
    return lax.ppermute(block, "chan", [(i, i ^ step) for i in range(size)])


def after(values, *earlier):
    return lax.optimization_barrier((values, earlier))[0]


def spread(block, gate=None, near_gate=None):
    far = swap(block, 2)
    near = swap(block if near_gate is None else after(block, near_gate), 1)
    return [block, far, near, swap(far if gate is None else after(far, gate), 1)]


def fold_near(send):
    return swap(send, 1)


def fold_away(keep, arrived):
    half = keep.shape[0] // 2
    return (keep[half:].astype(WIDE) + arrived[half:].astype(WIDE)).astype(LOW)


def fold_far(keep, arrived):
    return swap(fold_away(keep, arrived), 2)


def ring_steps(block, shift):
    count = len(RING)
    pairs = [(RING[i], RING[(i + shift) % count]) for i in range(count)]
    return lax.ppermute(block, "batch", pairs)


def ring_place():
    index = lax.axis_index("batch")
    return jnp.where(index % 2 == 0, index // 2, len(RING) - 1 - index // 2)


def ring_member(place):
    place = lax.rem(place, len(RING))
    return jnp.where(place < len(RING) // 2, 2 * place, 2 * (len(RING) - 1 - place) + 1)


OFFSETS = (0, 7, 1, 6, 2, 5, 3)


def ring_blocks(block):
    if lax.axis_size("batch") != len(RING):
        whole = [lax.all_gather(block, "batch", axis=0, tiled=True)]
        for _ in range(5):
            yield whole
        return
    half = block.shape[0] // 2
    blocks = [block]
    up = down = block
    for step in range(4):
        gate = yield blocks
        if gate is not None:
            up, down = after((up, down), gate)
        if step == 3:
            up, down = up[:half], down[half:]
        up, down = ring_steps(up, 1), ring_steps(down, -1)
        blocks = [*blocks, up, down]
    yield blocks


def place_mixer_kernel(get, outs, leave, joined):
    w_in, filters, w_out = outs
    blocks = [get(i) for i in range(9)]
    rows = blocks[0].shape[0]
    half = rows // 2
    spare = rows // 3
    channels = filters.shape[1] // 2
    gap = LANES - channels
    place = ring_place()
    joined[:half, :] = blocks[7][...]
    joined[half:, :] = blocks[8][...]
    w_out[:, channels:] = jnp.zeros((w_out.shape[0], gap), w_out.dtype)
    for block, offset in zip((*blocks[:7], joined), (*OFFSETS, 4)):
        member = ring_member(place + offset)
        start = pl.multiple_of(member * rows, rows)
        w_in[pl.ds(start, rows), :] = block[:, : 3 * LANES]
        for s in range(3):
            w_out[pl.ds(start, rows), s * gap : (s + 1) * gap] = block[
                :, s * LANES + channels : (s + 1) * LANES
            ]
        start = pl.multiple_of(member * (rows + spare), rows + spare)
        filters[pl.ds(start, rows), :] = block[:, 3 * LANES : 3 * LANES + 2 * channels]
        start = pl.multiple_of(start + rows, spare)
        for j in range(3):
            filters[pl.ds(start, spare), j * 128 : (j + 1) * 128] = block[
                j * spare : (j + 1) * spare, 3 * LANES + 2 * channels :
            ]
    for i in range(3):
        leave(i)


def gather_mixer(block, channels):
    count = lax.axis_size("batch")
    rows, columns = block.shape
    if count != len(RING):
        pack = lax.all_gather(block, "batch", axis=0, tiled=True)
        return unpack_mixer(pack, rows, channels), [pack]
    blocks = list(ring_blocks(block))[-1]
    whole = call(
        place_mixer_kernel,
        [],
        blocks,
        [
            ((count * rows, 3 * LANES), block.dtype),
            ((count * (rows + rows // 3), 2 * channels), block.dtype),
            ((count * rows, LANES), block.dtype),
        ],
        [pltpu.VMEM((rows, columns), block.dtype)],
        2 * 10**9,
        "place_mixer",
    )
    return whole, blocks[7:]


def ring_sums(partial):
    count = lax.axis_size("batch")
    if count != len(RING):
        total = lax.psum_scatter(partial.astype(LOW), "batch", scatter_dimension=0, tiled=True)
        for _ in range(5):
            gate, _ = (yield total) or (None, None)
            if gate is not None:
                total = after(total, gate)
        yield total.astype(WIDE)
        return
    place = ring_place()
    rows = partial.shape[0] // count
    half = rows // 2

    def part(offset, first=0, size=rows):
        start = ring_member(place + offset) * rows + first
        return lax.dynamic_slice_in_dim(partial, start, size, 0).astype(WIDE)

    up, down = part(4, 0, half).astype(LOW), part(4, half, half).astype(LOW)
    gate, _ = (yield up, down) or (None, None)
    if gate is not None:
        up, down = after((up, down), gate)
    up, down = ring_steps(up, 1).astype(WIDE), ring_steps(down, -1).astype(WIDE)
    up = part(3) + jnp.concatenate([up, jnp.zeros_like(up)], axis=0)
    down = part(5) + jnp.concatenate([jnp.zeros_like(down), down], axis=0)
    for step in (2, 1, 0):
        up, down = up.astype(LOW), down.astype(LOW)
        gate, behind = (yield up, down) or (None, None)
        if gate is not None:
            up, down = after((up, down), gate)
        up, down = ring_steps(up, 1), ring_steps(down, -1)
        if behind is not None:
            up, down = after((up, down), behind)
        if step:
            up = up.astype(WIDE) + part(step)
            down = down.astype(WIDE) + part(count - step)
    gate, _ = (yield up, down) or (None, None)
    if gate is not None:
        up, down = after((up, down), gate)
    yield up.astype(WIDE) + down.astype(WIDE) + part(0)


def small_sums(values, axis):
    size = lax.axis_size(axis)
    if size & (size - 1) or size > 8:
        values = lax.psum(values, axis)
        yield values
        yield values
        return
    step = 1
    while step < size:
        gate = yield values
        if gate is not None:
            values = after(values, gate)
        values = values + lax.ppermute(values, axis, [(i, i ^ step) for i in range(size)])
        step *= 2
    yield values


def norm_forward(values):
    centre = jnp.mean(values, axis=-1, keepdims=True)
    scale = lax.rsqrt(jnp.mean(values * values, axis=-1, keepdims=True) - centre * centre + EPSILON)
    return (values - centre) * scale, scale


def block_start(code, rows):
    return pl.multiple_of((lax.axis_index("chan") ^ code) * rows, rows)


def shifted(series, offset, row):
    if offset == 0:
        return series
    length = series.shape[0]
    moved = pltpu.roll(series, offset % length, 0)
    inside = row >= offset if offset > 0 else row < length + offset
    return jnp.where(inside, moved, 0.0)


def tap_sum(series, taps, first, row, direction):
    total = taps[first : first + 1, :] * series
    for j in (1, 2):
        total = total + taps[first + j : first + j + 1, :] * shifted(series, direction * j, row)
    return total


def split_places(value, halves, even, odd):
    half = value.shape[0] // 2
    for i in range(2):
        lanes = slice(i * 128, (i + 1) * 128)
        halves[i] = value[:, lanes]
        even[:, lanes] = halves[i, pl.ds(0, half, stride=2), :].astype(LOW)
        odd[:, lanes] = halves[i, pl.ds(1, half, stride=2), :].astype(LOW)


def mirrored(table, even, odd):
    half = table.shape[1] // 2
    first = dot(table[:, :half], even[...], 1, 0)
    second = dot(table[:, half:], odd[...], 1, 0)
    total, rest = first + second, first - second
    size = table.shape[0] // 2
    return total[:size], total[size:], rest[:size], rest[size:]


def join_places(waves_t, even, odd, halves):
    length = waves_t.shape[0]
    half = length // 2
    for start, source in enumerate((even, odd)):
        part = dot(waves_t[start * half : (start + 1) * half, :], source[...], 1, 0) * (1.0 / length)
        for i in range(2):
            halves[i, pl.ds(start, half, stride=2), :] = part[:, i * 128 : (i + 1) * 128]
    return jnp.concatenate([halves[0], halves[1]], axis=1)


def mixer_kernel(
    index, lengths, buckets, get, outs, leave,
    wide_buf, series_wide, gate_buf, kernel_even, kernel_odd, series_even, series_odd, even_buf, odd_buf,
):
    mixed, h_first, projected, convolved, kernel_spec, series_spec = outs
    gain, w_in = get(1), None
    for i, code in enumerate(CODES):
        block = get((0, 3, 4, 5)[i])
        normed, _ = norm_forward(block[...].astype(WIDE))
        low = (normed * gain[...]).astype(LOW)
        rows = block.shape[0]
        place = pl.ds(block_start(code, rows), rows)
        h_first[place, :] = low
        leave(1, place)
        w_in = get(2)
        projected[place, :] = dot(low, w_in[...], 1, 0).astype(LOW)
        leave(2, place)
    length = projected.shape[0]
    row = lax.broadcasted_iota(jnp.int32, (length, LANES), 0)
    mask = (row < lengths[index]).astype(WIDE)
    filters, taps = get(6), get(7)

    def stream(s):
        raw = projected[:, s * LANES : (s + 1) * LANES].astype(WIDE)
        return mask * tap_sum(raw, taps, 3 * s, row, 1)

    channels = filters.shape[1] // 2
    both = filters[...].astype(WIDE)
    chosen = jnp.where(buckets[index] == 0, both, pltpu.roll(both, channels, 1))[:, :LANES]
    kernel = chosen + tap_sum(stream(1), taps, 9, row, 1)
    split_places(kernel, wide_buf, kernel_even, kernel_odd)
    split_places(stream(2), series_wide, series_even, series_odd)
    gate_buf[...] = stream(0)
    waves = get(8)
    size = length // TILES
    half = size // 2
    for i in range(TILES):
        table = waves[i * size : (i + 1) * size, :]
        k = mirrored(table, kernel_even, kernel_odd)
        s = mirrored(table, series_even, series_odd)
        for j in range(4):
            place = slice((2 * i + j // 2) * size + (j % 2) * half, (2 * i + j // 2) * size + (j % 2 + 1) * half)
            kernel_spec[place, :] = k[j].astype(LOW)
            series_spec[place, :] = s[j].astype(LOW)
        place = slice(2 * i * size, 2 * (i + 1) * size)
        leave(4, place)
        leave(5, place)
        real, imag = k[0] * s[0] - k[1] * s[1], k[0] * s[1] + k[1] * s[0]
        real_rest, imag_rest = k[2] * s[2] - k[3] * s[3], k[2] * s[3] + k[3] * s[2]
        upper, lower = slice(i * size, i * size + half), slice(i * size + half, (i + 1) * size)
        even_buf[upper, :] = (real + real_rest).astype(LOW)
        even_buf[lower, :] = (imag + imag_rest).astype(LOW)
        odd_buf[upper, :] = (real - real_rest).astype(LOW)
        odd_buf[lower, :] = (imag - imag_rest).astype(LOW)
    value = join_places(get(9), even_buf, odd_buf, wide_buf)
    mixed[...] = (value * gate_buf[...]).astype(LOW)
    leave(0)
    convolved[...] = value.astype(LOW)
    leave(3)


def middle_kernel(index, pieces, lengths, get, outs, leave):
    h_out, grads_out, hidden_out, d_out_out, send_d, send_o, keep_d, keep_o, residual = outs[:9]
    hidden = hidden_out.shape[1]
    gain, outs_first, tile_first, weights_first = get(0), 1, 5, 29
    for tile in (1, 0):
        operands = tile_first + 12 * (1 - tile)
        rows, width = get(operands).shape
        whole = slice(2 * tile * rows, 2 * (tile + 1) * rows)
        for i in range(2):
            block = 2 * tile + i
            start = block_start(CODES[block], rows)
            place = slice(block * rows, (block + 1) * rows)
            value = get(operands + 6 * i)[...].astype(WIDE)
            for j in range(4):
                value = value + dot(get(operands + 6 * i + 1 + j)[...], get(outs_first + j)[...], 1, 1)
            if block == 0:
                residual[...] = value
                leave(8)
            normed, _ = norm_forward(value)
            h_out[place, :] = (normed * gain[...]).astype(LOW)
            row = start + lax.broadcasted_iota(jnp.int32, (rows, width), 0)
            grads = get(operands + 6 * i + 5)[...].astype(WIDE)
            d_out_out[place, :] = jnp.where(row < lengths[index], grads, 0.0).astype(LOW)
        leave(0, whole)
        leave(3, whole)
        if not pieces:
            weights = get(weights_first)
        elif tile == 1:
            weights = outs[9]
            for i in range(9):
                get(weights_first + i)
            leave(9)
        for first in range(0, hidden, 256):
            gate_place = slice(first, first + 256)
            up_place = slice(hidden + first, hidden + first + 256)
            down_place = slice(2 * hidden + first, 2 * hidden + first + 256)
            gate = dot(h_out[whole, :], weights[:, gate_place], 1, 0)
            up = dot(h_out[whole, :], weights[:, up_place], 1, 0)
            d_hidden = dot(d_out_out[whole, :], weights[:, down_place], 1, 0)
            slope = math.sqrt(2.0 / math.pi)
            square = gate * gate
            bent = jnp.tanh(slope * gate * (1.0 + 0.044715 * square))
            rise = 0.5 * (1.0 + bent)
            active = gate * rise
            hidden_out[whole, gate_place] = (active * up).astype(LOW)
            d_active = rise + 0.5 * gate * (1.0 - bent * bent) * (slope * (1.0 + 0.134145 * square))
            grads_out[whole, gate_place] = (d_hidden * up * d_active).astype(LOW)
            grads_out[whole, up_place] = (d_hidden * active).astype(LOW)
        leave(1, whole)
        leave(2, whole)
        d_normed = dot(grads_out[whole, :], weights[:, : 2 * hidden], 1, 1)
        (send_d if tile else keep_d)[...] = d_normed.astype(LOW)
        leave(4 if tile else 6)
        out = dot(hidden_out[whole, :], weights[:, 2 * hidden :], 1, 1)
        (send_o if tile else keep_o)[...] = out.astype(LOW)
        leave(5 if tile else 7)


def norm_step(d_out, values, extra, gain):
    normed, scale = norm_forward(values)
    scaled = d_out * gain
    first_mean = jnp.mean(scaled, axis=-1, keepdims=True)
    second_mean = jnp.mean(scaled * normed, axis=-1, keepdims=True)
    return extra + scale * (scaled - first_mean - normed * second_mean), normed


def norm_kernel(get, outs, leave):
    keep, arrived, last, values, extra, gain = (get(i) for i in range(6))
    d_wide, d_low, gain_grad = outs
    d_out = keep[...].astype(WIDE) + arrived[...].astype(WIDE) + last[...].astype(WIDE)
    total, normed = norm_step(d_out, values[...], extra[...].astype(WIDE), gain[...])
    d_low[...] = total.astype(LOW)
    leave(1)
    d_wide[...] = total
    leave(0)
    gain_grad[...] = jnp.sum(d_out * normed, axis=0, keepdims=True)
    leave(2)


def finish_kernel(get, outs, leave):
    gain = get(0)
    for r in range(2):
        keep, arrived, last, tokens, extra = (get(1 + 5 * r + i) for i in range(5))
        d_out = keep[...].astype(WIDE) + arrived[...].astype(WIDE) + last[...].astype(WIDE)
        outs[0][r], _ = norm_step(d_out, tokens[...].astype(WIDE), extra[...], gain[...])
        leave(0, r)


def output_kernel(lengths, get, outs, leave):
    for r in range(2):
        keep, arrived, last, residual = (get(4 * r + i) for i in range(4))
        value = residual[...] + keep[...].astype(WIDE) + arrived[...].astype(WIDE) + last[...].astype(WIDE)
        row = block_start(0, value.shape[0]) + lax.broadcasted_iota(jnp.int32, value.shape, 0)
        outs[0][r] = jnp.where(row < lengths[r], value, 0.0).astype(LOW)
        leave(0, r)


def back_kernel(
    index, lengths, get, outs, leave,
    mix_buf, conv_buf, series_halves, kernel_halves, conv_even, conv_odd, kernel_even, kernel_odd, series_even, series_odd,
):
    d_projected, kernel_out, tap_grads, out_grad, send, keep, gain_grad = outs
    w_out = get(0)
    for i, code in enumerate(CODES):
        block = get(1 + i)
        rows = block.shape[0]
        mix_buf[pl.ds(block_start(code, rows), rows), :] = dot(block[...], w_out[...], 1, 0)
    projected, taps = get(5), get(6)
    length = projected.shape[0]
    row = lax.broadcasted_iota(jnp.int32, (length, LANES), 0)
    mask = (row < lengths[index]).astype(WIDE)

    def raw(s):
        return projected[:, s * LANES : (s + 1) * LANES].astype(WIDE)

    d_conv = mix_buf[...] * mask * tap_sum(raw(0), taps, 0, row, 1)
    split_places(d_conv, conv_buf, conv_even, conv_odd)
    waves, series_spec, kernel_spec = get(7), get(8), get(9)
    size = length // TILES
    half = size // 2
    for i in range(TILES):
        g = mirrored(waves[i * size : (i + 1) * size, :], conv_even, conv_odd)
        upper, lower = slice(i * size, i * size + half), slice(i * size + half, (i + 1) * size)
        for spec, even, odd in (
            (series_spec, kernel_even, kernel_odd),
            (kernel_spec, series_even, series_odd),
        ):
            start = 2 * i * size
            a = [spec[start + j * half : start + (j + 1) * half, :].astype(WIDE) for j in range(4)]
            real, imag = g[0] * a[0] + g[1] * a[1], g[1] * a[0] - g[0] * a[1]
            real_rest, imag_rest = g[2] * a[2] + g[3] * a[3], g[3] * a[2] - g[2] * a[3]
            even[upper, :] = (real + real_rest).astype(LOW)
            even[lower, :] = (imag + imag_rest).astype(LOW)
            odd[upper, :] = (real - real_rest).astype(LOW)
            odd[lower, :] = (imag - imag_rest).astype(LOW)
    waves_t = get(10)
    d_kernel = join_places(waves_t, kernel_even, kernel_odd, kernel_halves)
    kernel_out[...] = d_kernel.astype(LOW)
    leave(1)
    d_series = join_places(waves_t, series_even, series_odd, series_halves)

    def finish(s, grads):
        series = raw(s)
        for j in range(3):
            tap_grads[3 * s + j : 3 * s + j + 1, :] = jnp.sum(
                grads * shifted(series, j, row), axis=0, keepdims=True
            )
        d_projected[:, s * LANES : (s + 1) * LANES] = tap_sum(grads, taps, 3 * s, row, -1).astype(LOW)

    finish(2, d_series * mask)
    grads = d_kernel
    condition = mask * tap_sum(raw(1), taps, 3, row, 1)
    for j in range(3):
        tap_grads[9 + j : 10 + j, :] = jnp.sum(
            grads * shifted(condition, j, row), axis=0, keepdims=True
        )
    finish(1, mask * tap_sum(grads, taps, 9, row, -1))
    convolved = get(11)
    finish(0, mix_buf[...] * convolved[...].astype(WIDE) * mask)
    leave(0)
    leave(2)
    w_in, h_first = get(12), get(14)
    gain_sum = 0.0
    for i in (2, 3, 0, 1):
        place = pl.ds(block_start(CODES[i], rows), rows)
        part = dot(d_projected[place, :], w_in[...], 1, 1)
        gain_sum = gain_sum + jnp.sum(part * h_first[place, :].astype(WIDE), axis=0, keepdims=True)
        if i < 2:
            keep[i * rows : (i + 1) * rows, :] = part.astype(LOW)
        else:
            send[(i - 2) * rows : (i - 1) * rows, :] = part.astype(LOW)
        if i == 3:
            leave(4)
    leave(5)
    gain_grad[...] = gain_sum
    leave(6)
    mixed = get(13)
    total = None
    for i, code in enumerate(CODES):
        place = pl.ds(block_start(code, rows), rows)
        part = dot(get(1 + i)[...], mixed[place, :], 0, 0)
        total = part if total is None else total + part
    out_grad[...] = total.astype(LOW)
    leave(3)


def tail_kernel(packed, channels, buckets, get, outs, leave):
    grad_in, g0, g1, k0, k1 = (get(i) for i in range(5))
    grads, filters = outs
    gap = LANES - channels
    width = grad_in.shape[0]
    out_grad = g0[...].astype(WIDE) + g1[...].astype(WIDE)
    lane = lax.broadcasted_iota(jnp.int32, (width, LANES), 1)
    for s in range(3):
        place = slice(s * LANES, (s + 1) * LANES)
        grad = grad_in[:, place].astype(WIDE)
        behind = pltpu.roll(out_grad, channels - s * gap, 1)
        grads[:, place] = jnp.where(lane < channels, grad, behind).astype(LOW)
    first = [jnp.where(buckets[r] == 0, 1.0, 0.0) for r in range(2)]
    parts = [k0[...].astype(WIDE), k1[...].astype(WIDE)]
    zeros = jnp.zeros((k0.shape[0], 2 * channels - LANES), WIDE)
    sums = [
        jnp.concatenate([parts[0] * a + parts[1] * b, zeros], axis=1)
        for a, b in (first, [1.0 - first[0], 1.0 - first[1]])
    ]
    filters[...] = (sums[0] + pltpu.roll(sums[1], channels, 1)).astype(filters.dtype)
    if packed:
        rows = width // len(RING)
        spare = rows // 3
        for i in range(len(RING)):
            start = i * (rows + spare)
            place = slice(i * rows, (i + 1) * rows)
            grads[place, 3 * LANES : 3 * LANES + 2 * channels] = filters[start : start + rows, :].astype(LOW)
            for j in range(3):
                place = slice(i * rows + j * spare, i * rows + (j + 1) * spare)
                grads[place, 3 * LANES + 2 * channels :] = filters[
                    start + rows : start + rows + spare, j * 128 : (j + 1) * 128
                ].astype(LOW)
    else:
        leave(1)
    leave(0)


ANY = pl.BlockSpec(memory_space=pl.ANY)
SCALARS = pl.BlockSpec(memory_space=pltpu.SMEM)


def call(kernel, scalars, operands, results, scratch, flops, name, limit=60, pieces=()):
    operands = [x if isinstance(x, tuple) else (x, None, x.shape) for x in operands]
    count, first_piece = len(operands), len(operands)
    blocks = [block for block, _ in pieces]
    buffers = [pltpu.VMEM(shape, x.dtype) for x, _, shape in operands]
    finals = [pltpu.VMEM(shape, kind) for shape, kind in results]
    taken = len(scalars) + count + len(blocks)
    spare = 2 * len(results) + 12

    def body(*refs):
        outside, ours = refs[: taken + len(results)], refs[taken + len(results) :]
        left, ours = outside[taken:], ours
        inside, outs = ours[:count], ours[count : count + len(finals)]
        extra, sems = ours[count + len(finals) : -1], ours[-1]
        copies = []
        for i, (_, view, _) in enumerate(operands):
            source = outside[len(scalars) + i]
            source = source if view is None else view(source)
            copies.append(pltpu.make_async_copy(source, inside[i], sems.at[i]))
        for i, (block, start) in enumerate(pieces):
            size = block.shape[0]
            place = pl.ds(pl.multiple_of(start(), 16), size)
            copies.append(
                pltpu.make_async_copy(
                    outside[len(scalars) + count + i], outs[-1].at[place, :], sems.at[count + i]
                )
            )
        for copy in copies:
            copy.start()
        waited = set()
        leaving = []

        def get(i):
            if i not in waited:
                copies[i].wait()
                waited.add(i)
            return inside[i] if i < first_piece else None

        def leave(i, place=None):
            source, target = outs[i], left[i]
            if isinstance(place, int):
                source, target = source.at[place], target.at[place]
            elif place is not None:
                source, target = source.at[place, :], target.at[place, :]
            sem = sems.at[len(copies) + len(leaving)]
            leaving.append(pltpu.make_async_copy(source, target, sem))
            leaving[-1].start()

        kernel(*outside[: len(scalars)], get, outs, leave, *extra)
        for i in range(len(copies)):
            get(i)
        for copy in leaving:
            copy.wait()

    moved = sum(math.prod(shape) * x.dtype.itemsize for x, _, shape in operands)
    moved += sum(math.prod(shape) * jnp.dtype(kind).itemsize for shape, kind in results)
    return pl.pallas_call(
        body,
        in_specs=[SCALARS] * len(scalars) + [ANY] * (count + len(blocks)),
        out_specs=[ANY] * len(results),
        out_shape=[jax.ShapeDtypeStruct(shape, kind) for shape, kind in results],
        scratch_shapes=[
            *buffers,
            *finals,
            *scratch,
            pltpu.SemaphoreType.DMA((count + len(blocks) + spare,)),
        ],
        compiler_params=pltpu.CompilerParams(vmem_limit_bytes=limit * 2**20),
        cost_estimate=pl.CostEstimate(flops=flops, bytes_accessed=moved, transcendentals=0),
        name=name,
    )(*scalars, *[x for x, _, _ in operands], *blocks)


def of_row(index, array):
    return array, lambda ref: ref.at[index], array.shape[1:]


def first_rows(rows, array):
    return array, lambda ref: ref.at[pl.ds(0, rows), :], (rows,) + array.shape[1:]


def block_rows(code, rows, array):
    view = lambda ref: ref.at[pl.ds(block_start(code, rows), rows), :]
    return array, view, (rows,) + array.shape[1:]


def mixer_forward(index, scalars, tokens, w_in, filters, taps, gain, tables):
    _, rows, width = tokens[0].shape
    length = 4 * rows
    spec = ((2 * length, LANES), LOW)
    blocks = [of_row(index, block) for block in tokens]
    return call(
        functools.partial(mixer_kernel, index),
        scalars,
        [blocks[0], gain, w_in, *blocks[1:], filters, taps, *tables],
        [
            ((length, LANES), LOW),
            ((length, width), LOW),
            ((length, 3 * LANES), LOW),
            ((length, LANES), LOW),
            spec,
            spec,
        ],
        [pltpu.VMEM((2, length, 128), WIDE)] * 2
        + [pltpu.VMEM((length, LANES), WIDE)]
        + [pltpu.VMEM((length // 2, LANES), LOW)] * 4
        + [pltpu.VMEM((length, LANES), LOW)] * 2,
        10**10,
        "mixer",
    )


def middle(index, lengths, tokens, grads, mixed, outs, gain, weights, gate):
    _, rows, width = tokens[0].shape
    length = 4 * rows
    hidden = weights[0].shape[1] // 3
    results = [
        ((length, width), LOW),
        ((length, 2 * hidden), LOW),
        ((length, hidden), LOW),
        ((length, width), LOW),
        *[((2 * rows, width), LOW)] * 4,
        ((rows, width), WIDE),
    ]
    operands = [after(gain, gate), *outs]
    for block in (2, 3, 0, 1):
        operands.append(of_row(index, tokens[block]))
        operands += [block_rows(CODES[block], rows, part) for part in mixed]
        operands.append(of_row(index, grads[block]))
    pieces = []
    if len(weights) > 1:
        size = weights[0].shape[0]

        def start(offset, first=0):
            return lambda: ring_member(ring_place() + offset) * size + first

        offsets = [(offset, 0) for offset in OFFSETS] + [(4, 0), (4, size // 2)]
        pieces = [(block, start(*where)) for block, where in zip(weights, offsets)]
        results.append(((width, 3 * hidden), LOW))
    else:
        operands += weights
    return call(
        functools.partial(middle_kernel, index, bool(pieces)),
        [lengths],
        operands,
        results,
        [],
        16 * 10**9,
        "middle",
        60,
        pieces,
    )


def norm_back(keep, arrived, last, values, extra, gain):
    rows, width = last.shape
    return call(
        norm_kernel,
        [],
        [first_rows(rows, keep), first_rows(rows, arrived), last, values, first_rows(rows, extra), gain],
        [((rows, width), WIDE), ((rows, width), LOW), ((1, width), WIDE)],
        [],
        2 * 10**9,
        "norm_back",
        24,
    )


def finish(keeps, arrived, lasts, tokens, extras, gain):
    rows, width = lasts[0].shape
    operands = [gain]
    for r in range(2):
        operands += [first_rows(rows, keeps[r]), first_rows(rows, arrived[r]), lasts[r]]
        operands += [of_row(r, tokens), extras[r]]
    return call(finish_kernel, [], operands, [((2, rows, width), WIDE)], [], 3 * 10**9, "finish", 24)[0]


def output(lengths, keeps, arrived, lasts, residuals):
    rows, width = lasts[0].shape
    operands = []
    for r in range(2):
        operands += [first_rows(rows, keeps[r]), first_rows(rows, arrived[r]), lasts[r], residuals[r]]
    return call(
        output_kernel, [lengths], operands, [((2, rows, width), LOW)], [], 3 * 10**9, "output", 24
    )[0]


def mixer_backward(index, lengths, grads, w_out, w_in, kept, taps, tables):
    rows, width = grads[0].shape
    length = 4 * rows
    mixed, h_first, projected, convolved, kernel_spec, series_spec = kept
    return call(
        functools.partial(back_kernel, index),
        [lengths],
        [
            w_out,
            *grads,
            projected,
            taps,
            tables[0],
            series_spec,
            kernel_spec,
            tables[1],
            convolved,
            w_in,
            mixed,
            h_first,
        ],
        [
            ((length, 3 * LANES), LOW),
            ((length, LANES), LOW),
            ((12, LANES), WIDE),
            ((width, LANES), LOW),
            ((2 * rows, width), LOW),
            ((2 * rows, width), LOW),
            ((1, width), WIDE),
        ],
        [pltpu.VMEM((length, LANES), WIDE)]
        + [pltpu.VMEM((2, length, 128), WIDE)] * 3
        + [pltpu.VMEM((length // 2, LANES), LOW)] * 2
        + [pltpu.VMEM((length, LANES), LOW)] * 4,
        14 * 10**9,
        "mixer_back",
    )


def tail(packed, channels, buckets, grad_in, out_grads, d_kernels):
    width = grad_in.shape[0]
    length = d_kernels[0].shape[0]
    extra = 2 * channels + 128 if packed else 0
    return call(
        functools.partial(tail_kernel, packed, channels),
        [buckets],
        [grad_in, *out_grads, *d_kernels],
        [
            ((width, 3 * LANES + extra), LOW),
            ((length, 2 * channels), WIDE),
        ],
        [],
        4 * 10**9,
        "tail",
    )


def pack_mixer(w_in, long_filter, w_out):
    rows, _, channels = w_in.shape
    gap = LANES - channels
    turned = w_out.T
    pieces = []
    for s in range(3):
        pieces += [w_in[:, s], turned[:, s * gap : (s + 1) * gap]]
    both = jnp.concatenate([long_filter[0], long_filter[1]], axis=1)
    spare = both[rows:].reshape(both.shape[0] - rows, 3, -1)
    pieces += [both[:rows], spare.transpose(1, 0, 2).reshape(rows, -1)]
    return jnp.concatenate(pieces, axis=1)


def unpack_rows(blocks, channels):
    count, rows, _ = blocks.shape
    spare = blocks[:, :, 2 * channels :].reshape(count, 3, rows // 3, -1)
    spare = spare.transpose(0, 2, 1, 3).reshape(count, rows // 3, -1)
    return jnp.concatenate([blocks[:, :, : 2 * channels], spare], axis=1)


def unpack_out(pack, channels):
    gap = LANES - channels
    return jnp.concatenate(
        [pack[:, s * LANES + channels : s * LANES + channels + gap] for s in range(3)], axis=1
    )


def unpack_mixer(pack, rows, channels):
    w_out = jnp.pad(unpack_out(pack, channels), ((0, 0), (0, LANES - channels)))
    blocks = pack[:, 3 * LANES :].reshape(-1, rows, pack.shape[1] - 3 * LANES)
    filters = unpack_rows(blocks, channels).reshape(-1, 2 * channels)
    return pack[:, : 3 * LANES], filters, w_out


def per_device(
    tokens,
    lengths,
    buckets,
    w_in,
    long_filter,
    w_out,
    w_gu,
    w_down,
    norm_gains,
    short_taps,
    cond_taps,
    cotangent,
):
    row_count, part_len, width = tokens.shape
    channels = short_taps.shape[-1]
    hidden = w_down.shape[0]
    shard = w_in.shape[0]
    rows = range(row_count)
    gains = norm_gains.astype(WIDE)
    taps = jnp.concatenate([short_taps.reshape(9, channels), cond_taps], axis=0).astype(WIDE)
    taps = jnp.pad(taps, ((0, 0), (0, LANES - channels)))
    tables = tuple(jnp.asarray(table) for table in wave_tables(4 * part_len))

    all_tokens = spread(tokens)
    (full_in, filters, part_out), packed_last = gather_mixer(
        pack_mixer(w_in, long_filter, w_out), channels
    )
    w_ff = jnp.concatenate([w_gu.reshape(shard, -1), w_down.T], axis=1)
    ff_blocks = ring_blocks(after(w_ff, packed_last))
    for _ in range(3):
        arrived_ff = next(ff_blocks)

    first = mixer_forward(0, (lengths, buckets), all_tokens, full_in, filters, taps, gains[:1], tables)
    first = after(first, arrived_ff[-2:])
    arrived_ff = ff_blocks.send(first[0])
    second = mixer_forward(
        1, (lengths, buckets), all_tokens, full_in, filters, taps, after(gains[:1], first[0]), tables
    )
    second = after(second, arrived_ff[-2:])
    cotangent = after(cotangent, all_tokens[1])
    all_grads = spread(cotangent, second[0], second[0])
    outs = spread(after(part_out, all_grads[1]), second[0], second[0])
    weights = ff_blocks.send(second[0])
    forward = [first, second]
    first_mixed = first[0]
    inputs = (lengths, all_tokens, all_grads)
    centre = []
    arrived_d = []
    gate = first_mixed
    for r in rows:
        mixed = spread(forward[r][0], gate if r else None)
        centre.append(middle(r, *inputs, mixed, outs, gains[1:], weights, gate))
        if len(weights) > 1:
            weights = [centre[r][9]]
        arrived_d.append(fold_near(centre[r][4]))
        gate = centre[r][4]
    away_d = [fold_away(centre[r][6], arrived_d[r]) for r in rows]
    last_d = [swap(away_d[r], 2) for r in rows]

    d_residual = []
    gain_second = 0.0
    d_low = []
    for r in rows:
        keep_d, residual, d_out = centre[r][6], centre[r][8], centre[r][3]
        d_wide, low, gain_grad = norm_back(
            keep_d, arrived_d[r], after(last_d[r], away_d), residual, d_out, gains[1:]
        )
        d_residual.append(d_wide)
        gain_second = gain_second + gain_grad
        d_low.append(low)

    kept_ff = [after(centre[0][:4], away_d[0]), after(centre[1][:4], away_d)]
    arrived_o = [fold_near(after(centre[r][5], away_d)) for r in rows]
    grad_gu = sum(dot(kept[0], kept[1], 0, 0) for kept in kept_ff)
    grad_down = sum(dot(kept[3], kept[2], 0, 0) for kept in kept_ff)
    grad_gu, grad_down = after((grad_gu.astype(LOW), grad_down.astype(LOW)), last_d, arrived_o)
    ff_steps = ring_sums(jnp.concatenate([grad_gu, grad_down], axis=1))
    ff_sums = [next(ff_steps)]

    backward = []
    arrived_h = []
    gate = None
    for r in rows:
        spread_d = spread(d_low[r], gate)
        if r == 0:
            spread_d[3] = after(spread_d[3], d_low[1])
            beside = ()
        else:
            last_o = [fold_far(centre[i][7], after(arrived_o[i], spread_d[1])) for i in rows]
            spread_d[3] = after(spread_d[3], ff_sums[1])
            beside = last_o
        back = mixer_backward(r, lengths, spread_d, part_out, full_in, forward[r], taps, tables)
        ff_sums.append(next(ff_steps))
        back = after(back, ff_sums[-1], beside)
        backward.append(back)
        arrived_h.append(fold_near(back[4]))
        gate = back[4]
    away_h = [fold_away(backward[r][5], arrived_h[r]) for r in rows]
    last_h = [swap(away_h[r], 2) for r in rows]

    packed = lax.axis_size("batch") == len(RING)
    d_projected = [after(backward[0][0], away_h[0]), after(backward[1][0], arrived_h)]
    grads_in = [dot(forward[r][1], d_projected[r], 0, 0) for r in rows]
    ff_sums.append(ff_steps.send((None, grads_in[0])))
    ff_sums.append(next(ff_steps))
    grad_taps = sum(backward[r][2] for r in rows)[:, :channels]
    gain_first = sum(backward[r][6] for r in rows) / gains[:1]
    smalls = jnp.concatenate(
        [gain_first.reshape(-1), gain_second.reshape(-1), grad_taps.reshape(-1)]
    )
    grad_in = grads_in[0] + grads_in[1]
    grad_in = after(grad_in.astype(LOW), away_h)
    grad_mixer, grad_filter = tail(
        packed,
        channels,
        buckets,
        grad_in,
        [backward[r][3] for r in rows],
        [backward[r][1] for r in rows],
    )
    grad_mixer, grad_filter = after((grad_mixer, grad_filter), last_h)
    smalls = list(small_sums(after(smalls.reshape(-1, 128), grad_mixer), "batch"))
    mixer_steps = ring_sums(grad_mixer)
    mixer_sums = [next(mixer_steps)]
    mixer_sums.append(next(mixer_steps))
    outputs = output(
        after(lengths, mixer_sums[0]),
        [centre[r][7] for r in rows],
        arrived_o,
        last_o,
        [centre[r][8] for r in rows],
    )
    mixer_sums[1], outputs = after((mixer_sums[1], outputs), ff_sums[4], smalls[1])
    mixer_sums.append(mixer_steps.send((outputs, None)))
    grad_ff = ff_steps.send((mixer_sums[1], None))
    d_inputs = finish(
        [backward[r][5] for r in rows],
        arrived_h,
        last_h,
        tokens,
        d_residual,
        after(gains[:1], mixer_sums[1]),
    )
    mixer_sums.append(mixer_steps.send(((d_inputs, smalls[min(2, len(smalls) - 1)]), None)))
    next(mixer_steps)
    grad_mixer = next(mixer_steps)
    if packed:
        grad_filter = unpack_rows(grad_mixer[None, :, 3 * LANES :], channels)[0]
    else:
        grad_filter = list(ring_sums(grad_filter))[-1]
    grad_in = grad_mixer[:, : 3 * LANES].reshape(-1, 3, LANES)[:, :, :channels]
    smalls = smalls[-1].reshape(-1)
    small_steps = small_sums(after(smalls[: 2 * width].reshape(-1, 128), mixer_sums[3]), "chan")
    grad_gains = list(small_steps)[-1].reshape(2, width)
    grad_taps = smalls[2 * width :].reshape(12, channels)
    return (
        outputs,
        d_inputs,
        grad_in,
        jnp.stack([grad_filter[:, :channels], grad_filter[:, channels:]]),
        unpack_out(grad_mixer, channels).T,
        grad_ff[:, : 2 * hidden].reshape(-1, 2, hidden),
        grad_ff[:, 2 * hidden :].T,
        grad_gains,
        grad_taps[:9].reshape(3, 3, channels),
        grad_taps[9:],
    )


def solution(mesh):
    placed = (
        P("batch", "chan", None),
        P("batch"),
        P("batch"),
        P("batch", None, "chan"),
        P(None, "batch", "chan"),
        P("chan", "batch"),
        P("batch", None, "chan"),
        P("chan", "batch"),
        P(),
        P(None, None, "chan"),
        P(None, "chan"),
        P("batch", "chan", None),
    )
    return jax.shard_map(
        per_device,
        mesh=mesh,
        in_specs=placed,
        out_specs=(
            P("batch", "chan", None),
            P("batch", "chan", None),
            P("batch", None, "chan"),
            P(None, "batch", "chan"),
            P("chan", "batch"),
            P("batch", None, "chan"),
            P("chan", "batch"),
            P(),
            P(None, None, "chan"),
            P(None, "chan"),
        ),
        check_vma=False,
    )
```
